32 devices in a mesh: dp: 8 (over z, y), tensor: 4 (over x, core).
Axes of the slice: x: 2, y: 2, z: 4, core: 2. Of those that a mesh axis runs over, the one named last changes fastest.
Arguments:
- tokens: bfloat16 [24, 1024, 768], P('dp', 'tensor'), may hold values from -6 to 6
- cotangent: bfloat16 [24, 1024, 768], P('dp', 'tensor'), may hold values from -6 to 6
- lengths: int32 [24, 4], P('dp'), may hold values from 1 to 640, 1024 in all within a row
- row_counts: int32 [8], P('dp'), may hold values from 1 to 3, as said below
- attn_gain: float32 [768], replicated, may hold values from 0.25 to 1.75
- attn_shift: float32 [768], replicated, may hold values from -1.5 to 1.5
- qkv_weight: bfloat16 [3, 768, 768], P(None, None, 'tensor'), may hold values from -0.21875 to 0.21875
- qkv_bias: float32 [3, 768], P(None, 'tensor'), may hold values from -1.5 to 1.5
- out_weight: bfloat16 [768, 768], P('tensor'), may hold values from -1.25 to 1.25
- out_bias: float32 [768], replicated, may hold values from -1.5 to 1.5
- ffn_gain: float32 [768], replicated, may hold values from 0.25 to 1.75
- ffn_shift: float32 [768], replicated, may hold values from -1.5 to 1.5
- up_weight: bfloat16 [768, 3072], P(None, 'tensor'), may hold values from -0.21875 to 0.21875
- up_bias: float32 [3072], P('tensor'), may hold values from -1.5 to 1.5
- down_weight: bfloat16 [3072, 768], P('tensor'), may hold values from -0.109375 to 0.109375
- down_bias: float32 [768], replicated, may hold values from -1.5 to 1.5
- head_weight: bfloat16 [768, 70], replicated, may hold values from -0.3125 to 0.3125
- codon_freq: float32 [70], replicated, may hold values from 0.004 to 0.04
Outputs:
- mixed: bfloat16 [24, 1024, 768], P('dp', 'tensor')
- input_grad: bfloat16 [24, 1024, 768], P('dp', 'tensor')
- attn_gain_grad: float32 [768], replicated
- attn_shift_grad: float32 [768], replicated
- qkv_weight_grad: float32 [3, 768, 768], P(None, None, 'tensor')
- qkv_bias_grad: float32 [3, 768], P(None, 'tensor')
- out_weight_grad: float32 [768, 768], P('tensor')
- out_bias_grad: float32 [768], replicated
- ffn_gain_grad: float32 [768], replicated
- ffn_shift_grad: float32 [768], replicated
- up_weight_grad: float32 [768, 3072], P(None, 'tensor')
- up_bias_grad: float32 [3072], P('tensor')
- down_weight_grad: float32 [3072, 768], P('tensor')
- down_bias_grad: float32 [768], replicated
- codon_gap: float32 [8, 4, 70], P('dp', 'tensor')
The draws below stay inside these ranges and needn't reach their ends.
Inputs may be any that keep to these rules, and one draw needn't show every extreme that they name: `row_counts`: the counts of the first j indices of dp sum to j * 2 or j * 2 + 1 for every j, and all counts to 2 times the number of dp indices; some index holds 3 live rows and some holds 1. Live rows come first in each index's slots.
All inputs are finite; a program needn't handle non-finite values.
Results may differ from the reference program's by a relative error of at most 0.018.
Values may be sent and summed in bfloat16 or wider, within the bound.
A program may use at most 128 MiB of HBM per device.

```python
import math
from functools import partial
import jax
import jax.numpy as jnp
import numpy as np
from jax import lax

D = 768
HEADS = 12
HEAD_DIM = 64
FF = 3072
VOCAB = 70
ROW_LEN = 1024
GENES = 4
GENE_MAX = 640
ROWS_OWN = 2
ROWS_IN = 3
ROWS_ALL = 24
N_DP = 8
N_TENSOR = 4


def draw_row_counts(key, part):
    key = jax.random.fold_in(key, 11)
    marks = jax.random.randint(key, (N_DP + 1,), 0, 2).astype(jnp.int32)
    places = jnp.arange(N_DP + 1, dtype=jnp.int32)
    centre = N_DP // 2
    cleared = (places == 0) | (places == N_DP) | (places == centre - 1) | (places == centre + 1)
    marks = jnp.where(cleared, 0, marks)
    marks = jnp.where(places == centre, 1, marks).astype(jnp.int32)
    return (ROWS_OWN + marks[1:] - marks[:-1]).astype(jnp.int32)


def steps_of(key, shape, split, smallest, largest):
    factor_of, own = 1.0, jax.random.fold_in(key, 6)
    for dim, blocks in split:
        heights = jnp.exp(jax.random.uniform(jax.random.fold_in(own, dim), (blocks,), jnp.float32, smallest / len(split), largest / len(split)))
        factor_of = factor_of * jnp.repeat(heights, shape[dim] // blocks).reshape([-1 if axis == dim else 1 for axis in range(len(shape))])
    return factor_of


def length_profile(count, total, bound, slope):
    portions = [(1 << 20) // math.isqrt(rank ** slope) + 1 for rank in range(2, count + 1)]
    surplus, given = total - bound - (count - 1), [1] * (count - 1)
    while surplus > 0:
        movable = [i for i in range(count - 1) if given[i] < bound]
        whole, left = sum([portions[i] for i in movable]), surplus
        for i in movable:
            more = min(bound - given[i], max(1, left * portions[i] // whole), surplus)
            given[i] = given[i] + more
            surplus = surplus - more
    return np.array([bound] + given)


def uneven(stream_key, number_of, total, reach, skew):
    if number_of == 2:
        one = jax.random.randint(stream_key, (), max(1, total - reach), min(reach, total - 1) + 1)
        return jnp.stack([one, total - one])
    sizes = jnp.asarray(length_profile(number_of, total, reach, skew), jnp.int32)
    twos = (number_of - 1) // 2
    source_of, receiver = sizes[1:1 + 2 * twos:2], sizes[2:2 + 2 * twos:2]
    slack = jnp.minimum(source_of - 1, reach - receiver)
    shifted = jax.random.randint(jax.random.fold_in(stream_key, 1), (twos,), 0, 1 << 20) % (slack + 1)
    sizes = sizes.at[1:1 + 2 * twos:2].set(source_of - shifted).at[2:2 + 2 * twos:2].set(receiver + shifted)
    return sizes[jax.random.permutation(jax.random.fold_in(stream_key, 2), number_of)]


def gaussian(rng, dims, width, most, split=(), kind=jnp.bfloat16):
    array = width * jax.random.normal(rng, dims, jnp.float32)
    if split:
        array = array * steps_of(rng, dims, split, -0.22, 0.18)
    return jnp.clip(array, -most, most).astype(kind)


def setup_inputs(seed: int = 0) -> dict:
    key_of = jax.random.split(jax.random.key(seed), 19)
    return {
        "tokens": gaussian(key_of[0], (ROWS_ALL, ROW_LEN, D), 1.0, 6.0, ((0, 8), (1, 4))),
        "cotangent": gaussian(key_of[1], (ROWS_ALL, ROW_LEN, D), 1.0, 6.0, ((0, 8), (1, 4))),
        "lengths": jax.vmap(lambda own: uneven(own, GENES, ROW_LEN, GENE_MAX, 2))(jax.random.split(key_of[2], ROWS_ALL)).reshape((ROWS_ALL, GENES)).astype(jnp.int32),
        "row_counts": draw_row_counts(jax.random.fold_in(key_of[18], 71), 0),
        "attn_gain": jnp.clip(1.0 + 0.15 * jax.random.normal(key_of[4], (D,), jnp.float32), 0.25, 1.75),
        "attn_shift": gaussian(key_of[5], (D,), 0.3, 1.5, (), jnp.float32),
        "qkv_weight": gaussian(key_of[6], (3, D, D), D ** -0.5, 0.21875, ((2, 4),)),
        "qkv_bias": gaussian(key_of[7], (3, D), 0.3, 1.5, ((1, 4),), jnp.float32),
        "out_weight": gaussian(key_of[8], (D, D), (D // 32) ** -0.5, 1.25, ((0, 4),)),
        "out_bias": gaussian(key_of[9], (D,), 0.3, 1.5, (), jnp.float32),
        "ffn_gain": jnp.clip(1.0 + 0.15 * jax.random.normal(key_of[10], (D,), jnp.float32), 0.25, 1.75),
        "ffn_shift": gaussian(key_of[11], (D,), 0.3, 1.5, (), jnp.float32),
        "up_weight": gaussian(key_of[12], (D, FF), D ** -0.5, 0.21875, ((1, 4),)),
        "up_bias": gaussian(key_of[13], (FF,), 0.3, 1.5, ((0, 4),), jnp.float32),
        "down_weight": gaussian(key_of[14], (FF, D), FF ** -0.5, 0.109375, ((0, 4),)),
        "down_bias": gaussian(key_of[15], (D,), 0.3, 1.5, (), jnp.float32),
        "head_weight": gaussian(key_of[16], (D, VOCAB), (D // 2) ** -0.5, 0.3125),
        "codon_freq": jnp.clip(jnp.exp(jax.random.uniform(key_of[17], (VOCAB,), jnp.float32, math.log(0.004), math.log(0.04))), 0.004, 0.04),
    }


EPS = 1e-05
BASE = 10000.0
HIGH = lax.Precision.HIGHEST

@jax.custom_vjp
def low(v):
    return lax.optimization_barrier(v.astype(jnp.bfloat16)).astype(jnp.float32)

@jax.custom_vjp
def low_back(v):
    return v

def low_keep(v):
    return (low(v), None)

def low_pass(kept, grad):
    return (grad,)

def back_keep(v):
    return (v, None)

def back_low(kept, grad):
    return (low(grad),)
low.defvjp(low_keep, low_pass)
low_back.defvjp(back_keep, back_low)

def layer_norm(value, gain, shift):
    average = lax.optimization_barrier(jnp.mean(value, -1, keepdims=True))
    centred = value - average
    return centred * lax.rsqrt(lax.optimization_barrier(jnp.mean(centred * centred, -1, keepdims=True)) + EPS) * gain + shift

def gene_layout(lens):
    gene_ends = jnp.cumsum(lens, axis=1).astype(jnp.int32)
    starts = (gene_ends - lens).astype(jnp.int32)
    places = jnp.arange(ROW_LEN, dtype=jnp.int32)
    segment = lax.optimization_barrier(jnp.sum((places[None, :, None] >= gene_ends[:, None, :]).astype(jnp.int32), axis=2))
    onehot = segment[:, :, None] == jnp.arange(GENES, dtype=jnp.int32)[None, None, :]
    gene_start = lax.optimization_barrier(jnp.sum(jnp.where(onehot, starts[:, None, :], 0), axis=2)).astype(jnp.int32)
    return (segment, places[None, :] - gene_start)

def rope_tables(position, half_dim):
    freqs = BASE ** (-jnp.arange(half_dim, dtype=jnp.float32) / half_dim)
    angles = position.astype(jnp.float32)[..., None] * freqs
    return (jnp.cos(angles), jnp.sin(angles))

def rotate_pairs(value, cosine, sine_table):
    half_dim = value.shape[-1] // 2
    front = value[..., :half_dim]
    back_half = value[..., half_dim:]
    cos_b = cosine[:, :, None, :]
    sin_b = sine_table[:, :, None, :]
    return jnp.concatenate([front * cos_b - back_half * sin_b, back_half * cos_b + front * sin_b], axis=-1)

def row_attention(parts):
    queries, keys, values, segment = parts
    raw_scores = jnp.einsum('qhe,khe->hqk', queries, keys, precision=HIGH) * HEAD_DIM ** (-0.5)
    scores = low_back(raw_scores)
    same_gene = segment[:, None] == segment[None, :]
    scores = jnp.where(same_gene[None], scores, -1e+30)
    probs = jax.nn.softmax(scores, axis=-1)
    return jnp.einsum('hqk,khe->qhe', low(probs), values, precision=HIGH)

def layer_block(lens, params, rows_in):
    attn_gain, attn_shift, qkv_weight, qkv_bias, out_weight, out_bias, ffn_gain, ffn_shift, up_weight, up_bias, down_weight, down_bias = params
    row_total = rows_in.shape[0]
    normed = low(layer_norm(rows_in, attn_gain, attn_shift))
    projected = low_back(jnp.einsum('nld,jde->jnle', normed, qkv_weight, precision=HIGH)) + qkv_bias[:, None, None, :]
    shaped = projected.reshape(3, row_total, ROW_LEN, HEADS, HEAD_DIM)
    segment, position = gene_layout(lens)
    cosine, sine_table = rope_tables(position, HEAD_DIM // 2)
    queries = low(rotate_pairs(shaped[0], cosine, sine_table))
    keys = low(rotate_pairs(shaped[1], cosine, sine_table))
    values = low(shaped[2])
    heads_out = lax.map(jax.checkpoint(row_attention), (queries, keys, values, segment))
    head_out = low(low_back(heads_out.reshape(row_total, ROW_LEN, D)))
    attention = low_back(jnp.einsum('nle,ed->nld', head_out, out_weight, precision=HIGH)) + out_bias
    middle = rows_in + attention
    normed2 = low(layer_norm(middle, ffn_gain, ffn_shift))
    hidden = low_back(jnp.einsum('nld,df->nlf', normed2, up_weight, precision=HIGH)) + up_bias
    activated = low(jax.nn.gelu(hidden, approximate=False))
    return middle + low_back(jnp.einsum('nlf,fd->nld', activated, down_weight, precision=HIGH)) + down_bias

def read_out(head_matrix, mixed_rows):
    logits = jnp.einsum('grld,dv->grlv', mixed_rows, head_matrix, precision=HIGH)
    return jax.nn.softmax(logits, axis=-1)

def reference(tokens, cotangent, lengths, row_counts, attn_gain, attn_shift, qkv_weight, qkv_bias, out_weight, out_bias, ffn_gain, ffn_shift, up_weight, up_bias, down_weight, down_bias, head_weight, codon_freq):
    params = (attn_gain.astype(jnp.float32), attn_shift.astype(jnp.float32), qkv_weight.astype(jnp.float32), qkv_bias.astype(jnp.float32), out_weight.astype(jnp.float32), out_bias.astype(jnp.float32), ffn_gain.astype(jnp.float32), ffn_shift.astype(jnp.float32), up_weight.astype(jnp.float32), up_bias.astype(jnp.float32), down_weight.astype(jnp.float32), down_bias.astype(jnp.float32))
    live_rows = jnp.arange(ROWS_IN, dtype=jnp.int32)[None, :] < row_counts[:, None]
    live_float = live_rows.astype(jnp.float32)[:, :, None, None]
    token_groups = tokens.astype(jnp.float32).reshape(N_DP, ROWS_IN, ROW_LEN, D)
    grad_groups = cotangent.astype(jnp.float32).reshape(N_DP, ROWS_IN, ROW_LEN, D) * live_float
    lens_groups = lengths.reshape(N_DP, ROWS_IN, GENES)

    def group_step(running, pieces):
        rows_in, rows_grad, lens = pieces
        outputs, pullback = jax.vjp(partial(layer_block, lens), params, rows_in)
        param_grads, input_grads = pullback(rows_grad)
        running = jax.tree.map(lambda total, extra: total + extra, running, param_grads)
        return (running, (outputs, input_grads))
    zeros_start = jax.tree.map(lambda value: jnp.zeros(value.shape, jnp.float32), params)
    summed, (outputs, input_grads) = lax.scan(group_step, zeros_start, (token_groups, grad_groups, lens_groups))
    mixed = (outputs * live_float).astype(jnp.bfloat16)
    input_grad = (input_grads * live_float).astype(jnp.bfloat16)
    probs, unused_pullback = jax.vjp(partial(read_out, head_weight.astype(jnp.float32)), mixed.astype(jnp.float32))
    quarter = ROW_LEN // N_TENSOR
    per_quarter = lax.optimization_barrier(jnp.sum(probs.reshape(N_DP, ROWS_IN, N_TENSOR, quarter, VOCAB), axis=3))
    per_device = lax.optimization_barrier(jnp.sum(per_quarter * live_rows.astype(jnp.float32)[:, :, None, None], axis=1))
    mean_prob = per_device / (row_counts.astype(jnp.float32) * quarter)[:, None, None]
    codon_gap = jnp.log(mean_prob) - jnp.log(codon_freq)[None, None, :]
    return (mixed.reshape(ROWS_ALL, ROW_LEN, D), input_grad.reshape(ROWS_ALL, ROW_LEN, D), summed[0], summed[1], summed[2], summed[3], summed[4], summed[5], summed[6], summed[7], summed[8], summed[9], summed[10], summed[11], codon_gap)
```

```python
import functools

import jax
import jax.numpy as jnp
import numpy as np
from jax import lax
from jax.experimental import pallas as pl
from jax.experimental.pallas import tpu as pltpu
from jax.sharding import PartitionSpec as P

HEAD_DIM = 64
EPS = 1e-05
BASE = 10000.0
F32 = jnp.float32
BF16 = jnp.bfloat16
MESH = pl.DeviceIdType.MESH
LANE = 128
CHUNK = 64
FAR = -1e30
MASK_AT = 64
TOTAL_AT = 68


def dot_nn(a, b):
    return lax.dot_general(a, b, (((1,), (0,)), ((), ())), preferred_element_type=F32)


def dot_nt(a, b):
    return lax.dot_general(a, b, (((1,), (1,)), ((), ())), preferred_element_type=F32)


def dot_tn(a, b):
    return lax.dot_general(a, b, (((0,), (0,)), ((), ())), preferred_element_type=F32)


def lanes(shape):
    return lax.broadcasted_iota(jnp.int32, shape, 1)


def three_parts(value):
    high = value.astype(BF16).astype(F32)
    rest = value - high
    middle = rest.astype(BF16).astype(F32)
    return high, middle, rest - middle


def normalize(value):
    average = jnp.mean(value, -1, keepdims=True)
    centred = value - average
    inv_std = lax.rsqrt(jnp.mean(centred * centred, -1, keepdims=True) + EPS)
    return centred * inv_std, inv_std


def norm_back(incoming, normed, inv_std, gain):
    scaled = incoming * gain
    return inv_std * (
        scaled
        - jnp.mean(scaled, -1, keepdims=True)
        - normed * jnp.mean(scaled * normed, -1, keepdims=True)
    )


def swap_halves(value):
    lane = lanes(value.shape)
    return jnp.where(lane < 32, pltpu.roll(value, 96, 1), pltpu.roll(value, 32, 1))


class Copies:
    def __init__(self, send, recv):
        self.send, self.recv, self.count = send, recv, 0

    def make(self, src, dst, device):
        at = self.count
        self.count += 1
        return functools.partial(
            pltpu.make_async_remote_copy,
            src_ref=src,
            dst_ref=dst,
            send_sem=self.send.at[at],
            recv_sem=self.recv.at[at],
            device_id=device,
            device_id_type=MESH,
        )


class Reduce:
    def __init__(self, copies, ref, land, out, store_sem, rows, order, d, t):
        self.ref, self.land = ref, land
        self.plan = []
        offset, used = 0, 0
        backs = []
        for bit in order:
            partner = (d ^ (1 << bit), t)
            side = (d >> bit) & 1
            if rows % 32 == 0:
                half = rows // 2
                keep = offset + half * side
                give = offset + half * (1 - side)
                copy = copies.make(self.at(ref, give, half), land.at[pl.ds(used, half)], partner)
                self.plan.append((copy, keep, half, used))
                backs.append((partner, keep, half))
                used, offset, rows = used + half, keep, half
            else:
                copy = copies.make(self.at(ref, offset, rows), land.at[pl.ds(used, rows)], partner)
                self.plan.append((copy, offset, rows, used))
                used += rows
        self.adds = len(self.plan)
        source, target = self.at(ref, offset, rows), self.at(out, offset, rows)
        self.store = functools.partial(pltpu.make_async_copy, source, target, store_sem)
        for i, (partner, keep, half) in enumerate(reversed(backs)):
            own = self.at(ref if i == 0 else out, keep, half)
            self.plan.append((copies.make(own, self.at(out, keep, half), partner), keep, half, 0))
        self.place = 0

    @staticmethod
    def land_rows(rows, steps):
        used = 0
        for _ in range(steps):
            if rows % 32 == 0:
                rows //= 2
            used += rows
        return used

    @staticmethod
    def at(ref, offset, rows):
        if not isinstance(offset, int):
            offset = pl.multiple_of(offset, 16)
        return ref.at[pl.ds(offset, rows)]

    def start(self):
        self.plan[0][0]().start()

    def left(self):
        return len(self.plan) - self.place

    def tick(self):
        if self.place >= len(self.plan):
            return
        copy, keep, rows, used = self.plan[self.place]
        copy().wait()
        if self.place < self.adds:
            step = max(s for s in (16, 32, 48, 64, 96) if rows % s == 0)

            def add(i, _):
                here = pl.ds(pl.multiple_of(keep + i * step, 16), step)
                there = pl.ds(pl.multiple_of(used + i * step, 16), step)
                total = self.ref[here].astype(F32) + self.land[there].astype(F32)
                self.ref[here] = total.astype(BF16)
                return _

            lax.fori_loop(0, rows // step, add, None)
        if self.place == self.adds - 1:
            self.store().start()
        if self.place == self.adds or (self.place + 1 == len(self.plan) and self.place < self.adds):
            self.store().wait()
        self.place += 1
        if self.place < len(self.plan):
            self.plan[self.place][0]().start()


def layer_kernel(
    n_dp,
    slots,
    quarter,
    features,
    count_ref,
    lens_ref,
    tok_ref,
    cotan_ref,
    wqkv_ref,
    bqkv_ref,
    wout_ref,
    wup_ref,
    wdown_ref,
    bup_ref,
    vec_ref,
    head_ref,
    freq_ref,
    rope_ref,
    base_ref,
    line_ref,
    mixed_out,
    grad_out,
    gdown_out,
    gup_out,
    gout_out,
    gqkv_out,
    small_out,
    codon_out,
    n1,
    n2,
    cot,
    gm,
    heads_q,
    heads_k,
    heads_v,
    head_out,
    head_grad,
    dq_acc,
    dp_low,
    act,
    slope,
    part,
    land_core,
    land_x,
    mid,
    gmid,
    table_c,
    table_s,
    wc,
    bc,
    woe,
    tok_b,
    got_cot,
    scan_mine,
    scan_land,
    lens_mine,
    lens_land,
    gdown,
    gup,
    gout,
    gqkv,
    land_down,
    land_up,
    back_mixed,
    back_grad,
    sums,
    sums_land,
    bias_acc,
    send_sems,
    recv_sems,
    out_sems,
):
    d, t = lax.axis_index("dp"), lax.axis_index("tensor")
    core, across = (d, t ^ 1), (d, t ^ 2)
    own_rows = slots - 1
    dp_steps = n_dp.bit_length() - 1
    copies = Copies(send_sems, recv_sems)

    attn_gain, attn_shift = vec_ref[0:1], vec_ref[1:2]
    out_bias, ffn_gain, ffn_shift, down_bias = (vec_ref[i : i + 1] for i in range(2, 6))

    barrier = pltpu.get_barrier_semaphore()
    greeted = [core, across]
    for k in range(dp_steps):
        greeted.append((d ^ (1 << k), t))
        greeted.append(((d + (1 << k)) % n_dp, t))
        greeted.append(((d + n_dp - (1 << k)) % n_dp, t))
    for other in greeted:
        pl.semaphore_signal(barrier, inc=1, device_id=other, device_id_type=MESH)
    pl.semaphore_wait(barrier, len(greeted))

    def over_chunks(rows, body, step=CHUNK):
        def run(i, _):
            body(pl.ds(pl.multiple_of(i * step, step), step))
            return _

        lax.fori_loop(0, rows // step, run, None)

    mixed, ingrad = n2.at[0, pl.ds(0, slots)], n2.at[1, pl.ds(0, slots)]
    land_qkv = act.at[0, :, pl.ds(0, 5 * LANE)]
    land_out = act.at[1]

    tail_tok, tail_cot = mixed.at[slots - 1], ingrad.at[slots - 1]
    count = count_ref[0]
    count_wide = jnp.full((CHUNK, features), count, jnp.int32)

    def pick_tail(rows):
        for source, target in ((tok_ref, tail_tok), (cotan_ref, tail_cot)):
            value = source[slots - 1, rows].astype(F32)
            for slot in range(slots - 2, -1, -1):
                value = jnp.where(count_wide == slot + 1, source[slot, rows].astype(F32), value)
            target[rows] = value.astype(BF16)

    over_chunks(quarter, pick_tail)
    after, before = (d + 1, t), (d - 1, t)
    send_tok = copies.make(tail_tok, tok_b, after)
    send_cot = copies.make(tail_cot, got_cot, after)
    send_lens = copies.make(lens_mine, lens_land, after)

    def lens_tile(slot):
        row_at = lax.broadcasted_iota(jnp.int32, (8, LANE), 0)
        tile = jnp.zeros((8, LANE), jnp.int32)
        for gene in range(4):
            tile = jnp.where(row_at == gene, lens_ref[slot, gene], tile)
        return tile

    tail_lens = lens_tile(slots - 1)
    for slot in range(slots - 2, -1, -1):
        tail_lens = jnp.where(jnp.full((8, LANE), count, jnp.int32) == slot + 1, lens_tile(slot), tail_lens)
    lens_mine[...] = tail_lens

    @pl.when(d < n_dp - 1)
    def _():
        send_tok().start()
        send_lens().start()

    @pl.when(d == 0)
    def _():
        tok_b[...] = jnp.zeros_like(tok_b)
        got_cot[...] = jnp.zeros_like(got_cot)
        lens_land[...] = jnp.zeros_like(lens_land)

    @pl.when(d == n_dp - 1)
    def _():
        back_mixed[...] = jnp.zeros_like(back_mixed)
        back_grad[...] = jnp.zeros_like(back_grad)

    scan_copies = [copies.make(scan_mine.at[k], scan_land.at[k], (d + (1 << k), t)) for k in range(dp_steps)]
    scan_mine[0] = jnp.full((8, LANE), count, jnp.int32)

    def scan_start(k):
        @pl.when(d + (1 << k) < n_dp)
        def _():
            scan_copies[k]().start()

    def scan_end(k):
        scan_mine[k + 1] = scan_mine[k]

        @pl.when(d + (1 << k) < n_dp)
        def _():
            scan_copies[k]().wait_send()

        @pl.when(d >= (1 << k))
        def _():
            scan_copies[k]().wait_recv()
            scan_mine[k + 1] = scan_mine[k] + scan_land[k]

    scan_start(0)

    def gather(full, r):
        mine = full.at[r, t]
        return (
            copies.make(mine, mine, across),
            copies.make(mine, mine, core),
            copies.make(full.at[r, t ^ 2], full.at[r, t ^ 2], core),
        )

    def gather_start(link):
        link[0]().start()
        link[1]().start()

    def gather_pass(link):
        link[0]().wait_recv()
        link[2]().start()

    def gather_end(link):
        link[0]().wait_send()
        link[1]().wait()
        link[2]().wait()

    def summing(kind, r):
        return (
            copies.make(part.at[kind, r, t ^ 1], land_core.at[kind, r, 0], core),
            copies.make(part.at[kind, r, t ^ 3], land_core.at[kind, r, 1], core),
            copies.make(part.at[kind, r, t ^ 2], land_x.at[kind, r], across),
        )

    def quarter_of(i):
        return t ^ jnp.where(i == 0, 3, jnp.where(i == 3, 0, i))

    def sum_step(link, kind, r, i, q, value):
        @pl.when(i < 2)
        def _():
            part[kind, r, q] = value.astype(BF16)

        @pl.when(i == 0)
        def _():
            link[1]().start()

        @pl.when(i == 1)
        def _():
            link[0]().start()

        @pl.when(i == 2)
        def _():
            link[1]().wait_recv()
            part[kind, r, q] = (value + land_core[kind, r, 1].astype(F32)).astype(BF16)
            link[2]().start()

        @pl.when(i == 3)
        def _():
            link[0]().wait_recv()
            part[kind, r, q] = (value + land_core[kind, r, 0].astype(F32)).astype(BF16)

    def sum_all(link, kind, r, make_part):
        def run(i, _):
            q = quarter_of(i)
            sum_step(link, kind, r, i, q, make_part(q))
            return _

        lax.fori_loop(0, 4, run, None)

    def sum_end(link):
        link[0]().wait_send()
        link[1]().wait_send()
        link[2]().wait()

    def sum_total(kind, r, rows):
        return part[kind, r, t, rows].astype(F32) + land_x[kind, r, rows].astype(F32)

    link_n1 = [gather(n1, r) for r in range(2)]
    link_n2 = [gather(n2, r) for r in range(2)]
    link_cot = [gather(cot, r) for r in range(2)]
    link_gm = [gather(gm, r) for r in range(2)]

    def rows_of(q):
        return pl.ds(pl.multiple_of(q * quarter, quarter), quarter)

    def first_tokens(r, rows):
        return (tok_ref[0, rows] if r == 0 else tok_b[rows]).astype(F32)

    def first_norm(r):
        def body(rows):
            normed, _ = normalize(first_tokens(r, rows))
            n1[r, t, rows] = (normed * attn_gain + attn_shift).astype(BF16)

        over_chunks(quarter, body)

    sums[...] = jnp.zeros_like(sums)
    bias_acc[...] = jnp.zeros_like(bias_acc)

    def add_sum(row, value):
        sums[row : row + 1] = sums[row : row + 1] + jnp.sum(value, axis=0, keepdims=True)

    def load_cotangent(r):
        def body(rows):
            value = cotan_ref[0, rows].astype(F32)
            if r == 1:
                value = jnp.where(carried_wide, got_cot[rows].astype(F32), cotan_ref[1, rows].astype(F32))
            cot[r, t, rows] = value.astype(BF16)
            add_sum(5, value)

        over_chunks(quarter, body)

    first_norm(0)
    gather_start(link_n1[0])
    load_cotangent(0)

    third = 3 * HEAD_DIM
    for j in range(3):
        wc[:, j * LANE : (j + 1) * LANE] = wqkv_ref[j, :, 0:LANE]
        bc[:, j * LANE : (j + 1) * LANE] = bqkv_ref[j : j + 1, 0:LANE]
    last = [wqkv_ref[j, :, LANE:third].astype(F32) for j in range(3)]
    wc[:, 3 * LANE : 4 * LANE] = jnp.concatenate([last[0], last[1]], axis=1).astype(BF16)
    wc[:, 4 * LANE : 5 * LANE] = jnp.concatenate([last[2], jnp.zeros_like(last[2])], axis=1).astype(BF16)
    last = [bqkv_ref[j : j + 1, LANE:third] for j in range(3)]
    bc[:, 3 * LANE : 4 * LANE] = jnp.concatenate([last[0], last[1]], axis=1)
    bc[:, 4 * LANE : 5 * LANE] = jnp.concatenate([last[2], jnp.zeros_like(last[2])], axis=1)
    for h in range(3):
        woe[h * LANE : h * LANE + HEAD_DIM] = wout_ref[h * HEAD_DIM : (h + 1) * HEAD_DIM]
        woe[h * LANE + HEAD_DIM : (h + 1) * LANE] = jnp.zeros((HEAD_DIM, features), BF16)

    def ends_of(r):
        tile = lens_tile(0) if r == 0 else jnp.where(carried_tile, lens_land[...], lens_tile(1))
        first = tile[0:1]
        second = first + tile[1:2]
        return first, second, second + tile[2:3]

    def segment_of(ends, base, rows):
        place = lax.broadcasted_iota(jnp.int32, (rows, LANE), 0) + base
        return [place >= end for end in ends]

    def tables(r):
        ends = ends_of(r)
        turns = [end.astype(F32) * freq_ref[...] for end in ends]
        cosines = [jnp.cos(turn) for turn in turns]
        sines = [jnp.sin(turn) * line_ref[...] for turn in turns]

        def body(rows):
            passed = segment_of(ends, rows.start, CHUNK)
            at = pl.ds(rows.start // CHUNK, 1)
            cos_base, sin_base = base_ref[0, at], base_ref[1, at]
            cos_start = jnp.broadcast_to(cos_base, (CHUNK, LANE))
            sin_start = jnp.broadcast_to(sin_base, (CHUNK, LANE))
            for ge, cosine, sine in zip(passed, cosines, sines):
                cos_start = jnp.where(ge, cos_base * cosine + sin_base * sine, cos_start)
                sin_start = jnp.where(ge, sin_base * cosine - cos_base * sine, sin_start)
            cos_place, sin_place = rope_ref[0], rope_ref[1]
            table_c[r, rows] = cos_place * cos_start - sin_place * sin_start
            table_s[r, rows] = sin_place * cos_start + cos_place * sin_start

        over_chunks(4 * quarter, body)

    tables(0)
    scan_end(0)
    for k in range(1, dp_steps):
        scan_start(k)
        scan_end(k)
    carried_tile = (scan_mine[dp_steps] - count - d * own_rows) > 0
    carried_wide = jnp.broadcast_to(carried_tile[0:1, 0:1], (CHUNK, features))

    @pl.when(d > 0)
    def _():
        send_lens().wait_recv()
        send_tok().wait_recv()

    @pl.when(d < n_dp - 1)
    def _():
        send_lens().wait_send()
        send_tok().wait_send()
        send_cot().start()

    def pick_b(rows):
        value = jnp.where(carried_wide, tok_b[rows].astype(F32), tok_ref[1, rows].astype(F32))
        tok_b[rows] = value.astype(BF16)

    over_chunks(quarter, pick_b)
    first_norm(1)
    gather_pass(link_n1[0])
    gather_start(link_n1[1])
    tables(1)

    def project(r):
        ends = ends_of(r)

        def run(q, _):
            rows = rows_of(q)
            both = dot_nn(n1[r, q], wc[...]) + bc[...]
            lane = lanes((quarter, LANE))
            ge = segment_of(ends, q * quarter, quarter)
            gene = sum(g.astype(jnp.int32) for g in ge)
            in_mask = (lane >= MASK_AT) & (lane < TOTAL_AT)
            same = in_mask & (lane - MASK_AT == gene)
            extra_q = jnp.where(in_mask & ~same, FAR, 0.0)
            extra_k = jnp.where(same | ((lane >= TOTAL_AT) & (lane < TOTAL_AT + 3)), 1.0, 0.0)
            extra_v = jnp.where((lane >= MASK_AT) & (lane < MASK_AT + 3), 1.0, 0.0)
            cosine, sine = table_c[r, rows], table_s[r, rows]
            blocks = [both[:, j * LANE : (j + 1) * LANE] for j in range(5)]
            for h in range(3):
                query = (blocks[0], pltpu.roll(blocks[0], 64, 1), blocks[3])[h]
                key = (blocks[1], pltpu.roll(blocks[1], 64, 1), pltpu.roll(blocks[3], 64, 1))[h]
                value = (blocks[2], pltpu.roll(blocks[2], 64, 1), blocks[4])[h]
                query = (query * cosine + swap_halves(query) * sine) * HEAD_DIM**-0.5 + extra_q
                key = key * cosine + swap_halves(key) * sine + extra_k
                value = jnp.where(lane < HEAD_DIM, value, extra_v)
                heads_q[r, h, rows] = query.astype(BF16)
                heads_k[r, h, rows] = key.astype(BF16)
                heads_v[r, h, rows] = value.astype(BF16)
            return _

        lax.fori_loop(0, 4, run, None)

    def attend(r):
        def run(i, _):
            h, q = i // 4, i % 4
            rows = rows_of(q)
            query = heads_q[r, h, rows]
            scores = dot_nt(query, heads_k[r, h])
            top = jnp.max(scores, -1, keepdims=True)
            probs = jnp.exp(scores - top).astype(BF16)
            mixed_values = dot_nn(probs, heads_v[r, h])
            lane = lanes((quarter, LANE))
            total = mixed_values[:, MASK_AT : MASK_AT + 1]
            out = mixed_values * (1.0 / total)
            head_out[r, h, rows] = jnp.where(lane < HEAD_DIM, out, 0.0).astype(BF16)
            parts = three_parts(-(top + jnp.log(total)))
            query = query.astype(F32)
            for at, value in enumerate(parts):
                query = jnp.where(lane == TOTAL_AT + at, value, query)
            heads_q[r, h, rows] = query.astype(BF16)
            return _

        lax.fori_loop(0, 12, run, None)

    def close_attention(r, link):
        def make(q):
            rows = rows_of(q)
            joined = jnp.concatenate([head_out[r, h, rows] for h in range(3)], axis=1)
            return dot_nn(joined, woe[...])

        sum_all(link, 0, r, make)

    def second_norm(r):
        def body(rows):
            middle = first_tokens(r, rows) + sum_total(0, r, rows) + out_bias
            mid[r, rows] = middle
            normed, _ = normalize(middle)
            n2[r, t, rows] = (normed * ffn_gain + ffn_shift).astype(BF16)

        over_chunks(quarter, body)

    def feed(r, link):
        def make(q):
            hidden = dot_nn(n2[r, q], wup_ref[...]) + bup_ref[...]
            below = 0.5 * (1.0 + lax.erf(hidden * 0.5**0.5))
            density = jnp.exp(hidden * hidden * -0.5) * (2.0 * np.pi) ** -0.5
            act[r, rows_of(q)] = (hidden * below).astype(BF16)
            grad = dot_nt(cot[r, q], wdown_ref[...]) * (below + hidden * density)
            add_sum(6, grad)
            low = grad.astype(BF16)
            slope[r, q] = low
            return dot_nt(low, wup_ref[...])

        sum_all(link, 0, r, make)

    def close_feed(r, link):
        sum_all(link, 1, r, lambda q: dot_nn(act[r, rows_of(q)], wdown_ref[...]))

    def finish_mixed(r):
        def body(rows):
            mixed[r, rows] = (mid[r, rows] + sum_total(1, r, rows) + down_bias).astype(BF16)

        over_chunks(quarter, body)

    def back_second_norm(r):
        def body(rows):
            incoming = sum_total(0, r, rows)
            normed, inv_std = normalize(mid[r, rows])
            grad = cot[r, t, rows].astype(F32) + norm_back(incoming, normed, inv_std, ffn_gain)
            gmid[r, rows] = grad
            gm[r, t, rows] = grad.astype(BF16)
            add_sum(3, incoming * normed)
            add_sum(4, incoming)
            add_sum(2, grad)

        over_chunks(quarter, body)

    def open_heads(r):
        def run(q, _):
            rows = rows_of(q)
            grads = dot_nt(gm[r, q], woe[...])
            lane = lanes((quarter, LANE))
            for h in range(3):
                low = grads[:, h * LANE : (h + 1) * LANE].astype(BF16).astype(F32)
                dots = jnp.sum(low * head_out[r, h, rows].astype(F32), -1, keepdims=True)
                for at, value in enumerate(three_parts(-dots)):
                    low = jnp.where(lane == MASK_AT + at, value, low)
                head_grad[h, rows] = low.astype(BF16)
            return _

        lax.fori_loop(0, 4, run, None)

    def unrotate(r, rows, value):
        return value * table_c[r, rows] - swap_halves(value) * table_s[r, rows]

    def put(r, j, h, rows, value):
        at = h * 3 + j
        bias_acc[pl.ds(at, 1)] = bias_acc[pl.ds(at, 1)] + jnp.sum(value, axis=0, keepdims=True)
        block = slice(j * LANE, (j + 1) * LANE)
        tail = slice(3 * LANE, 4 * LANE) if j < 2 else slice(4 * LANE, 5 * LANE)

        @pl.when(h == 0)
        def _():
            dp_low[r, rows, block] = value.astype(BF16)

        @pl.when(h == 1)
        def _():
            first = dp_low[r, rows, block].astype(F32)
            dp_low[r, rows, block] = (first + pltpu.roll(value, 64, 1)).astype(BF16)

        @pl.when(h == 2)
        def _():
            if j == 0:
                other = dp_low[r, rows, tail].astype(F32)
                dp_low[r, rows, tail] = (other + value).astype(BF16)
            else:
                moved = pltpu.roll(value, 64, 1) if j == 1 else value
                dp_low[r, rows, tail] = moved.astype(BF16)

    def attend_back(r, h):
        dq_acc[...] = jnp.zeros_like(dq_acc)

        def run(b, _):
            rows = rows_of(b)
            keys = heads_k[r, h, rows]
            lane = lanes((quarter, LANE))
            probs = jnp.exp(dot_nt(keys, heads_q[r, h]))
            grads = probs * dot_nt(heads_v[r, h, rows], head_grad[h])
            low = grads.astype(BF16)
            dv = dot_nn(probs.astype(BF16), head_grad[h])
            put(r, 2, h, rows, jnp.where(lane < HEAD_DIM, dv, 0.0))
            dk = dot_nn(low, heads_q[r, h])
            put(r, 1, h, rows, unrotate(r, rows, jnp.where(lane < HEAD_DIM, dk, 0.0)))
            dq_acc[...] += dot_tn(low, keys)
            return _

        lax.fori_loop(0, 4, run, None)

        def close(q, _):
            rows = rows_of(q)
            lane = lanes((quarter, LANE))
            dq = jnp.where(lane < HEAD_DIM, dq_acc[rows], 0.0) * HEAD_DIM**-0.5
            put(r, 0, h, rows, unrotate(r, rows, dq))
            return _

        lax.fori_loop(0, 4, close, None)

    def close_back(r, link):
        def make(q):
            rows = rows_of(q)
            return dot_nt(dp_low[r, rows], wc[...])

        sum_all(link, 0, r, make)

    def back_first_norm(r):
        def body(rows):
            incoming = sum_total(0, r, rows)
            normed, inv_std = normalize(first_tokens(r, rows))
            grad = gmid[r, rows] + norm_back(incoming, normed, inv_std, attn_gain)
            ingrad[r, rows] = grad.astype(BF16)
            add_sum(0, incoming * normed)
            add_sum(1, incoming)

        over_chunks(quarter, body)

    def flat(ref, r, at):
        here = pl.ds(pl.multiple_of(at, LANE), 256)
        return ref[r, :, here] if ref is act else ref[r, :, :, here].reshape(4 * quarter, 256)

    def weight_grad(left, right, target):
        def run(i, _):
            total = sum(dot_tn(flat(left, r, i * 256), right[r].reshape(4 * quarter, features)) for r in range(2))
            target[pl.ds(pl.multiple_of(i * 256, 256), 256)] = total.astype(BF16)
            return _

        lax.fori_loop(0, features // 256, run, None)

    def up_grad():
        weight_grad(n2, slope, gup)

    def down_grad():
        weight_grad(act, cot, gdown)

    def out_grad():
        for h in range(3):
            total = sum(dot_tn(head_out[r, h], gm[r].reshape(4 * quarter, features)) for r in range(2))
            gout[h * HEAD_DIM : (h + 1) * HEAD_DIM] = total[0:HEAD_DIM].astype(BF16)

    def qkv_grad():
        def run(i, _):
            total = sum(dot_tn(flat(n1, r, i * 256), dp_low[r]) for r in range(2))
            gqkv[pl.ds(pl.multiple_of(i * 256, 256), 256)] = total.astype(BF16)
            return _

        lax.fori_loop(0, features // 256, run, None)

    order = tuple(range(dp_steps))
    turned = (order[1], order[0]) + order[2:] if dp_steps > 1 else order
    red_down = Reduce(copies, gdown, land_down, gdown_out, out_sems.at[2], features, order, d, t)
    red_up = Reduce(copies, gup, land_up, gup_out, out_sems.at[3], features, turned, d, t)
    red_out = Reduce(copies, gout, land_out, gout_out, out_sems.at[4], 3 * HEAD_DIM, order, d, t)
    red_qkv = Reduce(copies, gqkv, land_qkv, gqkv_out, out_sems.at[5], features, order, d, t)

    gather_end(link_n1[0])
    project(0)
    gather_start(link_cot[0])
    attend(0)
    link_o0 = summing(0, 0)
    close_attention(0, link_o0)
    gather_pass(link_n1[1])
    gather_end(link_n1[1])
    project(1)
    sum_end(link_o0)
    second_norm(0)
    gather_start(link_n2[0])

    @pl.when(d > 0)
    def _():
        send_cot().wait_recv()

    @pl.when(d < n_dp - 1)
    def _():
        send_cot().wait_send()

    load_cotangent(1)
    gather_pass(link_cot[0])
    attend(1)
    gather_pass(link_n2[0])
    gather_start(link_cot[1])
    link_o1 = summing(0, 1)
    close_attention(1, link_o1)
    gather_end(link_n2[0])
    gather_end(link_cot[0])
    link_g0 = summing(0, 0)
    feed(0, link_g0)
    sum_end(link_o1)
    second_norm(1)
    gather_start(link_n2[1])
    link_m0 = summing(1, 0)
    close_feed(0, link_m0)
    gather_pass(link_cot[1])
    sum_end(link_g0)
    back_second_norm(0)
    gather_start(link_gm[0])
    gather_pass(link_n2[1])
    gather_end(link_cot[1])
    gather_end(link_n2[1])
    link_g1 = summing(0, 1)
    feed(1, link_g1)
    gather_pass(link_gm[0])
    down_grad()
    red_down.start()
    up_grad()
    red_up.start()
    link_m1 = summing(1, 1)
    close_feed(1, link_m1)
    gather_end(link_gm[0])
    open_heads(0)
    attend_back(0, 0)
    sum_end(link_g1)
    back_second_norm(1)
    gather_start(link_gm[1])
    red_down.tick()
    red_up.tick()
    attend_back(0, 1)
    red_down.tick()
    red_up.tick()
    attend_back(0, 2)
    link_f0 = summing(0, 0)
    close_back(0, link_f0)
    gather_pass(link_gm[1])
    sum_end(link_m0)
    finish_mixed(0)
    sum_end(link_m1)
    finish_mixed(1)
    return_mixed = copies.make(mixed.at[1], back_mixed, before)
    return_grad = copies.make(ingrad.at[1], back_grad, before)

    @pl.when(d > 0)
    def _():
        return_mixed().start()

    gather_end(link_gm[1])
    out_grad()
    red_out.start()
    open_heads(1)
    red_down.tick()
    red_up.tick()
    attend_back(1, 0)
    red_down.tick()
    red_up.tick()
    red_out.tick()
    sum_end(link_f0)
    back_first_norm(0)
    attend_back(1, 1)
    red_down.tick()
    red_up.tick()
    red_out.tick()
    attend_back(1, 2)
    link_f1 = summing(0, 1)
    close_back(1, link_f1)
    qkv_grad()
    red_qkv.start()
    while red_down.left() or red_up.left() or red_out.left():
        red_down.tick()
        red_up.tick()
        red_out.tick()
    sum_end(link_f1)
    back_first_norm(1)

    @pl.when(d > 0)
    def _():
        return_grad().start()

    acc = [[bias_acc[h * 3 + j : h * 3 + j + 1] for j in range(3)] for h in range(3)]
    for j in range(3):
        sums[7:8, j * LANE : (j + 1) * LANE] = acc[0][j] + pltpu.roll(acc[1][j], 64, 1)
    sums[7:8, 3 * LANE : 4 * LANE] = acc[2][0] + pltpu.roll(acc[2][1], 64, 1)
    sums[7:8, 4 * LANE : 5 * LANE] = acc[2][2]
    partners = [core, across] + [(d ^ (1 << k), t) for k in range(dp_steps)]
    shared = lax.broadcasted_iota(jnp.int32, (8, features), 0) < 6
    for k, partner in enumerate(partners):
        copy = copies.make(sums, sums_land.at[k], partner)
        copy().start()
        copy().wait()
        extra = sums_land[k]
        sums[...] = sums[...] + (jnp.where(shared, extra, 0.0) if k < 2 else extra)
        red_qkv.tick()

    @pl.when(d > 0)
    def _():
        return_mixed().wait_send()
        return_grad().wait_send()

    @pl.when(d < n_dp - 1)
    def _():
        return_mixed().wait_recv()
        return_grad().wait_recv()

    def settle(rows):
        for own, back in ((mixed, back_mixed), (ingrad, back_grad)):
            mine, returned = own[1, rows].astype(F32), back[rows].astype(F32)
            middle = jnp.where(carried_wide, returned, mine)
            own[1, rows] = jnp.where(count_wide >= 2, middle, 0.0).astype(BF16)
            own[2, rows] = jnp.where(count_wide >= 3, returned, 0.0).astype(BF16)

    over_chunks(quarter, settle)
    store_mixed = pltpu.make_async_copy(mixed, mixed_out, out_sems.at[0])
    store_grad = pltpu.make_async_copy(ingrad, grad_out, out_sems.at[1])
    store_mixed.start()
    store_grad.start()
    total = jnp.zeros((1, head_ref.shape[1]), F32)
    for slot in range(slots):
        logits = dot_nn(mixed[slot], head_ref[...])
        raised = jnp.exp(logits - jnp.max(logits, -1, keepdims=True))
        probs = raised / jnp.sum(raised, -1, keepdims=True)
        one = jnp.sum(probs, axis=0, keepdims=True)
        total = total + jnp.where(jnp.full(one.shape, count, jnp.int32) > slot, one, 0.0)
    codon_out[...] = total
    small_out[...] = sums[...]
    while red_qkv.left():
        red_qkv.tick()
    store_mixed.wait()
    store_grad.wait()


def body(
    tokens,
    cotangent,
    lengths,
    row_counts,
    attn_gain,
    attn_shift,
    qkv_weight,
    qkv_bias,
    out_weight,
    out_bias,
    ffn_gain,
    ffn_shift,
    up_weight,
    up_bias,
    down_weight,
    down_bias,
    head_weight,
    codon_freq,
):
    slots, quarter, features = tokens.shape
    n_dp = lax.axis_size("dp")
    steps = n_dp.bit_length() - 1
    length = 4 * quarter
    half = HEAD_DIM // 2
    freqs = np.float32(BASE) ** (-np.arange(half, dtype=np.float32) / np.float32(half))
    freq_lane = np.tile(freqs.astype(np.float32), LANE // half)
    sign = np.concatenate([-np.ones(half), np.ones(half), np.zeros(HEAD_DIM)]).astype(np.float32)

    def turned(places):
        angles = places[:, None].astype(np.float64) * freq_lane[None].astype(np.float64)
        return np.stack([np.cos(angles) * np.abs(sign), np.sin(angles) * sign]).astype(np.float32)

    rope, bases = turned(np.arange(CHUNK)), turned(np.arange(0, length, CHUNK))
    vectors = jnp.stack([attn_gain, attn_shift, out_bias, ffn_gain, ffn_shift, down_bias, down_bias, down_bias])
    vmem, smem = pl.BlockSpec(memory_space=pltpu.VMEM), pl.BlockSpec(memory_space=pltpu.SMEM)
    anywhere = pl.BlockSpec(memory_space=pl.ANY)
    wide = (quarter, features)

    def low(*shape):
        return pltpu.VMEM(shape, BF16)

    def full(*shape):
        return pltpu.VMEM(shape, F32)

    out_width = 3 * HEAD_DIM
    n_sems = 24 + 24 + 3 + steps + 2 + 4 * 2 * steps + 2 + steps
    scratch = [
        low(2, 4, *wide),
        low(2, 4, *wide),
        low(2, 4, *wide),
        low(2, 4, *wide),
        low(2, 3, length, LANE),
        low(2, 3, length, LANE),
        low(2, 3, length, LANE),
        low(2, 3, length, LANE),
        low(3, length, LANE),
        full(length, LANE),
        low(2, length, 5 * LANE),
        low(2, length, features),
        low(2, 4, *wide),
        low(2, 2, 4, *wide),
        low(2, 2, 2, *wide),
        low(2, 2, *wide),
        full(2, *wide),
        full(2, *wide),
        full(2, length, LANE),
        full(2, length, LANE),
        low(features, 5 * LANE),
        full(1, 5 * LANE),
        low(3 * LANE, features),
        low(*wide),
        low(*wide),
        pltpu.VMEM((steps + 1, 8, LANE), jnp.int32),
        pltpu.VMEM((steps, 8, LANE), jnp.int32),
        pltpu.VMEM((8, LANE), jnp.int32),
        pltpu.VMEM((8, LANE), jnp.int32),
        low(features, features),
        low(features, features),
        low(out_width, features),
        low(features, 5 * LANE),
        low(Reduce.land_rows(features, steps), features),
        low(Reduce.land_rows(features, steps), features),
        low(*wide),
        low(*wide),
        full(8, features),
        full(2 + steps, 8, features),
        full(16, LANE),
        pltpu.SemaphoreType.DMA((n_sems,)),
        pltpu.SemaphoreType.DMA((n_sems,)),
        pltpu.SemaphoreType.DMA((6,)),
    ]
    outs = pl.pallas_call(
        functools.partial(layer_kernel, n_dp, slots, quarter, features),
        out_shape=(
            jax.ShapeDtypeStruct(tokens.shape, BF16),
            jax.ShapeDtypeStruct(tokens.shape, BF16),
            jax.ShapeDtypeStruct((features, features), BF16),
            jax.ShapeDtypeStruct((features, features), BF16),
            jax.ShapeDtypeStruct((out_width, features), BF16),
            jax.ShapeDtypeStruct((features, 5 * LANE), BF16),
            jax.ShapeDtypeStruct((8, features), F32),
            jax.ShapeDtypeStruct((1, head_weight.shape[1]), F32),
        ),
        in_specs=[smem, smem] + [vmem] * 14,
        out_specs=(anywhere,) * 6 + (vmem, vmem),
        scratch_shapes=scratch,
        compiler_params=pltpu.CompilerParams(
            collective_id=0, has_side_effects=True, vmem_limit_bytes=64 * 1024 * 1024
        ),
    )(
        row_counts,
        lengths,
        tokens,
        cotangent,
        qkv_weight,
        qkv_bias,
        out_weight,
        up_weight,
        down_weight,
        up_bias[None],
        vectors,
        head_weight,
        jnp.asarray(freq_lane[None]),
        jnp.asarray(rope),
        jnp.asarray(bases),
        jnp.asarray(sign[None]),
    )
    mixed, input_grad, gdown, gup, gout, gqkv, small, codon = outs
    mean_prob = codon / (row_counts[0] * quarter).astype(F32)
    codon_gap = (jnp.log(mean_prob) - jnp.log(codon_freq)).reshape(1, 1, -1)

    def spread(packed):
        pairs = packed[..., : 3 * LANE].reshape(packed.shape[:-1] + (3, LANE))
        rest = packed[..., 3 * LANE : 3 * LANE + 3 * HEAD_DIM].reshape(packed.shape[:-1] + (3, HEAD_DIM))
        return jnp.moveaxis(jnp.concatenate([pairs, rest], axis=-1), -2, 0)

    return (
        mixed,
        input_grad,
        small[0],
        small[1],
        spread(gqkv).astype(F32),
        spread(small[7, : 5 * LANE]),
        gout.astype(F32),
        small[2],
        small[3],
        small[4],
        gup.astype(F32),
        small[6],
        gdown.astype(F32),
        small[5],
        codon_gap,
    )


def solution(mesh):
    placed = (
        P("dp", "tensor", None),
        P("dp", "tensor", None),
        P("dp", None),
        P("dp"),
        P(),
        P(),
        P(None, None, "tensor"),
        P(None, "tensor"),
        P("tensor", None),
        P(),
        P(),
        P(),
        P(None, "tensor"),
        P("tensor"),
        P("tensor", None),
        P(),
        P(),
        P(),
    )
    return jax.shard_map(
        body,
        mesh=mesh,
        in_specs=placed,
        out_specs=(
            P("dp", "tensor", None),
            P("dp", "tensor", None),
            P(),
            P(),
            P(None, None, "tensor"),
            P(None, "tensor"),
            P("tensor", None),
            P(),
            P(),
            P(),
            P(None, "tensor"),
            P("tensor"),
            P("tensor", None),
            P(),
            P("dp", "tensor", None),
        ),
        check_vma=False,
    )
```

```python
import functools

import jax
import jax.numpy as jnp
import numpy as np
from jax import lax
from jax.experimental import pallas as pl
from jax.experimental.pallas import tpu as pltpu
from jax.sharding import PartitionSpec as P

HEAD_DIM = 64
EPS = 1e-05
BASE = 10000.0
F32 = jnp.float32
BF16 = jnp.bfloat16
MESH = pl.DeviceIdType.MESH
LANE = 128
CHUNK = 64
FAR = -1e30
MASK_AT = 64
TOTAL_AT = 68
SUMS = {
    "D0": ((1,), (0,), (2,)),
    "D1": ((0,), (1,), (2,)),
    "D2": ((0,), (1,), (2,)),
    "D3": ((0,), (1,), (2,)),
    "U0": ((0,), (1, 2)),
    "U1": ((1,), (0,), (2,)),
    "U2": ((0,), (1,), (2,)),
    "U3": ((1,), (0,), (2,)),
    "O": ((0, 1, 2),),
    "Q0": ((1,), (0,), (2,)),
    "Q1": ((0,), (1,), (2,)),
    "Q2": ((0,), (1,), (2,)),
}


def dot_nn(a, b):
    return lax.dot_general(a, b, (((1,), (0,)), ((), ())), preferred_element_type=F32)


def dot_nt(a, b):
    return lax.dot_general(a, b, (((1,), (1,)), ((), ())), preferred_element_type=F32)


def dot_tn(a, b):
    return lax.dot_general(a, b, (((0,), (0,)), ((), ())), preferred_element_type=F32)


def lanes(shape):
    return lax.broadcasted_iota(jnp.int32, shape, 1)


def three_parts(value):
    high = value.astype(BF16).astype(F32)
    rest = value - high
    middle = rest.astype(BF16).astype(F32)
    return high, middle, rest - middle


def normalize(value):
    average = jnp.mean(value, -1, keepdims=True)
    centred = value - average
    inv_std = lax.rsqrt(jnp.mean(centred * centred, -1, keepdims=True) + EPS)
    return centred * inv_std, inv_std


def norm_back(incoming, normed, inv_std, gain):
    scaled = incoming * gain
    return inv_std * (
        scaled
        - jnp.mean(scaled, -1, keepdims=True)
        - normed * jnp.mean(scaled * normed, -1, keepdims=True)
    )


def swap_halves(value):
    lane = lanes(value.shape)
    return jnp.where(lane < 32, pltpu.roll(value, 96, 1), pltpu.roll(value, 32, 1))


class Copies:
    def __init__(self, send, recv):
        self.send, self.recv, self.count = send, recv, 0

    def make(self, src, dst, device):
        at = self.count
        self.count += 1
        return functools.partial(
            pltpu.make_async_remote_copy,
            src_ref=src,
            dst_ref=dst,
            send_sem=self.send.at[at],
            recv_sem=self.recv.at[at],
            device_id=device,
            device_id_type=MESH,
        )


class Region:
    def __init__(self, row, rows, lane, width):
        self.row, self.rows, self.lane, self.width = row, rows, lane, width

    def halves(self, side):
        if self.rows % 32 == 0:
            half = self.rows // 2
            cut = [Region(self.row + half * k, half, self.lane, self.width) for k in (side, 1 - side)]
        elif self.width % (2 * LANE) == 0:
            half = self.width // 2
            cut = [Region(self.row, self.rows, self.lane + half * k, half) for k in (side, 1 - side)]
        else:
            cut = None
        return cut

    def of(self, ref, start=0, rows=None):
        row, lane = self.row + start, self.lane
        if not isinstance(row, int):
            row = pl.multiple_of(row, 16)
        if not isinstance(lane, int):
            lane = pl.multiple_of(lane, LANE)
        return ref.at[pl.ds(row, rows or self.rows), pl.ds(lane, self.width)]


class Places:
    def __init__(self, width):
        self.width, self.used, self.spare = width, 0, []

    def take(self, region):
        at = (self.used, 0)
        if 2 * region.width == self.width:
            if (region.rows, region.width) in [size for size, _ in self.spare]:
                i = [size for size, _ in self.spare].index((region.rows, region.width))
                return self.spare.pop(i)[1]
            self.spare.append(((region.rows, region.width), Region(self.used, region.rows, region.width, region.width)))
        self.used += region.rows
        return Region(at[0], region.rows, at[1], region.width)


class Reduce:
    def __init__(self, copies, ref, land, out, store_sem, groups, d, t):
        self.ref, self.land = ref, land
        self.plan = []
        rows, width = ref.shape
        region, place, backs = Region(0, rows, 0, width), Places(width), []
        for group in groups:
            sends, mine = [], self.part(region, group, [(d >> bit) & 1 for bit in group])
            for mask in range(1, 1 << len(group)):
                turned = [(mask >> i) & 1 for i in range(len(group))]
                partner = (d ^ sum(turn << bit for turn, bit in zip(turned, group)), t)
                give = self.part(region, group, [((d >> bit) & 1) ^ turn for turn, bit in zip(turned, group)])
                there = place.take(mine)
                sends.append((copies.make(give.of(ref), there.of(land), partner), there, partner))
            self.plan.append(([copy for copy, _, _ in sends], mine, [there for _, there, _ in sends]))
            if mine.rows * mine.width < region.rows * region.width:
                backs.append((mine, [partner for _, _, partner in sends]))
            region = mine
        self.adds = len(self.plan)
        self.store = functools.partial(pltpu.make_async_copy, region.of(ref), region.of(out), store_sem)
        for i, (region, partners) in enumerate(reversed(backs)):
            own = region.of(ref if i == 0 else out)
            self.plan.append(([copies.make(own, region.of(out), partner) for partner in partners], region, ()))
        self.place = 0

    @staticmethod
    def part(region, group, sides):
        for side in sides:
            region = (region.halves(side) or (region,))[0]
        return region

    @staticmethod
    def land_rows(rows, width, groups):
        region, place = Region(0, rows, 0, width), Places(width)
        for group in groups:
            region = Reduce.part(region, group, [0] * len(group))
            for _ in range(1, 1 << len(group)):
                place.take(region)
        return place.used

    def start(self):
        for copy in self.plan[0][0]:
            copy().start()

    def left(self):
        return len(self.plan) - self.place

    def tick(self):
        if self.place >= len(self.plan):
            return
        group, region, landed = self.plan[self.place]
        for copy in group:
            copy().wait()
        if landed:
            step = max(size for size in (16, 32, 48, 64, 96) if region.rows % size == 0)

            def add(i, _):
                here = region.of(self.ref, i * step, step)
                total = here[...].astype(F32)
                for there in landed:
                    total += there.of(self.land, i * step, step)[...].astype(F32)
                here[...] = total.astype(BF16)
                return _

            lax.fori_loop(0, region.rows // step, add, None)
        if self.place == self.adds - 1:
            self.store().start()
        if self.place == self.adds or (self.place + 1 == len(self.plan) and self.place < self.adds):
            self.store().wait()
        self.place += 1
        if self.place < len(self.plan):
            for copy in self.plan[self.place][0]:
                copy().start()


def sum_groups(steps, name):
    first = [tuple(bit for bit in group if bit < steps) for group in SUMS[name]]
    return [group for group in first if group] + [(bit,) for bit in range(3, steps)]


def schedule(dp_steps, cliques):
    names = (
        "begin", "prep", "scan0", "x:cA", "scan1", "tabA", "p:n1A", "scan2", "LN1B", "x:n1B", "QKVA", "attA", "p:cA",
        "cB", "x:cB", "tabB", "clOA", "p:n1B", "QKVB", "attB", "clOB", "p:cB", "LN2A", "x:n2A", "LN2B", "x:n2B",
        "p:n2A", "feedA", "p:n2B", "feedB", "U0", "D0", "D2", "bk2A", "x:gmA", "t:U0", "clFB", "t:D1", "U2", "bk2B",
        "x:gmB", "t:U1", "x:mB", "t:D2", "clFA", "t:D1", "p:gmA", "t:D3", "t:U0", "t:D0", "t:U2", "openA", "t:U3",
        "ab0A", "t:D2", "t:D0", "t:U1", "p:gmB", "ab1A", "t:U3", "t:D3", "t:U2", "ab2A", "t:D1", "openB", "t:D0",
        "mixB", "retM", "ab0B", "ab1B", "t:U3", "Q1", "t:U2", "Q0", "t:D0", "clBA", "O", "ab2B", "Q2", "t:Q1", "t:Q0",
        "t:D2", "t:U2", "t:D3", "t:U0", "x:mA", "t:D1", "t:U1", "clBB", "t:Q2", "t:U3", "t:Q1", "t:D3", "t:Q0",
        "t:D0", "t:U2", "t:U1", "t:U0", "t:Q1", "bk1A", "mixA", "t:Q2", "t:D1", "t:D2", "t:Q0", "codA", "t:D3",
        "t:U3", "t:D2", "t:Q1", "t:Q2", "t:Q0", "t:U1", "t:D3", "t:O", "t:Q1", "t:D1", "bk1B", "t:D2", "t:Q2", "sums",
        "retG", "setM", "t:U3", "sum0", "t:D0", "t:Q0", "t:Q2", "t:Q1", "sum1", "t:O", "t:U2", "t:U1", "setG", "t:Q0",
        "t:Q2",
    )
    for name in names:
        if name in ("scan2", "sum1"):
            count = dp_steps if name == "scan2" else cliques
            yield from (name[:-1] + str(k) for k in range(int(name[-1]), count))
        else:
            yield name


def layer_kernel(
    n_dp,
    slots,
    quarter,
    features,
    count_ref,
    lens_ref,
    tok_ref,
    cotan_ref,
    wqkv_ref,
    bqkv_ref,
    wout_ref,
    wup_ref,
    wdown_ref,
    vec_ref,
    head_ref,
    freq_ref,
    rope_ref,
    base_ref,
    line_ref,
    mixed_out,
    grad_out,
    gdown_out,
    gup_out,
    gout_out,
    gqkv_out,
    small_out,
    qkv_bias_out,
    codon_out,
    n1,
    n2,
    cot,
    gm,
    heads_q,
    heads_k,
    heads_v,
    head_out,
    head_grad,
    dp_low,
    act,
    slope,
    part,
    land_core,
    land_x,
    mid,
    table_c,
    table_s,
    wc,
    bc,
    woe,
    tok_b,
    got_cot,
    scan_mine,
    scan_land,
    lens_mine,
    lens_land,
    gdown,
    gup,
    gout,
    gqkv,
    land_sums,
    back_mixed,
    back_grad,
    sums,
    sums_land,
    send_sems,
    recv_sems,
    out_sems,
    load_sems,
):
    d, t = lax.axis_index("dp"), lax.axis_index("tensor")
    core, across = (d, t ^ 1), (d, t ^ 2)
    own_rows = slots - 1
    dp_steps = n_dp.bit_length() - 1
    copies = Copies(send_sems, recv_sems)
    rows_ab = {"A": 0, "B": 1}

    attn_gain, attn_shift = vec_ref[0:1], vec_ref[1:2]
    out_bias, ffn_gain, ffn_shift, down_bias, up_bias = (vec_ref[i : i + 1] for i in range(2, 7))

    cliques = [[(d, t ^ m) for m in range(1, 4)]]
    for low_bit in range(0, dp_steps, 3):
        width = min(3, dp_steps - low_bit)
        cliques.append([(d ^ (m << low_bit), t) for m in range(1, 1 << width)])
    greeted = [other for clique in cliques for other in clique]
    for k in range(dp_steps):
        greeted.append(((d + (1 << k)) % n_dp, t))
        greeted.append(((d + n_dp - (1 << k)) % n_dp, t))
    barrier = pltpu.get_barrier_semaphore()
    for other in greeted:
        pl.semaphore_signal(barrier, inc=1, device_id=other, device_id_type=MESH)

    loads = []
    for h in range(3):
        for j in range(3):
            source = wqkv_ref.at[j, pl.ds(h * HEAD_DIM, HEAD_DIM)]
            target = wc.at[pl.ds(2 * LANE * h + HEAD_DIM * j, HEAD_DIM)]
            loads.append(pltpu.make_async_copy(source, target, load_sems.at[len(loads)]))
        source = wout_ref.at[pl.ds(h * HEAD_DIM, HEAD_DIM)]
        target = woe.at[pl.ds(h * LANE, HEAD_DIM)]
        loads.append(pltpu.make_async_copy(source, target, load_sems.at[len(loads)]))
    for load in loads:
        load.start()

    def over_chunks(rows, body, step=CHUNK):
        def run(i, _):
            body(pl.ds(pl.multiple_of(i * step, step), step))
            return _

        lax.fori_loop(0, rows // step, run, None)

    mixed, ingrad = n2.at[0, pl.ds(0, slots)], n2.at[1, pl.ds(0, slots)]

    tail_tok, tail_cot = mixed.at[slots - 1], ingrad.at[slots - 1]
    count = count_ref[0]
    count_wide = jnp.full((CHUNK, features), count, jnp.int32)

    def pick_tail(source, target):
        def body(rows):
            value = source[slots - 1, rows].astype(F32)
            for slot in range(slots - 2, -1, -1):
                value = jnp.where(count_wide == slot + 1, source[slot, rows].astype(F32), value)
            target[rows] = value.astype(BF16)

        over_chunks(quarter, body)

    after, before = (d + 1, t), (d - 1, t)
    send_tok = copies.make(tail_tok, tok_b, after)
    send_cot = copies.make(tail_cot, got_cot, after)
    send_lens = copies.make(lens_mine, lens_land, after)
    return_mixed = copies.make(mixed.at[1], back_mixed, before)
    return_grad = copies.make(ingrad.at[1], back_grad, before)

    def lens_tile(slot):
        row_at = lax.broadcasted_iota(jnp.int32, (8, LANE), 0)
        tile = jnp.zeros((8, LANE), jnp.int32)
        for gene in range(4):
            tile = jnp.where(row_at == gene, lens_ref[slot, gene], tile)
        return tile

    scan_copies = [copies.make(scan_mine.at[k], scan_land.at[k], (d + (1 << k), t)) for k in range(dp_steps)]

    def scan_start(k):
        @pl.when(d + (1 << k) < n_dp)
        def _():
            scan_copies[k]().start()

    def scan_end(k):
        scan_mine[k + 1] = scan_mine[k]

        @pl.when(d + (1 << k) < n_dp)
        def _():
            scan_copies[k]().wait_send()

        @pl.when(d >= (1 << k))
        def _():
            scan_copies[k]().wait_recv()
            scan_mine[k + 1] = scan_mine[k] + scan_land[k]

    def carried_tile():
        return (scan_mine[dp_steps] - count - d * own_rows) > 0

    def carried_wide():
        return jnp.broadcast_to(carried_tile()[0:1, 0:1], (CHUNK, features))

    def gather(full, r):
        mine = full.at[r, t]
        return (
            copies.make(mine, mine, across),
            copies.make(mine, mine, core),
            copies.make(full.at[r, t ^ 2], full.at[r, t ^ 2], core),
        )

    def gather_start(link):
        link[0]().start()
        link[1]().start()

    def gather_pass(link):
        link[0]().wait_recv()
        link[2]().start()

    def gather_end(link):
        link[0]().wait_send()
        link[1]().wait()
        link[2]().wait()

    def summing(kind, r):
        return (
            copies.make(part.at[kind, r, t ^ 1], land_core.at[kind, r, 0], core),
            copies.make(part.at[kind, r, t ^ 3], land_core.at[kind, r, 1], core),
            copies.make(part.at[kind, r, t ^ 2], land_x.at[kind, r], across),
        )

    def quarter_of(i):
        return t ^ jnp.where(i == 0, 3, jnp.where(i == 3, 0, i))

    def sum_step(link, kind, r, i, q, value):
        @pl.when(i < 2)
        def _():
            part[kind, r, q] = value.astype(BF16)

        @pl.when(i == 0)
        def _():
            link[1]().start()

        @pl.when(i == 1)
        def _():
            link[0]().start()

        @pl.when(i == 2)
        def _():
            link[1]().wait_recv()
            part[kind, r, q] = (value + land_core[kind, r, 1].astype(F32)).astype(BF16)
            if kind == 0:
                link[2]().start()

        @pl.when(i == 3)
        def _():
            link[0]().wait_recv()
            part[kind, r, q] = (value + land_core[kind, r, 0].astype(F32)).astype(BF16)

    def sum_all(link, kind, r, make_part):
        def run(i, _):
            q = quarter_of(i)
            sum_step(link, kind, r, i, q, make_part(q))
            return _

        lax.fori_loop(0, 4, run, None)

    def sum_end(link):
        link[0]().wait_send()
        link[1]().wait_send()
        link[2]().wait()

    def sum_total(kind, r, rows):
        return part[kind, r, t, rows].astype(F32) + land_x[kind, r, rows].astype(F32)

    links = {}
    for name, r in rows_ab.items():
        for key, full in (("n1", n1), ("c", cot), ("n2", n2), ("gm", gm)):
            links[key + name] = gather(full, r)
        for key, kind in (("o", 0), ("g", 0), ("f", 0), ("m", 1)):
            links[key + name] = summing(kind, r)

    def rows_of(q):
        return pl.ds(pl.multiple_of(q * quarter, quarter), quarter)

    def add_sum(row, value):
        sums[row : row + 1] = sums[row : row + 1] + jnp.sum(value, axis=0, keepdims=True)

    def first_tokens(r, rows):
        return (tok_ref[0, rows] if r == 0 else tok_b[rows]).astype(F32)

    def first_norm(r):
        def body(rows):
            normed, _ = normalize(first_tokens(r, rows))
            n1[r, t, rows] = (normed * attn_gain + attn_shift).astype(BF16)

        over_chunks(quarter, body)

    def load_cotangent(r):
        if r == 1:

            @pl.when(d > 0)
            def _():
                send_cot().wait_recv()

            @pl.when(d < n_dp - 1)
            def _():
                send_cot().wait_send()

        def body(rows):
            value = cotan_ref[0, rows].astype(F32)
            if r == 1:
                value = jnp.where(carried_wide(), got_cot[rows].astype(F32), cotan_ref[1, rows].astype(F32))
            cot[r, t, rows] = value.astype(BF16)
            add_sum(5, value)

        over_chunks(quarter, body)

    def ends_of(r):
        tile = lens_tile(0) if r == 0 else jnp.where(carried_tile(), lens_land[...], lens_tile(1))
        first = tile[0:1]
        second = first + tile[1:2]
        return first, second, second + tile[2:3]

    def segment_of(ends, base, rows):
        place = lax.broadcasted_iota(jnp.int32, (rows, LANE), 0) + base
        return [place >= end for end in ends]

    def tables(r):
        ends = ends_of(r)
        turns = [end.astype(F32) * freq_ref[...] for end in ends]
        cosines = [jnp.cos(turn) for turn in turns]
        sines = [jnp.sin(turn) * line_ref[...] for turn in turns]

        def body(rows):
            passed = segment_of(ends, rows.start, CHUNK)
            at = pl.ds(rows.start // CHUNK, 1)
            cos_base, sin_base = base_ref[0, at], base_ref[1, at]
            cos_start = jnp.broadcast_to(cos_base, (CHUNK, LANE))
            sin_start = jnp.broadcast_to(sin_base, (CHUNK, LANE))
            for ge, cosine, sine in zip(passed, cosines, sines):
                cos_start = jnp.where(ge, cos_base * cosine + sin_base * sine, cos_start)
                sin_start = jnp.where(ge, sin_base * cosine - cos_base * sine, sin_start)
            cos_place, sin_place = rope_ref[0], rope_ref[1]
            table_c[r, rows] = cos_place * cos_start - sin_place * sin_start
            table_s[r, rows] = sin_place * cos_start + cos_place * sin_start

        over_chunks(4 * quarter, body)

    def project(r):
        ends = ends_of(r)

        def run(q, _):
            rows = rows_of(q)
            both = dot_nt(n1[r, q], wc[...]) + bc[...]
            lane = lanes((quarter, LANE))
            ge = segment_of(ends, q * quarter, quarter)
            gene = sum(g.astype(jnp.int32) for g in ge)
            in_mask = (lane >= MASK_AT) & (lane < TOTAL_AT)
            same = in_mask & (lane - MASK_AT == gene)
            extra_q = jnp.where(in_mask & ~same, FAR, 0.0)
            extra_k = jnp.where(same | ((lane >= TOTAL_AT) & (lane < TOTAL_AT + 3)), 1.0, 0.0)
            extra_v = jnp.where((lane >= MASK_AT) & (lane < MASK_AT + 3), 1.0, 0.0)
            cosine, sine = table_c[r, rows], table_s[r, rows]
            for h in range(3):
                query = both[:, 2 * LANE * h : 2 * LANE * h + LANE]
                key = pltpu.roll(query, HEAD_DIM, 1)
                value = both[:, 2 * LANE * h + LANE : 2 * LANE * (h + 1)]
                query = (query * cosine + swap_halves(query) * sine) * HEAD_DIM**-0.5 + extra_q
                key = key * cosine + swap_halves(key) * sine + extra_k
                heads_q[r, h, rows] = query.astype(BF16)
                heads_k[r, h, rows] = key.astype(BF16)
                heads_v[r, h, rows] = (value + extra_v).astype(BF16)
            return _

        lax.fori_loop(0, 4, run, None)

    def attend(r):
        def run(q, _):
            rows = rows_of(q)
            lane = lanes((quarter, LANE))
            queries = [heads_q[r, h, rows] for h in range(3)]
            scores = [dot_nt(queries[h], heads_k[r, h]) for h in range(3)]
            for h in range(3):
                top = jnp.max(scores[h], -1, keepdims=True)
                probs = jnp.exp(scores[h] - top).astype(BF16)
                mixed_values = dot_nn(probs, heads_v[r, h])
                total = mixed_values[:, MASK_AT : MASK_AT + 1]
                out = mixed_values * (1.0 / total)
                head_out[r, h, rows] = jnp.where(lane < HEAD_DIM, out, 0.0).astype(BF16)
                query = queries[h].astype(F32)
                for at, value in enumerate(three_parts(-(top + jnp.log(total)))):
                    query = jnp.where(lane == TOTAL_AT + at, value, query)
                heads_q[r, h, rows] = query.astype(BF16)
            return _

        lax.fori_loop(0, 4, run, None)

    def close_attention(r, link):
        def make(q):
            rows = rows_of(q)
            joined = jnp.concatenate([head_out[r, h, rows] for h in range(3)], axis=1)
            return dot_nn(joined, woe[...])

        sum_all(link, 0, r, make)

    def second_norm(r):
        def body(rows):
            middle = first_tokens(r, rows) + sum_total(0, r, rows) + out_bias
            mid[r, rows] = middle
            normed, _ = normalize(middle)
            n2[r, t, rows] = (normed * ffn_gain + ffn_shift).astype(BF16)

        over_chunks(quarter, body)

    def feed(r, link):
        def make(q):
            hidden = dot_nn(n2[r, q], wup_ref[...]) + up_bias
            below = 0.5 * (1.0 + lax.erf(hidden * 0.5**0.5))
            density = jnp.exp(hidden * hidden * -0.5) * (2.0 * np.pi) ** -0.5
            act[r, q] = (hidden * below).astype(BF16)
            grad = dot_nt(cot[r, q], wdown_ref[...]) * (below + hidden * density)
            add_sum(6, grad)
            low = grad.astype(BF16)
            slope[r, q] = low
            return dot_nt(low, wup_ref[...])

        sum_all(link, 0, r, make)

    def close_feed(r, link):
        sum_all(link, 1, r, lambda q: dot_nn(act[r, q], wdown_ref[...]))

    def finish_mixed(r):
        def body(rows):
            mixed[r, rows] = (mid[r, rows] + sum_total(1, r, rows) + down_bias).astype(BF16)

        over_chunks(quarter, body)

    def back_second_norm(r):
        def body(rows):
            incoming = sum_total(0, r, rows)
            normed, inv_std = normalize(mid[r, rows])
            grad = cot[r, t, rows].astype(F32) + norm_back(incoming, normed, inv_std, ffn_gain)
            gm[r, t, rows] = grad.astype(BF16)
            add_sum(3, incoming * normed)
            add_sum(4, incoming)
            add_sum(2, grad)

        over_chunks(quarter, body)

    def open_heads(r):
        def run(q, _):
            rows = rows_of(q)
            grads = dot_nt(gm[r, q], woe[...])
            lane = lanes((quarter, LANE))
            for h in range(3):
                low = grads[:, h * LANE : (h + 1) * LANE].astype(BF16).astype(F32)
                dots = jnp.sum(low * head_out[r, h, rows].astype(F32), -1, keepdims=True)
                for at, value in enumerate(three_parts(-dots)):
                    low = jnp.where(lane == MASK_AT + at, value, low)
                head_grad[h, rows] = low.astype(BF16)
            return _

        lax.fori_loop(0, 4, run, None)

    def unrotate(r, rows, value):
        return value * table_c[r, rows] - swap_halves(value) * table_s[r, rows]

    def attend_back(r, h):
        first, second = 2 * LANE * h, 2 * LANE * h + LANE
        lane = lanes((quarter, LANE))
        dq_total, bias_k, bias_v = None, 0.0, 0.0
        for b in range(4):
            rows = slice(b * quarter, (b + 1) * quarter)
            keys = heads_k[r, h, rows]
            probs = jnp.exp(dot_nt(keys, heads_q[r, h]))
            low = (probs * dot_nt(heads_v[r, h, rows], head_grad[h])).astype(BF16)
            dv = jnp.where(lane < HEAD_DIM, dot_nn(probs.astype(BF16), head_grad[h]), 0.0)
            dk = unrotate(r, rows, jnp.where(lane < HEAD_DIM, dot_nn(low, heads_q[r, h]), 0.0))
            dp_low[r, rows, first:second] = pltpu.roll(dk, HEAD_DIM, 1).astype(BF16)
            dp_low[r, rows, second : second + LANE] = dv.astype(BF16)
            bias_k += jnp.sum(dk, axis=0, keepdims=True)
            bias_v += jnp.sum(dv, axis=0, keepdims=True)
            one = dot_tn(keys, low)
            dq_total = one if dq_total is None else dq_total + one
        dq_total = jnp.transpose(dq_total)
        bias_q = 0.0
        for b in range(4):
            rows = slice(b * quarter, (b + 1) * quarter)
            dq = unrotate(r, rows, jnp.where(lane < HEAD_DIM, dq_total[rows], 0.0) * HEAD_DIM**-0.5)
            dp_low[r, rows, first:second] = (dp_low[r, rows, first:second].astype(F32) + dq).astype(BF16)
            bias_q += jnp.sum(dq, axis=0, keepdims=True)
        sums[7:8, first:second] = sums[7:8, first:second] + bias_q + pltpu.roll(bias_k, HEAD_DIM, 1)
        sums[7:8, second : second + LANE] = sums[7:8, second : second + LANE] + bias_v

    def close_back(r, link):
        sum_all(link, 0, r, lambda q: dot_nn(dp_low[r, rows_of(q)], wc[...]))

    def back_first_norm(r):
        def body(rows):
            incoming = sum_total(0, r, rows)
            normed, inv_std = normalize(first_tokens(r, rows))
            grad = gm[r, t, rows].astype(F32) + norm_back(incoming, normed, inv_std, attn_gain)
            ingrad[r, rows] = grad.astype(BF16)
            add_sum(0, incoming * normed)
            add_sum(1, incoming)

        over_chunks(quarter, body)

    def tall(ref, r, here):
        return ref[r, :, :, here].reshape(4 * quarter, here.stop - here.start)

    everything = slice(0, features)

    def feed_grad(left, right, target, here):
        total = sum(dot_tn(tall(left, r, here), tall(right, r, everything)) for r in range(2))
        target[here] = total.astype(BF16)

    def out_grad():
        for h in range(3):
            total = sum(dot_tn(head_out[r, h], tall(gm, r, everything)) for r in range(2))
            gout[h * HEAD_DIM : (h + 1) * HEAD_DIM] = total[0:HEAD_DIM].astype(BF16)

    def qkv_grad(h):
        here = slice(2 * LANE * h, 2 * LANE * (h + 1))
        total = sum(dot_tn(dp_low[r, :, here], tall(n1, r, everything)) for r in range(2))
        gqkv[h] = total[0 : 3 * HEAD_DIM].astype(BF16)

    piece, half = features // 4, features // 2
    reduces, used = {}, 0
    for i, name in enumerate(SUMS):
        at = int(name[1:] or 0)
        if name[0] in "DU":
            ref, out = ((gdown, gdown_out) if name[0] == "D" else (gup, gup_out))
            ref, out = ref.at[pl.ds(piece * at, piece)], out.at[pl.ds(piece * at, piece)]
        else:
            ref, out = (gout, gout_out) if name == "O" else (gqkv.at[at], gqkv_out.at[at])
        groups = sum_groups(dp_steps, name)
        size = Reduce.land_rows(*ref.shape, groups)
        reduces[name] = Reduce(copies, ref, land_sums.at[pl.ds(used, size)], out, out_sems.at[2 + i], groups, d, t)
        used += size

    def settle(own, back):
        def body(rows):
            mine, returned = own[1, rows].astype(F32), back[rows].astype(F32)
            middle = jnp.where(carried_wide(), returned, mine)
            own[1, rows] = jnp.where(count_wide >= 2, middle, 0.0).astype(BF16)
            own[2, rows] = jnp.where(count_wide >= 3, returned, 0.0).astype(BF16)

        over_chunks(quarter, body)

    store_mixed = pltpu.make_async_copy(mixed, mixed_out, out_sems.at[0])
    store_grad = pltpu.make_async_copy(ingrad, grad_out, out_sems.at[1])

    def count_codons(slot):
        logits = dot_nt(mixed[slot], head_ref[...])
        raised = jnp.exp(logits - jnp.max(logits, -1, keepdims=True))
        probs = raised / jnp.sum(raised, -1, keepdims=True)
        one = jnp.sum(probs, axis=0, keepdims=True)
        one = jnp.where(jnp.full(one.shape, count, jnp.int32) > slot, one, 0.0)
        codon_out[...] = one if slot == 0 else codon_out[...] + one

    def send_back(copy):
        @pl.when(d > 0)
        def _():
            copy().start()

    def get_back(copy):
        @pl.when(d > 0)
        def _():
            copy().wait_send()

        @pl.when(d < n_dp - 1)
        def _():
            copy().wait_recv()

    shared = lax.broadcasted_iota(jnp.int32, (8, features), 0) < 6
    sum_links, used = [], 0
    for clique in cliques:
        sum_links.append([(copies.make(sums, sums_land.at[used + i], other), used + i) for i, other in enumerate(clique)])
        used += len(clique)

    def small_start(k):
        for copy, _ in sum_links[k]:
            copy().start()

    def small_end(k):
        for copy, _ in sum_links[k]:
            copy().wait()
        extra = sum(sums_land[at] for _, at in sum_links[k])
        sums[...] = sums[...] + (jnp.where(shared, extra, 0.0) if k == 0 else extra)

    def begin():
        sums[...] = jnp.zeros_like(sums)
        pick_tail(tok_ref, tail_tok)
        tail_lens = lens_tile(slots - 1)
        for slot in range(slots - 2, -1, -1):
            tail_lens = jnp.where(jnp.full((8, LANE), count, jnp.int32) == slot + 1, lens_tile(slot), tail_lens)
        lens_mine[...] = tail_lens
        scan_mine[0] = jnp.full((8, LANE), count, jnp.int32)
        first_norm(0)
        pl.semaphore_wait(barrier, len(greeted))
        gather_start(links["n1A"])
        scan_start(0)

        @pl.when(d < n_dp - 1)
        def _():
            send_lens().start()
            send_tok().start()

        @pl.when(d == 0)
        def _():
            tok_b[...] = jnp.zeros_like(tok_b)
            got_cot[...] = jnp.zeros_like(got_cot)
            lens_land[...] = jnp.zeros_like(lens_land)

        @pl.when(d == n_dp - 1)
        def _():
            back_mixed[...] = jnp.zeros_like(back_mixed)
            back_grad[...] = jnp.zeros_like(back_grad)

        pick_tail(cotan_ref, tail_cot)
        load_cotangent(0)

    def prepare():
        empty = jnp.zeros((HEAD_DIM, features), BF16)
        for h in range(3):
            wc[2 * LANE * h + 3 * HEAD_DIM : 2 * LANE * (h + 1)] = empty
            woe[h * LANE + HEAD_DIM : (h + 1) * LANE] = empty
            bias = [bqkv_ref[j : j + 1, h * HEAD_DIM : (h + 1) * HEAD_DIM] for j in range(3)]
            bc[:, 2 * LANE * h : 2 * LANE * (h + 1)] = jnp.concatenate(bias + [jnp.zeros_like(bias[0])], axis=1)
        for load in loads:
            load.wait()

    def second_row():
        @pl.when(d > 0)
        def _():
            send_lens().wait_recv()
            send_tok().wait_recv()

        @pl.when(d < n_dp - 1)
        def _():
            send_lens().wait_send()
            send_tok().wait_send()
            send_cot().start()

        def pick(rows):
            value = jnp.where(carried_wide(), tok_b[rows].astype(F32), tok_ref[1, rows].astype(F32))
            tok_b[rows] = value.astype(BF16)

        over_chunks(quarter, pick)
        first_norm(1)

    steps = {"begin": begin, "prep": prepare, "LN1B": second_row, "cB": lambda: load_cotangent(1)}
    for k in range(dp_steps):

        def scan(k=k):
            scan_end(k)
            if k + 1 < dp_steps:
                scan_start(k + 1)

        steps["scan%d" % k] = scan

    def after_wait(ends, work, *args):
        def run():
            for name in ends:
                (gather_end if name[:-1] in ("n1", "c", "n2", "gm") else sum_end)(links[name])
            work(*args)

        return run

    for name, r in rows_ab.items():
        steps["tab" + name] = after_wait((), tables, r)
        steps["QKV" + name] = after_wait(("n1" + name,), project, r)
        steps["att" + name] = after_wait((), attend, r)
        steps["clO" + name] = after_wait((), close_attention, r, links["o" + name])
        steps["LN2" + name] = after_wait(("o" + name,), second_norm, r)
        steps["feed" + name] = after_wait(("n2" + name, "c" + name), feed, r, links["g" + name])
        steps["clF" + name] = after_wait((), close_feed, r, links["m" + name])
        steps["mix" + name] = after_wait(("m" + name,), finish_mixed, r)
        steps["cod" + name] = after_wait((), count_codons, r)
        steps["bk2" + name] = after_wait(("g" + name,), back_second_norm, r)
        steps["open" + name] = after_wait(("gm" + name,), open_heads, r)
        for h in range(3):
            steps["ab%d%s" % (h, name)] = after_wait((), attend_back, r, h)
        steps["clB" + name] = after_wait((), close_back, r, links["f" + name])
        steps["bk1" + name] = after_wait(("f" + name,), back_first_norm, r)

    def with_start(names, work, *args):
        def run():
            work(*args)
            for name in names:
                reduces[name].start()

        return run

    for i in (0, 2):
        here = slice(piece * i, piece * i + half)
        steps["D%d" % i] = with_start(("D%d" % i, "D%d" % (i + 1)), feed_grad, act, cot, gdown, here)
        steps["U%d" % i] = with_start(("U%d" % i, "U%d" % (i + 1)), feed_grad, n2, slope, gup, here)
    steps["O"] = with_start(("O",), out_grad)
    for h in range(3):
        steps["Q%d" % h] = with_start(("Q%d" % h,), qkv_grad, h)

    def settle_mixed():
        get_back(return_mixed)
        settle(mixed, back_mixed)
        store_mixed.start()
        count_codons(1)
        count_codons(2)

    def settle_grad():
        get_back(return_grad)
        settle(ingrad, back_grad)
        store_grad.start()

    steps["retM"] = lambda: send_back(return_mixed)
    steps["retG"] = lambda: send_back(return_grad)
    steps["setM"] = settle_mixed
    steps["setG"] = settle_grad
    for k in range(len(cliques)):

        def small(k=k):
            small_end(k)
            if k + 1 < len(cliques):
                small_start(k + 1)

        steps["sum%d" % k] = small
    steps["sums"] = lambda: small_start(0)

    starts = {"n1", "c", "n2", "gm"}
    for step in schedule(dp_steps, len(cliques)):
        kind, _, name = step.partition(":")
        if kind == "x":
            if name[:-1] in starts:
                gather_start(links[name])
            else:
                links[name][2]().start()
        elif kind == "p":
            gather_pass(links[name])
        elif kind == "t":
            reduces[name.partition(".")[0]].tick()
        else:
            steps[kind]()
    while any(each.left() for each in reduces.values()):
        for each in reduces.values():
            each.tick()
    small_out[...] = sums[...]
    for j in range(3):
        pieces = [sums[7:8, (4 * h + j) * HEAD_DIM : (4 * h + j + 1) * HEAD_DIM] for h in range(3)]
        qkv_bias_out[j : j + 1] = jnp.concatenate(pieces, axis=1)
    store_mixed.wait()
    store_grad.wait()


def body(
    tokens,
    cotangent,
    lengths,
    row_counts,
    attn_gain,
    attn_shift,
    qkv_weight,
    qkv_bias,
    out_weight,
    out_bias,
    ffn_gain,
    ffn_shift,
    up_weight,
    up_bias,
    down_weight,
    down_bias,
    head_weight,
    codon_freq,
):
    slots, quarter, features = tokens.shape
    n_dp = lax.axis_size("dp")
    steps = n_dp.bit_length() - 1
    length = 4 * quarter
    half = HEAD_DIM // 2
    freqs = np.float32(BASE) ** (-np.arange(half, dtype=np.float32) / np.float32(half))
    freq_lane = np.tile(freqs.astype(np.float32), LANE // half)
    sign = np.concatenate([-np.ones(half), np.ones(half), np.zeros(HEAD_DIM)]).astype(np.float32)

    def turned(places):
        angles = places[:, None].astype(np.float64) * freq_lane[None].astype(np.float64)
        return np.stack([np.cos(angles) * np.abs(sign), np.sin(angles) * sign]).astype(np.float32)

    rope, bases = turned(np.arange(CHUNK)), turned(np.arange(0, length, CHUNK))
    vectors = jnp.stack([attn_gain, attn_shift, out_bias, ffn_gain, ffn_shift, down_bias, up_bias, up_bias])
    vmem, smem = pl.BlockSpec(memory_space=pltpu.VMEM), pl.BlockSpec(memory_space=pltpu.SMEM)
    anywhere = pl.BlockSpec(memory_space=pl.ANY)
    wide = (quarter, features)

    def low(*shape):
        return pltpu.VMEM(shape, BF16)

    def full(*shape):
        return pltpu.VMEM(shape, F32)

    out_width = 3 * HEAD_DIM
    cliques = 3 + sum((1 << min(3, steps - k)) - 1 for k in range(0, steps, 3))
    sum_land = sum(Reduce.land_rows(features // 4, features, sum_groups(steps, name)) for name in SUMS)
    n_sums = sum(2 * ((1 << len(group)) - 1) for name in SUMS for group in sum_groups(steps, name))
    n_sems = 24 + 24 + 5 + steps + n_sums + cliques
    scratch = [
        low(2, 4, *wide),
        low(2, 4, *wide),
        low(2, 4, *wide),
        low(2, 4, *wide),
        low(2, 3, length, LANE),
        low(2, 3, length, LANE),
        low(2, 3, length, LANE),
        low(2, 3, length, LANE),
        low(3, length, LANE),
        low(2, length, 6 * LANE),
        low(2, 4, *wide),
        low(2, 4, *wide),
        low(2, 2, 4, *wide),
        low(2, 2, 2, *wide),
        low(2, 2, *wide),
        full(2, *wide),
        full(2, length, LANE),
        full(2, length, LANE),
        low(6 * LANE, features),
        full(1, 6 * LANE),
        low(3 * LANE, features),
        low(*wide),
        low(*wide),
        pltpu.VMEM((steps + 1, 8, LANE), jnp.int32),
        pltpu.VMEM((steps, 8, LANE), jnp.int32),
        pltpu.VMEM((8, LANE), jnp.int32),
        pltpu.VMEM((8, LANE), jnp.int32),
        low(features, features),
        low(features, features),
        low(out_width, features),
        low(3, out_width, features),
        low(sum_land, features),
        low(*wide),
        low(*wide),
        full(8, features),
        full(cliques, 8, features),
        pltpu.SemaphoreType.DMA((n_sems,)),
        pltpu.SemaphoreType.DMA((n_sems,)),
        pltpu.SemaphoreType.DMA((2 + len(SUMS),)),
        pltpu.SemaphoreType.DMA((12,)),
    ]
    outs = pl.pallas_call(
        functools.partial(layer_kernel, n_dp, slots, quarter, features),
        out_shape=(
            jax.ShapeDtypeStruct(tokens.shape, BF16),
            jax.ShapeDtypeStruct(tokens.shape, BF16),
            jax.ShapeDtypeStruct((features, features), BF16),
            jax.ShapeDtypeStruct((features, features), BF16),
            jax.ShapeDtypeStruct((out_width, features), BF16),
            jax.ShapeDtypeStruct((3, out_width, features), BF16),
            jax.ShapeDtypeStruct((8, features), F32),
            jax.ShapeDtypeStruct((3, out_width), F32),
            jax.ShapeDtypeStruct((1, head_weight.shape[1]), F32),
        ),
        in_specs=[smem, smem, vmem, vmem, anywhere, vmem, anywhere] + [vmem] * 8,
        out_specs=(anywhere,) * 6 + (vmem,) * 3,
        scratch_shapes=scratch,
        compiler_params=pltpu.CompilerParams(
            collective_id=0, has_side_effects=True, vmem_limit_bytes=64 * 1024 * 1024
        ),
    )(
        row_counts,
        lengths,
        tokens,
        cotangent,
        jnp.swapaxes(qkv_weight, 1, 2),
        qkv_bias,
        out_weight,
        up_weight,
        down_weight,
        vectors,
        head_weight.T,
        jnp.asarray(freq_lane[None]),
        jnp.asarray(rope),
        jnp.asarray(bases),
        jnp.asarray(sign[None]),
    )
    mixed, input_grad, gdown, gup, gout, gqkv, small, qkv_bias_grad, codon = outs
    mean_prob = codon / (row_counts[0] * quarter).astype(F32)
    codon_gap = (jnp.log(mean_prob) - jnp.log(codon_freq)).reshape(1, 1, -1)
    by_head = gqkv.reshape(3, 3, HEAD_DIM, features).swapaxes(0, 1).reshape(3, out_width, features)
    qkv_grad = jnp.swapaxes(by_head.astype(F32), 1, 2)
    return (
        mixed,
        input_grad,
        small[0],
        small[1],
        qkv_grad,
        qkv_bias_grad,
        gout.astype(F32),
        small[2],
        small[3],
        small[4],
        gup.astype(F32),
        small[6],
        gdown.astype(F32),
        small[5],
        codon_gap,
    )


def solution(mesh):
    placed = (
        P("dp", "tensor", None),
        P("dp", "tensor", None),
        P("dp", None),
        P("dp"),
        P(),
        P(),
        P(None, None, "tensor"),
        P(None, "tensor"),
        P("tensor", None),
        P(),
        P(),
        P(),
        P(None, "tensor"),
        P("tensor"),
        P("tensor", None),
        P(),
        P(),
        P(),
    )
    return jax.shard_map(
        body,
        mesh=mesh,
        in_specs=placed,
        out_specs=(
            P("dp", "tensor", None),
            P("dp", "tensor", None),
            P(),
            P(),
            P(None, None, "tensor"),
            P(None, "tensor"),
            P("tensor", None),
            P(),
            P(),
            P(),
            P(None, "tensor"),
            P("tensor"),
            P("tensor", None),
            P(),
            P("dp", "tensor", None),
        ),
        check_vma=False,
    )
```

```python
import functools

import jax
import jax.numpy as jnp
import numpy as np
from jax import lax
from jax.experimental import pallas as pl
from jax.experimental.pallas import tpu as pltpu
from jax.sharding import PartitionSpec as P

HEAD_DIM = 64
EPS = 1e-05
BASE = 10000.0
F32 = jnp.float32
BF16 = jnp.bfloat16
MESH = pl.DeviceIdType.MESH
LANE = 128
CHUNK = 64
FAR = -1e30
MASK_AT = 64
TOTAL_AT = 68
SUMS = {
    "D0": ((1,), (0,), (2,)),
    "D1": ((0,), (1,), (2,)),
    "D2": ((0, 1, 2),),
    "D3": ((0,), (1,), (2,)),
    "U0": ((1,), (2,), (0,)),
    "U1": ((0,), (1,), (2,)),
    "U2": ((0,), (1,), (2,)),
    "U3": ((0,), (1,), (2,)),
    "O": ((1,), (0,), (2,)),
    "Q0": ((0,), (1,), (2,)),
    "Q1": ((0,), (1,), (2,)),
    "Q2": ((0,), (1,), (2,)),
}


def dot_nn(a, b):
    return lax.dot_general(a, b, (((1,), (0,)), ((), ())), preferred_element_type=F32)


def dot_nt(a, b):
    return lax.dot_general(a, b, (((1,), (1,)), ((), ())), preferred_element_type=F32)


def dot_tn(a, b):
    return lax.dot_general(a, b, (((0,), (0,)), ((), ())), preferred_element_type=F32)


def lanes(shape):
    return lax.broadcasted_iota(jnp.int32, shape, 1)


def three_parts(value):
    high = value.astype(BF16).astype(F32)
    rest = value - high
    middle = rest.astype(BF16).astype(F32)
    return high, middle, rest - middle


def normalize(value):
    average = jnp.mean(value, -1, keepdims=True)
    centred = value - average
    inv_std = lax.rsqrt(jnp.mean(centred * centred, -1, keepdims=True) + EPS)
    return centred * inv_std, inv_std


def norm_back(incoming, normed, inv_std, gain):
    scaled = incoming * gain
    return inv_std * (
        scaled
        - jnp.mean(scaled, -1, keepdims=True)
        - normed * jnp.mean(scaled * normed, -1, keepdims=True)
    )


def swap_halves(value):
    lane = lanes(value.shape)
    return jnp.where(lane < 32, pltpu.roll(value, 96, 1), pltpu.roll(value, 32, 1))


class Copies:
    def __init__(self, send, recv):
        self.send, self.recv, self.count = send, recv, 0

    def make(self, src, dst, device):
        at = self.count
        self.count += 1
        return functools.partial(
            pltpu.make_async_remote_copy,
            src_ref=src,
            dst_ref=dst,
            send_sem=self.send.at[at],
            recv_sem=self.recv.at[at],
            device_id=device,
            device_id_type=MESH,
        )


class Region:
    def __init__(self, row, rows, lane, width):
        self.row, self.rows, self.lane, self.width = row, rows, lane, width

    def halves(self, side):
        if self.rows % 32 == 0:
            half = self.rows // 2
            cut = [Region(self.row + half * k, half, self.lane, self.width) for k in (side, 1 - side)]
        elif self.width % (2 * LANE) == 0:
            half = self.width // 2
            cut = [Region(self.row, self.rows, self.lane + half * k, half) for k in (side, 1 - side)]
        else:
            cut = None
        return cut

    def of(self, ref, start=0, rows=None):
        row, lane = self.row + start, self.lane
        if not isinstance(row, int):
            row = pl.multiple_of(row, 16)
        if not isinstance(lane, int):
            lane = pl.multiple_of(lane, LANE)
        return ref.at[pl.ds(row, rows or self.rows), pl.ds(lane, self.width)]


class Places:
    def __init__(self, width):
        self.width, self.used, self.spare = width, 0, []

    def take(self, region):
        at = (self.used, 0)
        if 2 * region.width == self.width:
            if (region.rows, region.width) in [size for size, _ in self.spare]:
                i = [size for size, _ in self.spare].index((region.rows, region.width))
                return self.spare.pop(i)[1]
            self.spare.append(((region.rows, region.width), Region(self.used, region.rows, region.width, region.width)))
        self.used += region.rows
        return Region(at[0], region.rows, at[1], region.width)


class Reduce:
    def __init__(self, copies, ref, land, out, store_sem, groups, d, t):
        self.ref, self.land = ref, land
        self.plan = []
        rows, width = ref.shape
        region, place, backs = Region(0, rows, 0, width), Places(width), []
        for group in groups:
            sends, mine = [], self.part(region, group, [(d >> bit) & 1 for bit in group])
            for mask in range(1, 1 << len(group)):
                turned = [(mask >> i) & 1 for i in range(len(group))]
                partner = (d ^ sum(turn << bit for turn, bit in zip(turned, group)), t)
                give = self.part(region, group, [((d >> bit) & 1) ^ turn for turn, bit in zip(turned, group)])
                there = place.take(mine)
                sends.append((copies.make(give.of(ref), there.of(land), partner), there, partner))
            self.plan.append(([copy for copy, _, _ in sends], mine, [there for _, there, _ in sends]))
            if mine.rows * mine.width < region.rows * region.width:
                backs.append((mine, [partner for _, _, partner in sends]))
            region = mine
        self.adds = len(self.plan)
        self.store = functools.partial(pltpu.make_async_copy, region.of(ref), region.of(out), store_sem)
        for i, (region, partners) in enumerate(reversed(backs)):
            own = region.of(ref if i == 0 else out)
            self.plan.append(([copies.make(own, region.of(out), partner) for partner in partners], region, ()))
        self.place = 0

    @staticmethod
    def part(region, group, sides):
        for side in sides:
            region = (region.halves(side) or (region,))[0]
        return region

    @staticmethod
    def land_rows(rows, width, groups):
        region, place = Region(0, rows, 0, width), Places(width)
        for group in groups:
            region = Reduce.part(region, group, [0] * len(group))
            for _ in range(1, 1 << len(group)):
                place.take(region)
        return place.used

    def start(self):
        for copy in self.plan[0][0]:
            copy().start()

    def left(self):
        return len(self.plan) - self.place

    def tick(self):
        if self.place >= len(self.plan):
            return
        group, region, landed = self.plan[self.place]
        for copy in group:
            copy().wait()
        if landed:
            step = max(size for size in (16, 32, 48, 64, 96) if region.rows % size == 0)

            def add(i, _):
                here = region.of(self.ref, i * step, step)
                total = here[...].astype(F32)
                for there in landed:
                    total += there.of(self.land, i * step, step)[...].astype(F32)
                here[...] = total.astype(BF16)
                return _

            lax.fori_loop(0, region.rows // step, add, None)
        if self.place == self.adds - 1:
            self.store().start()
        if self.place == self.adds or (self.place + 1 == len(self.plan) and self.place < self.adds):
            self.store().wait()
        self.place += 1
        if self.place < len(self.plan):
            for copy in self.plan[self.place][0]:
                copy().start()


def sum_groups(steps, name):
    first = [tuple(bit for bit in group if bit < steps) for group in SUMS[name]]
    return [group for group in first if group] + [(bit,) for bit in range(3, steps)]


def schedule(dp_steps, cliques):
    names = (
        "begin", "scan0", "tabA", "prep", "QK0A", "scan1", "scan2", "p:tA", "LN1B", "tabB", "QK0B", "x:cA", "QK1A",
        "attA", "cB", "p:tB", "hpA", "QK1B", "attB", "p:w", "hpB", "x:cB", "p:cA", "LN2A", "fe0A", "LN2B", "fe1A",
        "clFA", "p:cB", "fe0B", "fe1B", "U0", "D2", "U2", "bk2A", "x:gmA", "t:U1", "D0", "bk2B", "op0A", "t:U1",
        "x:gmB", "t:D3", "t:U0", "clFB", "t:U2", "t:U1", "p:gmA", "t:U3", "t:D3", "t:D0", "x:mB", "t:D2", "op1A",
        "ab0A", "t:D1", "t:U2", "t:U0", "ab1A", "t:D3", "t:D0", "t:U1", "p:gmB", "ab2A", "t:U3", "t:U2", "x:mA",
        "op0B", "t:U0", "mixB", "retM", "op1B", "ab0B", "t:U3", "O", "Q0", "ab1B", "t:D1", "Q1", "t:D3", "t:U0",
        "ab2B", "t:Q0", "t:O", "t:D0", "Q2", "t:U1", "t:U2", "t:D1", "t:D3", "t:Q1", "clBB", "t:Q0", "t:U3", "mixA",
        "t:U2", "t:O", "t:Q2", "t:D0", "codA", "t:D2", "t:Q1", "t:Q0", "t:U1", "t:D1", "clBA", "t:O", "t:U3", "t:Q2",
        "t:Q0", "t:Q1", "bk1B", "retG", "t:O", "t:Q0", "t:Q2", "setM", "t:D1", "t:Q1", "bk1A", "t:U0", "t:U2", "sums",
        "t:Q2", "sum0", "t:Q1", "t:D0", "t:Q0", "t:O", "t:Q2", "sum1", "t:D3", "t:U0", "t:D1", "t:U3", "setG", "t:D0",
        "t:Q1", "t:Q2", "t:O",
    )
    for name in names:
        if name in ("scan2", "sum1"):
            count = dp_steps if name == "scan2" else cliques
            yield from (name[:-1] + str(k) for k in range(int(name[-1]), count))
        else:
            yield name


def layer_kernel(
    n_dp,
    slots,
    quarter,
    features,
    count_ref,
    lens_ref,
    tok_ref,
    cotan_ref,
    wqkv_ref,
    bqkv_ref,
    wout_ref,
    wup_ref,
    wdown_ref,
    attn_gain_ref,
    attn_shift_ref,
    out_bias_ref,
    ffn_gain_ref,
    ffn_shift_ref,
    down_bias_ref,
    up_bias_ref,
    head_ref,
    freq_ref,
    rope_ref,
    base_ref,
    line_ref,
    mixed_out,
    grad_out,
    gdown_out,
    gup_out,
    gout_out,
    gqkv_out,
    small_out,
    qkv_bias_out,
    codon_out,
    n1,
    n2,
    cot,
    gm,
    heads_q,
    heads_k,
    heads_v,
    head_out,
    head_grad,
    dp_low,
    act,
    slope,
    part,
    land_core,
    land_x,
    mid,
    table_c,
    table_s,
    wc,
    bc,
    wcat,
    tok_b,
    tok_x,
    got_cot,
    scan_mine,
    scan_land,
    lens_mine,
    lens_land,
    gdown,
    gup,
    gout,
    gqkv,
    land_sums,
    back_mixed,
    back_grad,
    sums,
    sums_land,
    vec,
    send_sems,
    recv_sems,
    out_sems,
    load_sems,
):
    d, t = lax.axis_index("dp"), lax.axis_index("tensor")
    core, across = (d, t ^ 1), (d, t ^ 2)
    own_rows = slots - 1
    dp_steps = n_dp.bit_length() - 1
    copies = Copies(send_sems, recv_sems)
    rows_ab = {"A": 0, "B": 1}

    vectors = (attn_gain_ref, attn_shift_ref, out_bias_ref, ffn_gain_ref, ffn_shift_ref, down_bias_ref, up_bias_ref)
    for i, ref in enumerate(vectors):
        vec[i : i + 1] = ref[...].reshape(1, features)
    attn_gain, attn_shift = vec[0:1], vec[1:2]
    out_bias, ffn_gain, ffn_shift, down_bias, up_bias = (vec[i : i + 1] for i in range(2, 7))

    cliques = [[(d, t ^ m) for m in range(1, 4)]]
    for low_bit in range(0, dp_steps, 3):
        width = min(3, dp_steps - low_bit)
        cliques.append([(d ^ (m << low_bit), t) for m in range(1, 1 << width)])
    greeted = [other for clique in cliques for other in clique]
    for k in range(dp_steps):
        greeted.append(((d + (1 << k)) % n_dp, t))
        greeted.append(((d + n_dp - (1 << k)) % n_dp, t))
    barrier = pltpu.get_barrier_semaphore()
    for other in greeted:
        pl.semaphore_signal(barrier, inc=1, device_id=other, device_id_type=MESH)

    loads = []
    for h in range(3):
        for j in range(3):
            source = wqkv_ref.at[j, pl.ds(h * HEAD_DIM, HEAD_DIM)]
            target = wc.at[pl.ds(2 * LANE * h + HEAD_DIM * j, HEAD_DIM)]
            loads.append(pltpu.make_async_copy(source, target, load_sems.at[len(loads)]))
    out_width = 3 * HEAD_DIM
    half_lanes = features // 2
    load_out = pltpu.make_async_copy(wout_ref, wcat.at[0, pl.ds(0, out_width)], load_sems.at[len(loads)])
    load_out.start()
    for load in loads:
        load.start()

    def over_chunks(rows, body, step=CHUNK):
        def run(i, _):
            body(pl.ds(pl.multiple_of(i * step, step), step))
            return _

        lax.fori_loop(0, rows // step, run, None)

    mixed, ingrad = n2.at[0, pl.ds(0, slots)], n2.at[1, pl.ds(0, slots)]

    tail_tok, tail_cot = mixed.at[slots - 1], ingrad.at[slots - 1]
    count = count_ref[0]
    count_wide = jnp.full((CHUNK, features), count, jnp.int32)

    def pick_tail(source, target):
        def body(rows):
            value = source[slots - 1, rows].astype(F32)
            for slot in range(slots - 2, -1, -1):
                value = jnp.where(count_wide == slot + 1, source[slot, rows].astype(F32), value)
            target[rows] = value.astype(BF16)

        over_chunks(quarter, body)

    after, before = (d + 1, t), (d - 1, t)
    send_tok = copies.make(tail_tok, tok_b, after)
    send_cot = copies.make(tail_cot, got_cot, after)
    send_lens = copies.make(lens_mine, lens_land, after)
    return_mixed = copies.make(mixed.at[1], back_mixed, before)
    return_grad = copies.make(ingrad.at[1], back_grad, before)

    def lens_tile(slot):
        row_at = lax.broadcasted_iota(jnp.int32, (8, LANE), 0)
        tile = jnp.zeros((8, LANE), jnp.int32)
        for gene in range(4):
            tile = jnp.where(row_at == gene, lens_ref[slot, gene], tile)
        return tile

    scan_copies = [copies.make(scan_mine.at[k], scan_land.at[k], (d + (1 << k), t)) for k in range(dp_steps)]

    def scan_start(k):
        @pl.when(d + (1 << k) < n_dp)
        def _():
            scan_copies[k]().start()

    def scan_end(k):
        scan_mine[k + 1] = scan_mine[k]

        @pl.when(d + (1 << k) < n_dp)
        def _():
            scan_copies[k]().wait_send()

        @pl.when(d >= (1 << k))
        def _():
            scan_copies[k]().wait_recv()
            scan_mine[k + 1] = scan_mine[k] + scan_land[k]

    def carried_tile():
        return (scan_mine[dp_steps] - count - d * own_rows) > 0

    def carried_wide():
        return jnp.broadcast_to(carried_tile()[0:1, 0:1], (CHUNK, features))

    heads_x = land_x.at[1]

    def gather(full, r):
        mine = full.at[r, t]
        return (
            copies.make(mine, mine, across),
            copies.make(mine, mine, core),
            copies.make(full.at[r, t ^ 2], full.at[r, t ^ 2], core),
        )

    def gather_start(link):
        link[0]().start()
        link[1]().start()

    def gather_pass(link):
        link[0]().wait_recv()
        link[2]().start()

    def gather_end(link):
        link[0]().wait_send()
        link[1]().wait()
        link[2]().wait()

    def summing(kind, r):
        return (
            copies.make(part.at[kind, r, t ^ 1], land_core.at[kind, r, 0], core),
            copies.make(part.at[kind, r, t ^ 3], land_core.at[kind, r, 1], core),
            copies.make(part.at[kind, r, t ^ 2], land_x.at[kind, r], across),
        )

    def quarter_of(i):
        return t ^ jnp.where(i == 0, 3, jnp.where(i == 3, 0, i))

    def sum_step(link, kind, r, i, q, value):
        @pl.when(i < 2)
        def _():
            part[kind, r, q] = value.astype(BF16)

        @pl.when(i == 0)
        def _():
            link[1]().start()

        @pl.when(i == 1)
        def _():
            link[0]().start()

        @pl.when(i == 2)
        def _():
            link[1]().wait_recv()
            part[kind, r, q] = (value + land_core[kind, r, 1].astype(F32)).astype(BF16)
            if kind == 0:
                link[2]().start()

        @pl.when(i == 3)
        def _():
            part[kind, r, q] = value.astype(BF16)

    def sum_all(link, kind, r, make_part):
        def run(i, _):
            q = quarter_of(i)
            sum_step(link, kind, r, i, q, make_part(q))
            return _

        lax.fori_loop(0, 4, run, None)

    def sum_end(link):
        link[0]().wait()
        link[1]().wait_send()
        link[2]().wait()

    def sum_total(kind, r, rows):
        near = part[kind, r, t, rows].astype(F32) + land_core[kind, r, 0, rows].astype(F32)
        return near + land_x[kind, r, rows].astype(F32)

    links = {}
    for name, r in rows_ab.items():
        for key, full in (("c", cot), ("gm", gm)):
            links[key + name] = gather(full, r)
        for key, kind in (("g", 0), ("f", 0), ("m", 1)):
            links[key + name] = summing(kind, r)
        source = tok_ref.at[0] if r == 0 else tok_b
        links["t" + name] = (
            copies.make(source, tok_x.at[r], across),
            copies.make(n1.at[r, t], n1.at[r, t], core),
            copies.make(n1.at[r, t ^ 2], n1.at[r, t ^ 2], core),
        )
        links["h" + name] = tuple(
            copies.make(part.at[0, r, t ^ m, :, pl.ds(0, half_lanes)], land_core.at[0, r, s, :, pl.ds(0, half_lanes)], core)
            for s, m in ((0, 1), (1, 3))
        ) + tuple(
            copies.make(
                part.at[0, r, t ^ m, :, pl.ds(half_lanes, half_lanes)],
                heads_x.at[r, :, pl.ds(half_lanes * s, half_lanes)],
                across,
            )
            for s, m in ((1, 0), (0, 2))
        )
        links["n2" + name] = tuple(copies.make(n2.at[r, t ^ m], n2.at[r, t ^ m], core) for m in (0, 2))
    own_out, got_out = wcat.at[0, pl.ds(0, out_width)], wcat.at[1, pl.ds(0, out_width)]
    links["w"] = (
        copies.make(own_out, got_out, across),
        copies.make(own_out, wcat.at[0, pl.ds(out_width, out_width)], core),
        copies.make(got_out, wcat.at[1, pl.ds(out_width, out_width)], core),
    )

    def rows_of(q):
        return pl.ds(pl.multiple_of(q * quarter, quarter), quarter)

    def add_sum(row, value):
        sums[row : row + 1] = sums[row : row + 1] + jnp.sum(value, axis=0, keepdims=True)

    def first_tokens(r, rows):
        return (tok_ref[0, rows] if r == 0 else tok_b[rows]).astype(F32)

    def first_norm(r, theirs=False):
        def body(rows):
            normed, _ = normalize(tok_x[r, rows].astype(F32) if theirs else first_tokens(r, rows))
            n1[r, t ^ 2 if theirs else t, rows] = (normed * attn_gain + attn_shift).astype(BF16)

        over_chunks(quarter, body)

    def pass_tokens(r, link):
        link[0]().wait_recv()
        first_norm(r, theirs=True)
        link[2]().start()

    def load_cotangent(r):
        if r == 1:

            @pl.when(d > 0)
            def _():
                send_cot().wait_recv()

            @pl.when(d < n_dp - 1)
            def _():
                send_cot().wait_send()

        def body(rows):
            value = cotan_ref[0, rows].astype(F32)
            if r == 1:
                value = jnp.where(carried_wide(), got_cot[rows].astype(F32), cotan_ref[1, rows].astype(F32))
            cot[r, t, rows] = value.astype(BF16)
            add_sum(5, value)

        over_chunks(quarter, body)

    def ends_of(r):
        tile = lens_tile(0) if r == 0 else jnp.where(carried_tile(), lens_land[...], lens_tile(1))
        first = tile[0:1]
        second = first + tile[1:2]
        return first, second, second + tile[2:3]

    def segment_of(ends, base, rows):
        place = lax.broadcasted_iota(jnp.int32, (rows, LANE), 0) + base
        return [place >= end for end in ends]

    def tables(r):
        ends = ends_of(r)
        turns = [end.astype(F32) * freq_ref[...] for end in ends]
        cosines = [jnp.cos(turn) for turn in turns]
        sines = [jnp.sin(turn) * line_ref[...] for turn in turns]

        def body(rows):
            passed = segment_of(ends, rows.start, CHUNK)
            at = pl.ds(rows.start // CHUNK, 1)
            cos_base, sin_base = base_ref[0, at], base_ref[1, at]
            cos_start = jnp.broadcast_to(cos_base, (CHUNK, LANE))
            sin_start = jnp.broadcast_to(sin_base, (CHUNK, LANE))
            for ge, cosine, sine in zip(passed, cosines, sines):
                cos_start = jnp.where(ge, cos_base * cosine + sin_base * sine, cos_start)
                sin_start = jnp.where(ge, sin_base * cosine - cos_base * sine, sin_start)
            cos_place, sin_place = rope_ref[0], rope_ref[1]
            table_c[r, rows] = cos_place * cos_start - sin_place * sin_start
            table_s[r, rows] = sin_place * cos_start + cos_place * sin_start

        over_chunks(4 * quarter, body)

    def project(r, first):
        ends = ends_of(r)

        def run(i, _):
            q = t ^ (i + first)
            rows = rows_of(q)
            both = dot_nt(n1[r, q], wc[...]) + bc[...]
            lane = lanes((quarter, LANE))
            ge = segment_of(ends, q * quarter, quarter)
            gene = sum(g.astype(jnp.int32) for g in ge)
            in_mask = (lane >= MASK_AT) & (lane < TOTAL_AT)
            same = in_mask & (lane - MASK_AT == gene)
            extra_q = jnp.where(in_mask & ~same, FAR, 0.0)
            extra_k = jnp.where(same | ((lane >= TOTAL_AT) & (lane < TOTAL_AT + 3)), 1.0, 0.0)
            extra_v = jnp.where((lane >= MASK_AT) & (lane < MASK_AT + 3), 1.0, 0.0)
            cosine, sine = table_c[r, rows], table_s[r, rows]
            for h in range(3):
                query = both[:, 2 * LANE * h : 2 * LANE * h + LANE]
                key = pltpu.roll(query, HEAD_DIM, 1)
                value = both[:, 2 * LANE * h + LANE : 2 * LANE * (h + 1)]
                query = (query * cosine + swap_halves(query) * sine) * HEAD_DIM**-0.5 + extra_q
                key = key * cosine + swap_halves(key) * sine + extra_k
                heads_q[r, h, rows] = query.astype(BF16)
                heads_k[r, h, rows] = key.astype(BF16)
                heads_v[r, h, rows] = (value + extra_v).astype(BF16)
            return _

        lax.fori_loop(0, 2, run, None)

    def attend(r, link):
        def run(q, _):
            rows = rows_of(q)
            lane = lanes((quarter, LANE))
            queries = [heads_q[r, h, rows] for h in range(3)]
            scores = [dot_nt(queries[h], heads_k[r, h]) for h in range(3)]
            for h in range(3):
                top = jnp.max(scores[h], -1, keepdims=True)
                probs = jnp.exp(scores[h] - top).astype(BF16)
                mixed_values = dot_nn(probs, heads_v[r, h])
                total = mixed_values[:, MASK_AT : MASK_AT + 1]
                out = jnp.where(lane < HEAD_DIM, mixed_values * (1.0 / total), 0.0).astype(BF16)
                head_out[r, h, rows] = out
                part[0, r, q, :, h * LANE : (h + 1) * LANE] = out
                query = queries[h].astype(F32)
                for at, value in enumerate(three_parts(-(top + jnp.log(total)))):
                    query = jnp.where(lane == TOTAL_AT + at, value, query)
                heads_q[r, h, rows] = query.astype(BF16)
            return _

        lax.fori_loop(0, 4, run, None)
        link[1]().start()
        link[0]().start()

    def pack_heads(r, link):
        for s, m in ((1, 2), (0, 0)):
            link[s]().wait_recv()
            q = t ^ m
            blocks = [part[0, r, q, :, h * LANE : (h + 1) * LANE].astype(F32) for h in range(3)]
            blocks += [land_core[0, r, s, :, h * LANE : (h + 1) * LANE].astype(F32) for h in range(3)]
            for j in range(3):
                pair = blocks[2 * j] + pltpu.roll(blocks[2 * j + 1], HEAD_DIM, 1)
                part[0, r, q, :, half_lanes + j * LANE : half_lanes + (j + 1) * LANE] = pair.astype(BF16)
            link[3 if m else 2]().start()

    def second_norm(r, heads, out):
        for s, m in ((1, 2), (0, 0)):
            q = t ^ m
            near = dot_nn(part[0, r, q, :, half_lanes:], wcat[0])
            heads[2 if s else 3]().wait_recv()
            attention = near + dot_nn(heads_x[r, :, half_lanes * s : half_lanes * (s + 1)], wcat[1])
            for k in range(quarter // CHUNK):
                rows = slice(k * CHUNK, (k + 1) * CHUNK)
                tokens = tok_x[r, rows].astype(F32) if s else first_tokens(r, rows)
                middle = tokens + attention[rows] + out_bias
                if s == 0:
                    mid[r, rows] = middle
                normed, _ = normalize(middle)
                n2[r, q, rows] = (normed * ffn_gain + ffn_shift).astype(BF16)
            out[1 if m else 0]().start()
        for copy in heads:
            copy().wait_send()

    def feed(r, q):
        hidden = dot_nn(n2[r, q], wup_ref[...]) + up_bias
        below = 0.5 * (1.0 + lax.erf(hidden * 0.5**0.5))
        density = jnp.exp(hidden * hidden * -0.5) * (2.0 * np.pi) ** -0.5
        act[r, q] = (hidden * below).astype(BF16)
        grad = dot_nt(cot[r, q], wdown_ref[...]) * (below + hidden * density)
        add_sum(6, grad)
        low = grad.astype(BF16)
        slope[r, q] = low
        part[0, r, q] = dot_nt(low, wup_ref[...]).astype(BF16)

    def feed_own(r):
        def run(i, _):
            feed(r, t ^ (2 - 2 * i))
            return _

        lax.fori_loop(0, 2, run, None)

    def feed_other(r, link):
        def run(i, _):
            feed(r, t ^ (3 - 2 * i))

            @pl.when(i == 0)
            def _():
                link[1]().start()

            @pl.when(i == 1)
            def _():
                link[0]().start()

            return _

        lax.fori_loop(0, 2, run, None)
        link[1]().wait_recv()

        def add(rows):
            total = part[0, r, t ^ 2, rows].astype(F32) + land_core[0, r, 1, rows].astype(F32)
            part[0, r, t ^ 2, rows] = total.astype(BF16)

        over_chunks(quarter, add)
        link[2]().start()

    def close_feed(r, link):
        sum_all(link, 1, r, lambda q: dot_nn(act[r, q], wdown_ref[...]))

    def finish_mixed(r):
        def body(rows):
            mixed[r, rows] = (mid[r, rows] + sum_total(1, r, rows) + down_bias).astype(BF16)

        over_chunks(quarter, body)

    def back_second_norm(r):
        def body(rows):
            incoming = sum_total(0, r, rows)
            normed, inv_std = normalize(mid[r, rows])
            grad = cot[r, t, rows].astype(F32) + norm_back(incoming, normed, inv_std, ffn_gain)
            gm[r, t, rows] = grad.astype(BF16)
            add_sum(3, incoming * normed)
            add_sum(4, incoming)
            add_sum(2, grad)

        over_chunks(quarter, body)

    def open_heads(r, first):
        def run(i, _):
            q = t ^ (i + first)
            rows = rows_of(q)
            grads = dot_nt(gm[r, q], wcat[0, 0 : 2 * LANE])
            lane = lanes((quarter, LANE))
            pair, last = grads[:, 0:LANE], grads[:, LANE : 2 * LANE]
            for h, low in enumerate((pair, pltpu.roll(pair, HEAD_DIM, 1), last)):
                low = jnp.where(lane < HEAD_DIM, low, 0.0).astype(BF16).astype(F32)
                dots = jnp.sum(low * head_out[r, h, rows].astype(F32), -1, keepdims=True)
                for at, value in enumerate(three_parts(-dots)):
                    low = jnp.where(lane == MASK_AT + at, value, low)
                head_grad[h, rows] = low.astype(BF16)
            return _

        lax.fori_loop(0, 2, run, None)

    def unrotate(r, rows, value):
        return value * table_c[r, rows] - swap_halves(value) * table_s[r, rows]

    def attend_back(r, h):
        first, second = 2 * LANE * h, 2 * LANE * h + LANE
        lane = lanes((quarter, LANE))
        dq_total, bias_k, bias_v = None, 0.0, 0.0
        for b in range(4):
            rows = slice(b * quarter, (b + 1) * quarter)
            keys = heads_k[r, h, rows]
            probs = jnp.exp(dot_nt(keys, heads_q[r, h]))
            low = (probs * dot_nt(heads_v[r, h, rows], head_grad[h])).astype(BF16)
            dv = jnp.where(lane < HEAD_DIM, dot_nn(probs.astype(BF16), head_grad[h]), 0.0)
            dk = unrotate(r, rows, jnp.where(lane < HEAD_DIM, dot_nn(low, heads_q[r, h]), 0.0))
            dp_low[r, rows, first:second] = pltpu.roll(dk, HEAD_DIM, 1).astype(BF16)
            dp_low[r, rows, second : second + LANE] = dv.astype(BF16)
            bias_k += jnp.sum(dk, axis=0, keepdims=True)
            bias_v += jnp.sum(dv, axis=0, keepdims=True)
            one = dot_tn(keys, low)
            dq_total = one if dq_total is None else dq_total + one
        dq_total = jnp.transpose(dq_total)
        bias_q = 0.0
        for b in range(4):
            rows = slice(b * quarter, (b + 1) * quarter)
            dq = unrotate(r, rows, jnp.where(lane < HEAD_DIM, dq_total[rows], 0.0) * HEAD_DIM**-0.5)
            dp_low[r, rows, first:second] = (dp_low[r, rows, first:second].astype(F32) + dq).astype(BF16)
            bias_q += jnp.sum(dq, axis=0, keepdims=True)
        sums[7:8, first:second] = sums[7:8, first:second] + bias_q + pltpu.roll(bias_k, HEAD_DIM, 1)
        sums[7:8, second : second + LANE] = sums[7:8, second : second + LANE] + bias_v

    def close_back(r, link):
        sum_all(link, 0, r, lambda q: dot_nn(dp_low[r, rows_of(q)], wc[...]))

    def back_first_norm(r):
        def body(rows):
            incoming = sum_total(0, r, rows)
            normed, inv_std = normalize(first_tokens(r, rows))
            grad = gm[r, t, rows].astype(F32) + norm_back(incoming, normed, inv_std, attn_gain)
            ingrad[r, rows] = grad.astype(BF16)
            add_sum(0, incoming * normed)
            add_sum(1, incoming)

        over_chunks(quarter, body)

    def tall(ref, r, here):
        return ref[r, :, :, here].reshape(4 * quarter, here.stop - here.start)

    everything = slice(0, features)

    def feed_grad(left, right, target, here):
        total = sum(dot_tn(tall(left, r, here), tall(right, r, everything)) for r in range(2))
        target[here] = total.astype(BF16)

    def out_grad():
        for h in range(3):
            total = sum(dot_tn(head_out[r, h], tall(gm, r, everything)) for r in range(2))
            gout[h * HEAD_DIM : (h + 1) * HEAD_DIM] = total[0:HEAD_DIM].astype(BF16)

    def qkv_grad(h):
        here = slice(2 * LANE * h, 2 * LANE * (h + 1))
        total = sum(dot_tn(dp_low[r, :, here], tall(n1, r, everything)) for r in range(2))
        gqkv[h] = total[0 : 3 * HEAD_DIM].astype(BF16)

    piece, half = features // 4, features // 2
    reduces, used = {}, 0
    for i, name in enumerate(SUMS):
        at = int(name[1:] or 0)
        if name[0] in "DU":
            ref, out = ((gdown, gdown_out) if name[0] == "D" else (gup, gup_out))
            ref, out = ref.at[pl.ds(piece * at, piece)], out.at[pl.ds(piece * at, piece)]
        else:
            ref, out = (gout, gout_out) if name == "O" else (gqkv.at[at], gqkv_out.at[at])
        groups = sum_groups(dp_steps, name)
        size = Reduce.land_rows(*ref.shape, groups)
        reduces[name] = Reduce(copies, ref, land_sums.at[pl.ds(used, size)], out, out_sems.at[2 + i], groups, d, t)
        used += size

    def settle(own, back):
        def body(rows):
            mine, returned = own[1, rows].astype(F32), back[rows].astype(F32)
            middle = jnp.where(carried_wide(), returned, mine)
            own[1, rows] = jnp.where(count_wide >= 2, middle, 0.0).astype(BF16)
            own[2, rows] = jnp.where(count_wide >= 3, returned, 0.0).astype(BF16)

        over_chunks(quarter, body)

    store_mixed = pltpu.make_async_copy(mixed, mixed_out, out_sems.at[0])
    store_grad = pltpu.make_async_copy(ingrad, grad_out, out_sems.at[1])

    def count_codons(slot):
        logits = dot_nt(mixed[slot], head_ref[...])
        raised = jnp.exp(logits - jnp.max(logits, -1, keepdims=True))
        probs = raised / jnp.sum(raised, -1, keepdims=True)
        one = jnp.sum(probs, axis=0, keepdims=True)
        one = jnp.where(jnp.full(one.shape, count, jnp.int32) > slot, one, 0.0)
        codon_out[...] = one if slot == 0 else codon_out[...] + one

    def send_back(copy):
        @pl.when(d > 0)
        def _():
            copy().start()

    def get_back(copy):
        @pl.when(d > 0)
        def _():
            copy().wait_send()

        @pl.when(d < n_dp - 1)
        def _():
            copy().wait_recv()

    shared = lax.broadcasted_iota(jnp.int32, (8, features), 0) < 6
    sum_links, used = [], 0
    for clique in cliques:
        sum_links.append([(copies.make(sums, sums_land.at[used + i], other), used + i) for i, other in enumerate(clique)])
        used += len(clique)

    def small_start(k):
        for copy, _ in sum_links[k]:
            copy().start()

    def small_end(k):
        for copy, _ in sum_links[k]:
            copy().wait()
        extra = sum(sums_land[at] for _, at in sum_links[k])
        sums[...] = sums[...] + (jnp.where(shared, extra, 0.0) if k == 0 else extra)

    def begin():
        sums[...] = jnp.zeros_like(sums)
        pick_tail(tok_ref, tail_tok)
        tail_lens = lens_tile(slots - 1)
        for slot in range(slots - 2, -1, -1):
            tail_lens = jnp.where(jnp.full((8, LANE), count, jnp.int32) == slot + 1, lens_tile(slot), tail_lens)
        lens_mine[...] = tail_lens
        scan_mine[0] = jnp.full((8, LANE), count, jnp.int32)
        pl.semaphore_wait(barrier, len(greeted))
        links["tA"][0]().start()
        scan_start(0)

        @pl.when(d < n_dp - 1)
        def _():
            send_lens().start()
            send_tok().start()

        load_out.wait()
        gather_start(links["w"])
        first_norm(0)
        links["tA"][1]().start()

        @pl.when(d == 0)
        def _():
            tok_b[...] = jnp.zeros_like(tok_b)
            got_cot[...] = jnp.zeros_like(got_cot)
            lens_land[...] = jnp.zeros_like(lens_land)

        @pl.when(d == n_dp - 1)
        def _():
            back_mixed[...] = jnp.zeros_like(back_mixed)
            back_grad[...] = jnp.zeros_like(back_grad)

        pick_tail(cotan_ref, tail_cot)
        load_cotangent(0)

    def prepare():
        empty = jnp.zeros((HEAD_DIM, features), BF16)
        for h in range(3):
            wc[2 * LANE * h + 3 * HEAD_DIM : 2 * LANE * (h + 1)] = empty
            bias = [bqkv_ref[j : j + 1, h * HEAD_DIM : (h + 1) * HEAD_DIM] for j in range(3)]
            bc[:, 2 * LANE * h : 2 * LANE * (h + 1)] = jnp.concatenate(bias + [jnp.zeros_like(bias[0])], axis=1)
        for load in loads:
            load.wait()

    def second_row():
        @pl.when(d > 0)
        def _():
            send_lens().wait_recv()
            send_tok().wait_recv()

        @pl.when(d < n_dp - 1)
        def _():
            send_lens().wait_send()
            send_tok().wait_send()
            send_cot().start()

        def pick(rows):
            value = jnp.where(carried_wide(), tok_b[rows].astype(F32), tok_ref[1, rows].astype(F32))
            tok_b[rows] = value.astype(BF16)

        over_chunks(quarter, pick)
        links["tB"][0]().start()
        first_norm(1)
        links["tB"][1]().start()

    steps = {"begin": begin, "prep": prepare, "LN1B": second_row, "cB": lambda: load_cotangent(1)}
    for k in range(dp_steps):

        def scan(k=k):
            scan_end(k)
            if k + 1 < dp_steps:
                scan_start(k + 1)

        steps["scan%d" % k] = scan

    def wait_all(*copies):
        for copy in copies:
            copy().wait()

    def after_wait(wait, work, *args):
        def run():
            wait()
            work(*args)

        return run

    def nothing():
        pass

    weights_late = ["w"]
    for name, r in rows_ab.items():
        tokens, heads, second, cots, mids = (links[key + name] for key in ("t", "h", "n2", "c", "gm"))
        near, far, last, back = (links[key + name] for key in ("g", "m", "f", "gm"))

        def first_ready(link=tokens):
            wait_all(link[1])

        def rest_ready(link=tokens):
            link[0]().wait_send()
            wait_all(link[2])

        def cot_near(link=cots):
            link[0]().wait_send()

        def cot_rest(link=cots, second=second):
            wait_all(link[1], link[2], *second)

        def weight_ready():
            if weights_late:
                weights_late.clear()
                links["w"][0]().wait_send()
                wait_all(links["w"][1], links["w"][2])

        def mids_near(link=mids):
            wait_all(link[1])

        def mids_rest(link=mids):
            link[0]().wait_send()
            wait_all(link[2])

        steps["tab" + name] = after_wait(nothing, tables, r)
        steps["QK0" + name] = after_wait(first_ready, project, r, 0)
        steps["QK1" + name] = after_wait(rest_ready, project, r, 2)
        steps["att" + name] = after_wait(nothing, attend, r, heads)
        steps["hp" + name] = after_wait(nothing, pack_heads, r, heads)
        steps["LN2" + name] = after_wait(weight_ready, second_norm, r, heads, second)
        steps["fe0" + name] = after_wait(cot_near, feed_own, r)
        steps["fe1" + name] = after_wait(cot_rest, feed_other, r, near)
        steps["clF" + name] = after_wait(nothing, close_feed, r, far)
        steps["mix" + name] = after_wait(functools.partial(sum_end, far), finish_mixed, r)
        steps["cod" + name] = after_wait(nothing, count_codons, r)
        steps["bk2" + name] = after_wait(functools.partial(sum_end, near), back_second_norm, r)
        steps["op0" + name] = after_wait(mids_near, open_heads, r, 0)
        steps["op1" + name] = after_wait(mids_rest, open_heads, r, 2)
        for h in range(3):
            steps["ab%d%s" % (h, name)] = after_wait(nothing, attend_back, r, h)
        steps["clB" + name] = after_wait(nothing, close_back, r, last)
        steps["bk1" + name] = after_wait(functools.partial(sum_end, last), back_first_norm, r)

    def with_start(names, work, *args):
        def run():
            work(*args)
            for name in names:
                reduces[name].start()

        return run

    for i in (0, 2):
        here = slice(piece * i, piece * i + half)
        steps["D%d" % i] = with_start(("D%d" % i, "D%d" % (i + 1)), feed_grad, act, cot, gdown, here)
        steps["U%d" % i] = with_start(("U%d" % i, "U%d" % (i + 1)), feed_grad, n2, slope, gup, here)
    steps["O"] = with_start(("O",), out_grad)
    for h in range(3):
        steps["Q%d" % h] = with_start(("Q%d" % h,), qkv_grad, h)

    def settle_mixed():
        get_back(return_mixed)
        settle(mixed, back_mixed)
        store_mixed.start()
        count_codons(1)
        count_codons(2)

    def settle_grad():
        get_back(return_grad)
        settle(ingrad, back_grad)
        store_grad.start()

    steps["retM"] = lambda: send_back(return_mixed)
    steps["retG"] = lambda: send_back(return_grad)
    steps["setM"] = settle_mixed
    steps["setG"] = settle_grad
    for k in range(len(cliques)):

        def small(k=k):
            small_end(k)
            if k + 1 < len(cliques):
                small_start(k + 1)

        steps["sum%d" % k] = small
    steps["sums"] = lambda: small_start(0)

    starts = {"c", "gm"}
    for step in schedule(dp_steps, len(cliques)):
        kind, _, name = step.partition(":")
        if kind == "x":
            if name[:-1] in starts:
                gather_start(links[name])
            else:
                links[name][2]().start()
        elif kind == "p" and name[0] == "t":
            pass_tokens(rows_ab[name[1]], links[name])
        elif kind == "p":
            gather_pass(links[name])
        elif kind == "t":
            reduces[name.partition(".")[0]].tick()
        else:
            steps[kind]()
    while any(each.left() for each in reduces.values()):
        for each in reduces.values():
            each.tick()
    small_out[...] = sums[...]
    for j in range(3):
        pieces = [sums[7:8, (4 * h + j) * HEAD_DIM : (4 * h + j + 1) * HEAD_DIM] for h in range(3)]
        qkv_bias_out[j : j + 1] = jnp.concatenate(pieces, axis=1)
    store_mixed.wait()
    store_grad.wait()


def finish_kernel(
    quarter,
    count_ref,
    mixed_in,
    grad_in,
    gdown_in,
    gup_in,
    gout_in,
    gqkv_in,
    small_ref,
    qkv_bias_ref,
    codon_ref,
    freq_ref,
    mixed_out,
    grad_out,
    gdown_out,
    gup_out,
    gout_out,
    gqkv_out,
    qkv_bias_out,
    codon_out,
    *refs,
):
    vectors, (gdown, gup, gout, gqkv, fdown, fup, fout, fqkv, rows, load_sems, store_sems) = refs[:7], refs[7:]
    pairs = ((gdown_in, gdown), (gup_in, gup), (gqkv_in, gqkv), (mixed_in, rows.at[0]), (grad_in, rows.at[1]), (gout_in, gout))
    loads = [pltpu.make_async_copy(source, target, load_sems.at[i]) for i, (source, target) in enumerate(pairs)]
    for load in loads:
        load.start()
    stores = []

    def store(source, target, i, k):
        stores.append(pltpu.make_async_copy(source, target, store_sems.at[i, k]))
        stores[-1].start()

    for i, vector in enumerate(vectors):
        vector[...] = small_ref[i : i + 1].reshape(vector.shape[0])
    qkv_bias_out[...] = qkv_bias_ref[...]
    scale = jnp.full(codon_ref.shape, count_ref[0] * quarter, jnp.int32).astype(F32)
    freq = freq_ref[...].reshape(codon_ref.shape)
    codon_out[0] = jnp.log(codon_ref[...] / scale) - jnp.log(freq)

    def widen(i, low, wide, out, pieces):
        loads[i].wait()
        size = low.shape[0] // pieces
        for k in range(pieces):
            here = pl.ds(k * size, size)
            wide[here] = low[here].astype(F32)
            store(wide.at[here], out.at[here], i, k)

    widen(0, gdown, fdown, gdown_out, 4)
    widen(1, gup, fup, gup_out, 4)
    loads[2].wait()
    for h in range(3):
        for j in range(3):
            block = gqkv[h, j * HEAD_DIM : (j + 1) * HEAD_DIM]
            fqkv[j, h * HEAD_DIM : (h + 1) * HEAD_DIM] = block.astype(F32)
    store(fqkv, gqkv_out, 2, 0)
    for i, out in ((3, mixed_out), (4, grad_out)):
        loads[i].wait()
        store(rows.at[i - 3], out, i, 0)
    widen(5, gout, fout, gout_out, 1)
    for each in stores:
        each.wait()


def body(
    tokens,
    cotangent,
    lengths,
    row_counts,
    attn_gain,
    attn_shift,
    qkv_weight,
    qkv_bias,
    out_weight,
    out_bias,
    ffn_gain,
    ffn_shift,
    up_weight,
    up_bias,
    down_weight,
    down_bias,
    head_weight,
    codon_freq,
):
    slots, quarter, features = tokens.shape
    n_dp = lax.axis_size("dp")
    steps = n_dp.bit_length() - 1
    length = 4 * quarter
    half = HEAD_DIM // 2
    freqs = np.float32(BASE) ** (-np.arange(half, dtype=np.float32) / np.float32(half))
    freq_lane = np.tile(freqs.astype(np.float32), LANE // half)
    sign = np.concatenate([-np.ones(half), np.ones(half), np.zeros(HEAD_DIM)]).astype(np.float32)

    def turned(places):
        angles = places[:, None].astype(np.float64) * freq_lane[None].astype(np.float64)
        return np.stack([np.cos(angles) * np.abs(sign), np.sin(angles) * sign]).astype(np.float32)

    rope, bases = turned(np.arange(CHUNK)), turned(np.arange(0, length, CHUNK))
    vmem, smem = pl.BlockSpec(memory_space=pltpu.VMEM), pl.BlockSpec(memory_space=pltpu.SMEM)
    anywhere = pl.BlockSpec(memory_space=pl.ANY)
    wide = (quarter, features)

    def low(*shape):
        return pltpu.VMEM(shape, BF16)

    def full(*shape):
        return pltpu.VMEM(shape, F32)

    out_width = 3 * HEAD_DIM
    cliques = 3 + sum((1 << min(3, steps - k)) - 1 for k in range(0, steps, 3))
    sum_land = sum(Reduce.land_rows(features // 4, features, sum_groups(steps, name)) for name in SUMS)
    n_sums = sum(2 * ((1 << len(group)) - 1) for name in SUMS for group in sum_groups(steps, name))
    n_sems = 2 * (3 * 2 + 3 * 3 + 3 + 4 + 2) + 3 + 5 + steps + n_sums + cliques
    scratch = [
        low(2, 4, *wide),
        low(2, 4, *wide),
        low(2, 4, *wide),
        low(2, 4, *wide),
        low(2, 3, length, LANE),
        low(2, 3, length, LANE),
        low(2, 3, length, LANE),
        low(2, 3, length, LANE),
        low(3, length, LANE),
        low(2, length, 6 * LANE),
        low(2, 4, *wide),
        low(2, 4, *wide),
        low(2, 2, 4, *wide),
        low(2, 2, 2, *wide),
        low(2, 2, *wide),
        full(2, *wide),
        full(2, length, LANE),
        full(2, length, LANE),
        low(6 * LANE, features),
        full(1, 6 * LANE),
        low(2, 2 * out_width, features),
        low(*wide),
        low(2, *wide),
        low(*wide),
        pltpu.VMEM((steps + 1, 8, LANE), jnp.int32),
        pltpu.VMEM((steps, 8, LANE), jnp.int32),
        pltpu.VMEM((8, LANE), jnp.int32),
        pltpu.VMEM((8, LANE), jnp.int32),
        low(features, features),
        low(features, features),
        low(out_width, features),
        low(3, out_width, features),
        low(sum_land, features),
        low(*wide),
        low(*wide),
        full(8, features),
        full(cliques, 8, features),
        full(8, features),
        pltpu.SemaphoreType.DMA((n_sems,)),
        pltpu.SemaphoreType.DMA((n_sems,)),
        pltpu.SemaphoreType.DMA((2 + len(SUMS),)),
        pltpu.SemaphoreType.DMA((12,)),
    ]
    outs = pl.pallas_call(
        functools.partial(layer_kernel, n_dp, slots, quarter, features),
        out_shape=(
            jax.ShapeDtypeStruct(tokens.shape, BF16),
            jax.ShapeDtypeStruct(tokens.shape, BF16),
            jax.ShapeDtypeStruct((features, features), BF16),
            jax.ShapeDtypeStruct((features, features), BF16),
            jax.ShapeDtypeStruct((out_width, features), BF16),
            jax.ShapeDtypeStruct((3, out_width, features), BF16),
            jax.ShapeDtypeStruct((8, features), F32),
            jax.ShapeDtypeStruct((3, out_width), F32),
            jax.ShapeDtypeStruct((1, head_weight.shape[1]), F32),
        ),
        in_specs=[smem, smem, vmem, vmem, anywhere, vmem, anywhere] + [vmem] * 14,
        out_specs=(anywhere,) * 6 + (vmem,) * 3,
        scratch_shapes=scratch,
        compiler_params=pltpu.CompilerParams(
            collective_id=0, has_side_effects=True, vmem_limit_bytes=64 * 1024 * 1024
        ),
    )(
        row_counts,
        lengths,
        tokens,
        cotangent,
        jnp.swapaxes(qkv_weight, 1, 2),
        qkv_bias,
        out_weight,
        up_weight,
        down_weight,
        attn_gain,
        attn_shift,
        out_bias,
        ffn_gain,
        ffn_shift,
        down_bias,
        up_bias,
        head_weight.T,
        jnp.asarray(freq_lane[None]),
        jnp.asarray(rope),
        jnp.asarray(bases),
        jnp.asarray(sign[None]),
    )
    mixed, input_grad, gdown, gup, gout, gqkv, small, qkv_bias_grad, codon = outs
    wide_out = (3, out_width, features)
    vector = jax.ShapeDtypeStruct((features,), F32)
    finished = pl.pallas_call(
        functools.partial(finish_kernel, quarter),
        out_shape=(
            jax.ShapeDtypeStruct(tokens.shape, BF16),
            jax.ShapeDtypeStruct(tokens.shape, BF16),
            jax.ShapeDtypeStruct(gdown.shape, F32),
            jax.ShapeDtypeStruct(gup.shape, F32),
            jax.ShapeDtypeStruct(gout.shape, F32),
            jax.ShapeDtypeStruct(wide_out, F32),
            jax.ShapeDtypeStruct((3, out_width), F32),
            jax.ShapeDtypeStruct((1, 1, codon_freq.shape[0]), F32),
        )
        + (vector,) * 7,
        in_specs=[smem] + [anywhere] * 6 + [vmem] * 4,
        out_specs=(anywhere,) * 6 + (vmem,) * 9,
        scratch_shapes=[
            low(*gdown.shape),
            low(*gup.shape),
            low(*gout.shape),
            low(*wide_out),
            full(*gdown.shape),
            full(*gup.shape),
            full(*gout.shape),
            full(*wide_out),
            low(2, *tokens.shape),
            pltpu.SemaphoreType.DMA((6,)),
            pltpu.SemaphoreType.DMA((6, 4)),
        ],
        compiler_params=pltpu.CompilerParams(vmem_limit_bytes=60 * 1024 * 1024),
    )(row_counts, mixed, input_grad, gdown, gup, gout, gqkv, small, qkv_bias_grad, codon, codon_freq)
    mixed, input_grad, gdown, gup, gout, gqkv, qkv_bias_grad, codon_gap = finished[:8]
    vectors = finished[8:]
    return (
        mixed,
        input_grad,
        vectors[0],
        vectors[1],
        jnp.swapaxes(gqkv, 1, 2),
        qkv_bias_grad,
        gout,
        vectors[2],
        vectors[3],
        vectors[4],
        gup,
        vectors[6],
        gdown,
        vectors[5],
        codon_gap,
    )


def solution(mesh):
    placed = (
        P("dp", "tensor", None),
        P("dp", "tensor", None),
        P("dp", None),
        P("dp"),
        P(),
        P(),
        P(None, None, "tensor"),
        P(None, "tensor"),
        P("tensor", None),
        P(),
        P(),
        P(),
        P(None, "tensor"),
        P("tensor"),
        P("tensor", None),
        P(),
        P(),
        P(),
    )
    return jax.shard_map(
        body,
        mesh=mesh,
        in_specs=placed,
        out_specs=(
            P("dp", "tensor", None),
            P("dp", "tensor", None),
            P(),
            P(),
            P(None, None, "tensor"),
            P(None, "tensor"),
            P("tensor", None),
            P(),
            P(),
            P(),
            P(None, "tensor"),
            P("tensor"),
            P("tensor", None),
            P(),
            P("dp", "tensor", None),
        ),
        check_vma=False,
    )
```

```python
import functools

import jax
import jax.numpy as jnp
import numpy as np
from jax import lax
from jax.experimental import pallas as pl
from jax.experimental.pallas import tpu as pltpu
from jax.sharding import PartitionSpec as P

HEAD_DIM = 64
EPS = 1e-05
BASE = 10000.0
F32 = jnp.float32
BF16 = jnp.bfloat16
MESH = pl.DeviceIdType.MESH
LANE = 128
CHUNK = 64
FAR = -1e30
MASK_AT = 64
TOTAL_AT = 68
TREE = "tree"
SUMS = {
    "D0": ((1,), (0,), (2,)),
    "D1": ((0,), (1,), (2,)),
    "D2": ((0,), (1,), (2,)),
    "D3": ((1,), (0,), (2,)),
    "U0": ((0,), 'tree'),
    "U1": ((0,), 'tree'),
    "U2": ((1,), (0,), (2,)),
    "U3": ((0,), 'tree'),
    "O": ((0,), 'tree'),
    "Q0": ((0,), (1,), (2,)),
    "Q1": ((0,), (1,), (2,)),
    "Q2": ((0,), 'tree'),
}


def dot_nn(a, b):
    return lax.dot_general(a, b, (((1,), (0,)), ((), ())), preferred_element_type=F32)


def dot_nt(a, b):
    return lax.dot_general(a, b, (((1,), (1,)), ((), ())), preferred_element_type=F32)


def dot_tn(a, b):
    return lax.dot_general(a, b, (((0,), (0,)), ((), ())), preferred_element_type=F32)


def lanes(shape):
    return lax.broadcasted_iota(jnp.int32, shape, 1)


def three_parts(value):
    high = value.astype(BF16).astype(F32)
    rest = value - high
    middle = rest.astype(BF16).astype(F32)
    return high, middle, rest - middle


def normalize(value):
    average = jnp.mean(value, -1, keepdims=True)
    centred = value - average
    inv_std = lax.rsqrt(jnp.mean(centred * centred, -1, keepdims=True) + EPS)
    return centred * inv_std, inv_std


def norm_back(incoming, normed, inv_std, gain):
    scaled = incoming * gain
    return inv_std * (
        scaled
        - jnp.mean(scaled, -1, keepdims=True)
        - normed * jnp.mean(scaled * normed, -1, keepdims=True)
    )


def swap_halves(value):
    lane = lanes(value.shape)
    return jnp.where(lane < 32, pltpu.roll(value, 96, 1), pltpu.roll(value, 32, 1))


class Copies:
    def __init__(self, send, recv):
        self.send, self.recv, self.count = send, recv, 0

    def make(self, src, dst, device):
        at = self.count
        self.count += 1
        return functools.partial(
            pltpu.make_async_remote_copy,
            src_ref=src,
            dst_ref=dst,
            send_sem=self.send.at[at],
            recv_sem=self.recv.at[at],
            device_id=device,
            device_id_type=MESH,
        )


class Region:
    def __init__(self, row, rows, lane, width):
        self.row, self.rows, self.lane, self.width = row, rows, lane, width

    def halves(self, side):
        if self.rows % 32 == 0:
            half = self.rows // 2
            cut = [Region(self.row + half * k, half, self.lane, self.width) for k in (side, 1 - side)]
        elif self.width % (2 * LANE) == 0:
            half = self.width // 2
            cut = [Region(self.row, self.rows, self.lane + half * k, half) for k in (side, 1 - side)]
        else:
            cut = None
        return cut

    def of(self, ref, start=0, rows=None):
        row, lane = self.row + start, self.lane
        if not isinstance(row, int):
            row = pl.multiple_of(row, 16)
        if not isinstance(lane, int):
            lane = pl.multiple_of(lane, LANE)
        return ref.at[pl.ds(row, rows or self.rows), pl.ds(lane, self.width)]


class Places:
    def __init__(self, width):
        self.width, self.used, self.spare = width, 0, []

    def take(self, region):
        at = (self.used, 0)
        if 2 * region.width == self.width:
            if (region.rows, region.width) in [size for size, _ in self.spare]:
                i = [size for size, _ in self.spare].index((region.rows, region.width))
                return self.spare.pop(i)[1]
            self.spare.append(((region.rows, region.width), Region(self.used, region.rows, region.width, region.width)))
        self.used += region.rows
        return Region(at[0], region.rows, at[1], region.width)


def under(condition, work):
    if condition is None:
        work()
    else:
        pl.when(condition)(work)


class Step:
    def __init__(self, copies, region, landed=(), sender=None, receiver=None):
        self.copies, self.region, self.landed = copies, region, landed
        self.sender, self.receiver = sender, receiver


class Reduce:
    def __init__(self, copies, ref, land, out, store_sem, groups, d, t):
        self.ref, self.land = ref, land
        self.plan, self.holder = [], None
        rows, width = ref.shape
        region, place, backs = Region(0, rows, 0, width), Places(width), []
        for group in groups:
            if group == TREE:
                inner = ((d >> 1) & 1) != ((d >> 2) & 1)
                there = place.take(region)
                copy = copies.make(region.of(ref), there.of(land), (d ^ 2, t))
                self.plan.append(Step([copy], region, [there], jnp.logical_not(inner), inner))
                backs.append((region, [(d ^ 2, t)], inner, jnp.logical_not(inner)))
                self.holder, group, masks = inner, (2,), [6]
            else:
                masks = None
            sends, mine = [], self.part(region, group, [(d >> bit) & 1 for bit in group])
            for mask in range(1, 1 << len(group)):
                turned = [(mask >> i) & 1 for i in range(len(group))]
                flips = masks[0] if masks else sum(turn << bit for turn, bit in zip(turned, group))
                partner = (d ^ flips, t)
                give = self.part(region, group, [((d >> bit) & 1) ^ turn for turn, bit in zip(turned, group)])
                there = place.take(mine)
                sends.append((copies.make(give.of(ref), there.of(land), partner), there, partner))
            landed = [there for _, there, _ in sends]
            self.plan.append(Step([copy for copy, _, _ in sends], mine, landed, self.holder, self.holder))
            if mine.rows * mine.width < region.rows * region.width:
                backs.append((mine, [partner for _, _, partner in sends], self.holder, self.holder))
            region = mine
        self.adds = len(self.plan)
        self.store = functools.partial(pltpu.make_async_copy, region.of(ref), region.of(out), store_sem)
        for i, (region, partners, sender, receiver) in enumerate(reversed(backs)):
            own = region.of(ref if i == 0 else out)
            sends = [copies.make(own, region.of(out), partner) for partner in partners]
            self.plan.append(Step(sends, region, (), sender, receiver))
        self.place = 0

    @staticmethod
    def part(region, group, sides):
        for side in sides:
            region = (region.halves(side) or (region,))[0]
        return region

    @staticmethod
    def land_rows(rows, width, groups):
        region, place = Region(0, rows, 0, width), Places(width)
        for group in groups:
            if group == TREE:
                place.take(region)
                group = (2,)
            region = Reduce.part(region, group, [0] * len(group))
            for _ in range(1, 1 << len(group)):
                place.take(region)
        return place.used

    @staticmethod
    def copies_of(groups):
        return sum(4 if group == TREE else 2 * ((1 << len(group)) - 1) for group in groups)

    def start(self):
        for copy in self.plan[0].copies:
            copy().start()

    def left(self):
        return len(self.plan) - self.place

    def tick(self):
        if self.place >= len(self.plan):
            return
        now, rows = self.plan[self.place], self.plan[self.place].region.rows
        size = max(size for size in (16, 32, 48, 64, 96) if rows % size == 0)

        def add(i, _):
            here = now.region.of(self.ref, i * size, size)
            total = here[...].astype(F32)
            for there in now.landed:
                total += there.of(self.land, i * size, size)[...].astype(F32)
            here[...] = total.astype(BF16)
            return _

        def receive():
            for copy in now.copies:
                copy().wait_recv()
            if now.landed:
                lax.fori_loop(0, rows // size, add, None)

        def sent():
            for copy in now.copies:
                copy().wait_send()

        under(now.sender, sent)
        under(now.receiver, receive)
        if self.place == self.adds - 1:
            under(self.holder, lambda: self.store().start())
        if self.place == self.adds or (self.place + 1 == len(self.plan) and self.place < self.adds):
            under(self.holder, lambda: self.store().wait())
        self.place += 1
        if self.place < len(self.plan):
            later = self.plan[self.place]

            def begin():
                for copy in later.copies:
                    copy().start()

            under(later.sender, begin)


def sum_groups(steps, name):
    groups = SUMS[name]
    if TREE in groups and steps < 3:
        groups = ((0,), (1,))
    first = [group if group == TREE else tuple(bit for bit in group if bit < steps) for group in groups]
    return [group for group in first if group] + [(bit,) for bit in range(3, steps)]


def schedule(dp_steps, cliques):
    names = (
        "begin", "tabA", "scan0", "prep", "QK0A", "x:cA", "scan1", "p:tA", "w0", "scan2", "LN1B", "QK1A", "attA",
        "tabB", "hpA", "p:cA", "w1", "cB", "QK0B", "p:tB", "x:cB", "w2", "QK1B", "attB", "w3", "hpB", "LN2A", "fe0A",
        "fe1A", "dD0", "p:cB", "LN2B", "fe0B", "fe1B", "D0", "dD2", "D2", "dU2", "bk2A", "x:gmA", "dU0", "U0", "t:D1",
        "U2", "clFB", "t:D3", "t:D2", "bk2B", "t:D1", "t:U0", "x:mB", "t:D0", "clFA", "t:U2", "t:D2", "t:U1", "op0A",
        "t:D1", "x:gmB", "p:gmA", "x:mA", "t:U3", "t:U0", "t:D3", "op1A", "ab0A", "t:D2", "t:U1", "dQ0", "t:D1",
        "t:U2", "dO", "t:U0", "mixB", "retM", "ab1A", "ab2A", "t:D1", "t:U1", "t:U2", "t:U3", "p:gmB", "op0B", "t:D0",
        "t:D2", "t:D3", "op1B", "O", "ab0B", "t:U2", "Q0", "t:U0", "ab1B", "t:D2", "t:O", "dQ1", "t:U1", "t:U2",
        "t:U3", "Q1", "dQ2", "ab2B", "Q2", "t:Q0", "t:O", "clBB", "t:D0", "t:U1", "t:D3", "t:Q1", "t:U0", "t:D1",
        "t:Q0", "t:U3", "t:O", "t:D2", "t:Q2", "clBA", "t:Q1", "t:D0", "t:Q0", "t:O", "mixA", "t:Q2", "t:U3", "t:Q1",
        "bk1B", "t:Q0", "retG", "t:Q2", "t:Q0", "t:U1", "t:Q1", "t:U3", "bk1A", "sums", "t:O", "codA", "t:Q2", "t:D0",
        "t:U2", "t:Q1", "setG", "t:D3", "sum0", "t:Q2", "t:Q1", "setM", "sum1", "t:Q0", "t:D0", "t:U0", "t:O", "t:D3",
        "t:Q2",
    )
    for name in names:
        if name in ("scan2", "sum1"):
            count = dp_steps if name == "scan2" else cliques
            yield from (name[:-1] + str(k) for k in range(int(name[-1]), count))
        else:
            yield name


def layer_kernel(
    n_dp,
    slots,
    quarter,
    features,
    count_ref,
    lens_ref,
    tok_ref,
    cotan_any,
    wqkv_ref,
    bqkv_ref,
    wout_ref,
    wup_any,
    wdown_any,
    attn_gain_ref,
    attn_shift_ref,
    out_bias_ref,
    ffn_gain_ref,
    ffn_shift_ref,
    down_bias_ref,
    up_bias_ref,
    head_ref,
    freq_ref,
    rope_ref,
    base_ref,
    line_ref,
    mixed_out,
    grad_out,
    gdown_out,
    gup_out,
    gout_out,
    gqkv_out,
    small_out,
    qkv_bias_out,
    codon_out,
    n1,
    n2,
    cot,
    gm,
    heads_q,
    heads_k,
    heads_v,
    head_out,
    head_grad,
    dp_low,
    act,
    slope,
    part,
    land_core,
    land_x,
    mid,
    table_c,
    table_s,
    wc,
    bc,
    wcat,
    tok_b,
    scan_mine,
    scan_land,
    lens_mine,
    lens_land,
    gdown,
    gup,
    gout,
    gqkv,
    land_sums,
    back_mixed,
    back_grad,
    sums,
    sums_land,
    vec,
    cotan_ref,
    wup_ref,
    wdown_ref,
    send_sems,
    recv_sems,
    out_sems,
    load_sems,
):
    d, t = lax.axis_index("dp"), lax.axis_index("tensor")
    core, across = (d, t ^ 1), (d, t ^ 2)
    own_rows = slots - 1
    dp_steps = n_dp.bit_length() - 1
    copies = Copies(send_sems, recv_sems)
    rows_ab = {"A": 0, "B": 1}

    vectors = (attn_gain_ref, attn_shift_ref, out_bias_ref, ffn_gain_ref, ffn_shift_ref, down_bias_ref, up_bias_ref)
    for i, ref in enumerate(vectors):
        vec[i : i + 1] = ref[...].reshape(1, features)
    attn_gain, attn_shift = vec[0:1], vec[1:2]
    out_bias, ffn_gain, ffn_shift, down_bias, up_bias = (vec[i : i + 1] for i in range(2, 7))

    cliques = [[(d, t ^ m) for m in range(1, 4)]]
    for low_bit in range(0, dp_steps, 3):
        width = min(3, dp_steps - low_bit)
        cliques.append([(d ^ (m << low_bit), t) for m in range(1, 1 << width)])
    greeted = [other for clique in cliques for other in clique]
    for k in range(dp_steps):
        greeted.append(((d + (1 << k)) % n_dp, t))
        greeted.append(((d + n_dp - (1 << k)) % n_dp, t))
    barrier = pltpu.get_barrier_semaphore()
    for other in greeted:
        pl.semaphore_signal(barrier, inc=1, device_id=other, device_id_type=MESH)

    loads = []
    for h in range(3):
        for j in range(3):
            source = wqkv_ref.at[j, pl.ds(h * HEAD_DIM, HEAD_DIM)]
            target = wc.at[pl.ds(2 * LANE * h + HEAD_DIM * j, HEAD_DIM)]
            loads.append(pltpu.make_async_copy(source, target, load_sems.at[len(loads)]))
    out_width = 3 * HEAD_DIM
    half_lanes = features // 2
    load_out = pltpu.make_async_copy(wout_ref, wcat.at[0, pl.ds(0, out_width)], load_sems.at[len(loads)])
    load_cot = pltpu.make_async_copy(cotan_any, cotan_ref, load_sems.at[len(loads) + 1])
    load_out.start()
    load_cot.start()
    loads.append(pltpu.make_async_copy(wup_any, wup_ref, load_sems.at[len(loads) + 2]))
    loads.append(pltpu.make_async_copy(wdown_any, wdown_ref, load_sems.at[len(loads) + 2]))
    for load in loads:
        load.start()

    def over_chunks(rows, body, step=CHUNK):
        def run(i, _):
            body(pl.ds(pl.multiple_of(i * step, step), step))
            return _

        lax.fori_loop(0, rows // step, run, None)

    mixed, ingrad = n2.at[0, pl.ds(0, slots)], n2.at[1, pl.ds(0, slots)]

    heads_x = land_x.at[1]
    tok_x, got_cot = gm.at[:, 1], gm.at[1, 0]

    tail_tok, tail_cot = mixed.at[slots - 1], ingrad.at[slots - 1]
    count = count_ref[0]
    count_wide = jnp.full((CHUNK, features), count, jnp.int32)

    def pick_tail(source, target):
        def body(rows):
            value = source[slots - 1, rows].astype(F32)
            for slot in range(slots - 2, -1, -1):
                value = jnp.where(count_wide == slot + 1, source[slot, rows].astype(F32), value)
            target[rows] = value.astype(BF16)

        over_chunks(quarter, body)

    after, before = (d + 1, t), (d - 1, t)
    send_tok = copies.make(tail_tok, tok_b, after)
    send_cot = copies.make(tail_cot, got_cot, after)
    send_lens = copies.make(lens_mine, lens_land, after)
    return_mixed = copies.make(mixed.at[1], back_mixed, before)
    return_grad = copies.make(ingrad.at[1], back_grad, before)

    def lens_tile(slot):
        row_at = lax.broadcasted_iota(jnp.int32, (8, LANE), 0)
        tile = jnp.zeros((8, LANE), jnp.int32)
        for gene in range(4):
            tile = jnp.where(row_at == gene, lens_ref[slot, gene], tile)
        return tile

    scan_copies = [copies.make(scan_mine.at[k], scan_land.at[k], (d + (1 << k), t)) for k in range(dp_steps)]

    def scan_start(k):
        @pl.when(d + (1 << k) < n_dp)
        def _():
            scan_copies[k]().start()

    def scan_end(k):
        scan_mine[k + 1] = scan_mine[k]

        @pl.when(d + (1 << k) < n_dp)
        def _():
            scan_copies[k]().wait_send()

        @pl.when(d >= (1 << k))
        def _():
            scan_copies[k]().wait_recv()
            scan_mine[k + 1] = scan_mine[k] + scan_land[k]

    def carried_tile():
        return (scan_mine[dp_steps] - count - d * own_rows) > 0

    def carried_wide():
        return jnp.broadcast_to(carried_tile()[0:1, 0:1], (CHUNK, features))

    def gather(full, r):
        mine = full.at[r, t]
        return (
            copies.make(mine, mine, across),
            copies.make(mine, mine, core),
            copies.make(full.at[r, t ^ 2], full.at[r, t ^ 2], core),
        )

    def gather_start(link):
        link[0]().start()
        link[1]().start()

    def gather_pass(link):
        link[0]().wait_recv()
        link[2]().start()

    def gather_end(link):
        link[0]().wait_send()
        link[1]().wait()
        link[2]().wait()

    def summing(kind, r):
        return (
            copies.make(part.at[kind, r, t ^ 1], land_core.at[kind, r, 0], core),
            copies.make(part.at[kind, r, t ^ 3], land_core.at[kind, r, 1], core),
            copies.make(part.at[kind, r, t ^ 2], land_x.at[kind, r], across),
        )

    def quarter_of(i):
        return t ^ jnp.where(i == 0, 3, jnp.where(i == 3, 0, i))

    def sum_step(link, kind, r, i, q, value):
        @pl.when(i < 2)
        def _():
            part[kind, r, q] = value.astype(BF16)

        @pl.when(i == 0)
        def _():
            link[1]().start()

        @pl.when(i == 1)
        def _():
            link[0]().start()

        @pl.when(i == 2)
        def _():
            link[1]().wait_recv()
            part[kind, r, q] = (value + land_core[kind, r, 1].astype(F32)).astype(BF16)
            if kind == 0:
                link[2]().start()

        @pl.when(i == 3)
        def _():
            part[kind, r, q] = value.astype(BF16)

    def sum_all(link, kind, r, make_part):
        def run(i, _):
            q = quarter_of(i)
            sum_step(link, kind, r, i, q, make_part(q))
            return _

        lax.fori_loop(0, 4, run, None)

    def sum_end(link):
        link[0]().wait()
        link[1]().wait_send()
        link[2]().wait()

    def sum_total(kind, r, rows):
        near = part[kind, r, t, rows].astype(F32) + land_core[kind, r, 0, rows].astype(F32)
        return near + land_x[kind, r, rows].astype(F32)

    links = {}
    for name, r in rows_ab.items():
        for key, full in (("c", cot), ("gm", gm)):
            links[key + name] = gather(full, r)
        for key, kind in (("g", 0), ("f", 0), ("m", 1)):
            links[key + name] = summing(kind, r)
        source = tok_ref.at[0] if r == 0 else tok_b
        links["t" + name] = (
            copies.make(source, tok_x.at[r], across),
            copies.make(n1.at[r, t], n1.at[r, t], core),
            copies.make(n1.at[r, t ^ 2], n1.at[r, t ^ 2], core),
        )
        links["h" + name] = tuple(
            copies.make(part.at[0, r, t ^ m, :, pl.ds(0, half_lanes)], land_core.at[0, r, s, :, pl.ds(0, half_lanes)], core)
            for s, m in ((0, 1), (1, 3))
        ) + tuple(
            copies.make(
                part.at[0, r, t ^ m, :, pl.ds(half_lanes, half_lanes)],
                heads_x.at[r, :, pl.ds(half_lanes * s, half_lanes)],
                across,
            )
            for s, m in ((1, 0), (0, 2))
        )
        links["n2" + name] = tuple(copies.make(n2.at[r, t ^ m], n2.at[r, t ^ m], core) for m in (0, 2))
    own_out, got_out = wcat.at[0, pl.ds(0, out_width)], wcat.at[1, pl.ds(0, out_width)]
    piece_of, pieces = Region(0, out_width, 0, features), []
    for bit in range(min(3, dp_steps)):
        piece_of = piece_of.halves((d >> bit) & 1)[0]
        pieces.insert(0, ((d ^ (1 << bit), t), piece_of))
    weight_links = [copies.make(piece_of.of(own_out), piece_of.of(got_out), across)]
    weight_links += [copies.make(region.of(got_out), region.of(got_out), partner) for partner, region in pieces]
    weight_links.append(copies.make(got_out, wcat.at[1, pl.ds(out_width, out_width)], core))
    share_weight = copies.make(own_out, wcat.at[0, pl.ds(out_width, out_width)], core)

    def rows_of(q):
        return pl.ds(pl.multiple_of(q * quarter, quarter), quarter)

    def add_sum(row, value):
        sums[row : row + 1] = sums[row : row + 1] + jnp.sum(value, axis=0, keepdims=True)

    def first_tokens(r, rows):
        return (tok_ref[0, rows] if r == 0 else tok_b[rows]).astype(F32)

    def first_norm(r, theirs=False):
        def body(rows):
            normed, _ = normalize(tok_x[r, rows].astype(F32) if theirs else first_tokens(r, rows))
            n1[r, t ^ 2 if theirs else t, rows] = (normed * attn_gain + attn_shift).astype(BF16)

        over_chunks(quarter, body)

    def pass_tokens(r, link):
        link[0]().wait_recv()
        first_norm(r, theirs=True)
        link[2]().start()

    def load_cotangent(r):
        if r == 1:

            @pl.when(d > 0)
            def _():
                send_cot().wait_recv()

            @pl.when(d < n_dp - 1)
            def _():
                send_cot().wait_send()

        def body(rows):
            value = cotan_ref[0, rows].astype(F32)
            if r == 1:
                value = jnp.where(carried_wide(), got_cot[rows].astype(F32), cotan_ref[1, rows].astype(F32))
            cot[r, t, rows] = value.astype(BF16)
            add_sum(5, value)

        over_chunks(quarter, body)

    def ends_of(r):
        tile = lens_tile(0) if r == 0 else jnp.where(carried_tile(), lens_land[...], lens_tile(1))
        first = tile[0:1]
        second = first + tile[1:2]
        return first, second, second + tile[2:3]

    def segment_of(ends, base, rows):
        place = lax.broadcasted_iota(jnp.int32, (rows, LANE), 0) + base
        return [place >= end for end in ends]

    def tables(r):
        ends = ends_of(r)
        turns = [end.astype(F32) * freq_ref[...] for end in ends]
        cosines = [jnp.cos(turn) for turn in turns]
        sines = [jnp.sin(turn) * line_ref[...] for turn in turns]

        def body(rows):
            passed = segment_of(ends, rows.start, CHUNK)
            at = pl.ds(rows.start // CHUNK, 1)
            cos_base, sin_base = base_ref[0, at], base_ref[1, at]
            cos_start = jnp.broadcast_to(cos_base, (CHUNK, LANE))
            sin_start = jnp.broadcast_to(sin_base, (CHUNK, LANE))
            for ge, cosine, sine in zip(passed, cosines, sines):
                cos_start = jnp.where(ge, cos_base * cosine + sin_base * sine, cos_start)
                sin_start = jnp.where(ge, sin_base * cosine - cos_base * sine, sin_start)
            cos_place, sin_place = rope_ref[0], rope_ref[1]
            table_c[r, rows] = cos_place * cos_start - sin_place * sin_start
            table_s[r, rows] = sin_place * cos_start + cos_place * sin_start

        over_chunks(4 * quarter, body)

    def project(r, first):
        ends = ends_of(r)

        def run(i, _):
            q = t ^ (i + first)
            rows = rows_of(q)
            both = dot_nt(n1[r, q], wc[...]) + bc[...]
            lane = lanes((quarter, LANE))
            ge = segment_of(ends, q * quarter, quarter)
            gene = sum(g.astype(jnp.int32) for g in ge)
            in_mask = (lane >= MASK_AT) & (lane < TOTAL_AT)
            same = in_mask & (lane - MASK_AT == gene)
            extra_q = jnp.where(in_mask & ~same, FAR, 0.0)
            extra_k = jnp.where(same | ((lane >= TOTAL_AT) & (lane < TOTAL_AT + 3)), 1.0, 0.0)
            extra_v = jnp.where((lane >= MASK_AT) & (lane < MASK_AT + 3), 1.0, 0.0)
            cosine, sine = table_c[r, rows], table_s[r, rows]
            for h in range(3):
                query = both[:, 2 * LANE * h : 2 * LANE * h + LANE]
                key = pltpu.roll(query, HEAD_DIM, 1)
                value = both[:, 2 * LANE * h + LANE : 2 * LANE * (h + 1)]
                query = (query * cosine + swap_halves(query) * sine) * HEAD_DIM**-0.5 + extra_q
                key = key * cosine + swap_halves(key) * sine + extra_k
                heads_q[r, h, rows] = query.astype(BF16)
                heads_k[r, h, rows] = key.astype(BF16)
                heads_v[r, h, rows] = (value + extra_v).astype(BF16)
            return _

        lax.fori_loop(0, 2, run, None)

    def attend(r, link):
        def run(q, _):
            rows = rows_of(q)
            lane = lanes((quarter, LANE))
            queries = [heads_q[r, h, rows] for h in range(3)]
            scores = [dot_nt(queries[h], heads_k[r, h]) for h in range(3)]
            for h in range(3):
                top = jnp.max(scores[h], -1, keepdims=True)
                probs = jnp.exp(scores[h] - top).astype(BF16)
                mixed_values = dot_nn(probs, heads_v[r, h])
                total = mixed_values[:, MASK_AT : MASK_AT + 1]
                out = jnp.where(lane < HEAD_DIM, mixed_values * (1.0 / total), 0.0).astype(BF16)
                head_out[r, h, rows] = out
                part[0, r, q, :, h * LANE : (h + 1) * LANE] = out
                query = queries[h].astype(F32)
                for at, value in enumerate(three_parts(-(top + jnp.log(total)))):
                    query = jnp.where(lane == TOTAL_AT + at, value, query)
                heads_q[r, h, rows] = query.astype(BF16)
            return _

        lax.fori_loop(0, 4, run, None)
        link[1]().start()
        link[0]().start()

    def pack_heads(r, link):
        for s, m in ((1, 2), (0, 0)):
            link[s]().wait_recv()
            q = t ^ m
            blocks = [part[0, r, q, :, h * LANE : (h + 1) * LANE].astype(F32) for h in range(3)]
            blocks += [land_core[0, r, s, :, h * LANE : (h + 1) * LANE].astype(F32) for h in range(3)]
            for j in range(3):
                pair = blocks[2 * j] + pltpu.roll(blocks[2 * j + 1], HEAD_DIM, 1)
                part[0, r, q, :, half_lanes + j * LANE : half_lanes + (j + 1) * LANE] = pair.astype(BF16)
            link[3 if m else 2]().start()

    def second_norm(r, heads, out):
        for s, m in ((1, 2), (0, 0)):
            q = t ^ m
            near = dot_nn(part[0, r, q, :, half_lanes:], wcat[0])
            heads[2 if s else 3]().wait_recv()
            attention = near + dot_nn(heads_x[r, :, half_lanes * s : half_lanes * (s + 1)], wcat[1])
            for k in range(quarter // CHUNK):
                rows = slice(k * CHUNK, (k + 1) * CHUNK)
                tokens = tok_x[r, rows].astype(F32) if s else first_tokens(r, rows)
                middle = tokens + attention[rows] + out_bias
                if s == 0:
                    mid[r, rows] = middle
                normed, _ = normalize(middle)
                n2[r, q, rows] = (normed * ffn_gain + ffn_shift).astype(BF16)
            out[1 if m else 0]().start()
        for copy in heads:
            copy().wait_send()

    def feed(r, q):
        hidden = dot_nn(n2[r, q], wup_ref[...]) + up_bias
        below = 0.5 * (1.0 + lax.erf(hidden * 0.5**0.5))
        density = jnp.exp(hidden * hidden * -0.5) * (2.0 * np.pi) ** -0.5
        act[r, q] = (hidden * below).astype(BF16)
        grad = dot_nt(cot[r, q], wdown_ref[...]) * (below + hidden * density)
        add_sum(6, grad)
        low = grad.astype(BF16)
        slope[r, q] = low
        part[0, r, q] = dot_nt(low, wup_ref[...]).astype(BF16)

    def feed_own(r):
        def run(i, _):
            feed(r, t ^ (2 - 2 * i))
            return _

        lax.fori_loop(0, 2, run, None)

    def feed_other(r, link):
        def run(i, _):
            feed(r, t ^ (3 - 2 * i))

            @pl.when(i == 0)
            def _():
                link[1]().start()

            @pl.when(i == 1)
            def _():
                link[0]().start()

            return _

        lax.fori_loop(0, 2, run, None)
        link[1]().wait_recv()

        def add(rows):
            total = part[0, r, t ^ 2, rows].astype(F32) + land_core[0, r, 1, rows].astype(F32)
            part[0, r, t ^ 2, rows] = total.astype(BF16)

        over_chunks(quarter, add)
        link[2]().start()

    def close_feed(r, link):
        sum_all(link, 1, r, lambda q: dot_nn(act[r, q], wdown_ref[...]))

    def finish_mixed(r):
        def body(rows):
            mixed[r, rows] = (mid[r, rows] + sum_total(1, r, rows) + down_bias).astype(BF16)

        over_chunks(quarter, body)

    def back_second_norm(r):
        def body(rows):
            incoming = sum_total(0, r, rows)
            normed, inv_std = normalize(mid[r, rows])
            grad = cot[r, t, rows].astype(F32) + norm_back(incoming, normed, inv_std, ffn_gain)
            gm[r, t, rows] = grad.astype(BF16)
            add_sum(3, incoming * normed)
            add_sum(4, incoming)
            add_sum(2, grad)

        over_chunks(quarter, body)

    def open_heads(r, first):
        def run(i, _):
            q = t ^ (i + first)
            rows = rows_of(q)
            grads = dot_nt(gm[r, q], wcat[0, 0 : 2 * LANE])
            lane = lanes((quarter, LANE))
            pair, last = grads[:, 0:LANE], grads[:, LANE : 2 * LANE]
            for h, low in enumerate((pair, pltpu.roll(pair, HEAD_DIM, 1), last)):
                low = jnp.where(lane < HEAD_DIM, low, 0.0).astype(BF16).astype(F32)
                dots = jnp.sum(low * head_out[r, h, rows].astype(F32), -1, keepdims=True)
                for at, value in enumerate(three_parts(-dots)):
                    low = jnp.where(lane == MASK_AT + at, value, low)
                head_grad[h, rows] = low.astype(BF16)
            return _

        lax.fori_loop(0, 2, run, None)

    def unrotate(r, rows, value):
        return value * table_c[r, rows] - swap_halves(value) * table_s[r, rows]

    def attend_back(r, h):
        first, second = 2 * LANE * h, 2 * LANE * h + LANE
        lane = lanes((quarter, LANE))
        dq_total, bias_k, bias_v = None, 0.0, 0.0
        for b in range(4):
            rows = slice(b * quarter, (b + 1) * quarter)
            keys = heads_k[r, h, rows]
            probs = jnp.exp(dot_nt(keys, heads_q[r, h]))
            low = (probs * dot_nt(heads_v[r, h, rows], head_grad[h])).astype(BF16)
            dv = jnp.where(lane < HEAD_DIM, dot_nn(probs.astype(BF16), head_grad[h]), 0.0)
            dk = unrotate(r, rows, jnp.where(lane < HEAD_DIM, dot_nn(low, heads_q[r, h]), 0.0))
            dp_low[r, rows, first:second] = pltpu.roll(dk, HEAD_DIM, 1).astype(BF16)
            dp_low[r, rows, second : second + LANE] = dv.astype(BF16)
            bias_k += jnp.sum(dk, axis=0, keepdims=True)
            bias_v += jnp.sum(dv, axis=0, keepdims=True)
            one = dot_tn(keys, low)
            dq_total = one if dq_total is None else dq_total + one
        dq_total = jnp.transpose(dq_total)
        bias_q = 0.0
        for b in range(4):
            rows = slice(b * quarter, (b + 1) * quarter)
            dq = unrotate(r, rows, jnp.where(lane < HEAD_DIM, dq_total[rows], 0.0) * HEAD_DIM**-0.5)
            dp_low[r, rows, first:second] = (dp_low[r, rows, first:second].astype(F32) + dq).astype(BF16)
            bias_q += jnp.sum(dq, axis=0, keepdims=True)
        sums[7:8, first:second] = sums[7:8, first:second] + bias_q + pltpu.roll(bias_k, HEAD_DIM, 1)
        sums[7:8, second : second + LANE] = sums[7:8, second : second + LANE] + bias_v

    def close_back(r, link):
        sum_all(link, 0, r, lambda q: dot_nn(dp_low[r, rows_of(q)], wc[...]))

    def back_first_norm(r):
        def body(rows):
            incoming = sum_total(0, r, rows)
            normed, inv_std = normalize(first_tokens(r, rows))
            grad = gm[r, t, rows].astype(F32) + norm_back(incoming, normed, inv_std, attn_gain)
            ingrad[r, rows] = grad.astype(BF16)
            add_sum(0, incoming * normed)
            add_sum(1, incoming)

        over_chunks(quarter, body)

    def tall(ref, r, here):
        return ref[r, :, :, here].reshape(4 * quarter, here.stop - here.start)

    everything = slice(0, features)

    def add_grad(r, target, here, one):
        target[here] = (one if r == 0 else one + target[here].astype(F32)).astype(BF16)

    def feed_grad(r, left, right, target, here):
        add_grad(r, target, here, dot_tn(tall(left, r, here), tall(right, r, everything)))

    def out_grad(r):
        for h in range(3):
            one = dot_tn(head_out[r, h], tall(gm, r, everything))
            add_grad(r, gout, slice(h * HEAD_DIM, (h + 1) * HEAD_DIM), one[0:HEAD_DIM])

    def qkv_grad(r, h):
        one = dot_tn(dp_low[r, :, 2 * LANE * h : 2 * LANE * (h + 1)], tall(n1, r, everything))
        add_grad(r, gqkv, h, one[0 : 3 * HEAD_DIM])

    piece, half = features // 4, features // 2
    reduces, used = {}, 0
    for i, name in enumerate(SUMS):
        at = int(name[1:] or 0)
        if name[0] in "DU":
            ref, out = ((gdown, gdown_out) if name[0] == "D" else (gup, gup_out))
            ref, out = ref.at[pl.ds(piece * at, piece)], out.at[pl.ds(piece * at, piece)]
        else:
            ref, out = (gout, gout_out) if name == "O" else (gqkv.at[at], gqkv_out.at[at])
        groups = sum_groups(dp_steps, name)
        size = Reduce.land_rows(*ref.shape, groups)
        reduces[name] = Reduce(copies, ref, land_sums.at[pl.ds(used, size)], out, out_sems.at[2 + i], groups, d, t)
        used += size

    def settle(own, back):
        def body(rows):
            mine, returned = own[1, rows].astype(F32), back[rows].astype(F32)
            middle = jnp.where(carried_wide(), returned, mine)
            own[1, rows] = jnp.where(count_wide >= 2, middle, 0.0).astype(BF16)
            own[2, rows] = jnp.where(count_wide >= 3, returned, 0.0).astype(BF16)

        over_chunks(quarter, body)

    store_mixed = pltpu.make_async_copy(mixed, mixed_out, out_sems.at[0])
    store_grad = pltpu.make_async_copy(ingrad, grad_out, out_sems.at[1])

    def count_codons(slot):
        logits = dot_nt(mixed[slot], head_ref[...])
        raised = jnp.exp(logits - jnp.max(logits, -1, keepdims=True))
        probs = raised / jnp.sum(raised, -1, keepdims=True)
        one = jnp.sum(probs, axis=0, keepdims=True)
        one = jnp.where(jnp.full(one.shape, count, jnp.int32) > slot, one, 0.0)
        codon_out[...] = one if slot == 0 else codon_out[...] + one

    def send_back(copy):
        @pl.when(d > 0)
        def _():
            copy().start()

    def get_back(copy):
        @pl.when(d > 0)
        def _():
            copy().wait_send()

        @pl.when(d < n_dp - 1)
        def _():
            copy().wait_recv()

    shared = lax.broadcasted_iota(jnp.int32, (8, features), 0) < 6
    sum_links, used = [], 0
    for clique in cliques:
        sum_links.append([(copies.make(sums, sums_land.at[used + i], other), used + i) for i, other in enumerate(clique)])
        used += len(clique)

    def small_start(k):
        for copy, _ in sum_links[k]:
            copy().start()

    def small_end(k):
        for copy, _ in sum_links[k]:
            copy().wait()
        extra = sum(sums_land[at] for _, at in sum_links[k])
        sums[...] = sums[...] + (jnp.where(shared, extra, 0.0) if k == 0 else extra)

    def begin():
        sums[...] = jnp.zeros_like(sums)
        pick_tail(tok_ref, tail_tok)
        tail_lens = lens_tile(slots - 1)
        for slot in range(slots - 2, -1, -1):
            tail_lens = jnp.where(jnp.full((8, LANE), count, jnp.int32) == slot + 1, lens_tile(slot), tail_lens)
        lens_mine[...] = tail_lens
        scan_mine[0] = jnp.full((8, LANE), count, jnp.int32)
        pl.semaphore_wait(barrier, len(greeted))
        links["tA"][0]().start()
        scan_start(0)

        @pl.when(d < n_dp - 1)
        def _():
            send_lens().start()
            send_tok().start()

        load_out.wait()
        weight_links[0]().start()
        share_weight().start()
        first_norm(0)
        links["tA"][1]().start()

        @pl.when(d == 0)
        def _():
            tok_b[...] = jnp.zeros_like(tok_b)
            got_cot[...] = jnp.zeros_like(got_cot)
            lens_land[...] = jnp.zeros_like(lens_land)

        @pl.when(d == n_dp - 1)
        def _():
            back_mixed[...] = jnp.zeros_like(back_mixed)
            back_grad[...] = jnp.zeros_like(back_grad)

        load_cot.wait()
        pick_tail(cotan_ref, tail_cot)
        load_cotangent(0)

    def prepare():
        empty = jnp.zeros((HEAD_DIM, features), BF16)
        for h in range(3):
            wc[2 * LANE * h + 3 * HEAD_DIM : 2 * LANE * (h + 1)] = empty
            bias = [bqkv_ref[j : j + 1, h * HEAD_DIM : (h + 1) * HEAD_DIM] for j in range(3)]
            bc[:, 2 * LANE * h : 2 * LANE * (h + 1)] = jnp.concatenate(bias + [jnp.zeros_like(bias[0])], axis=1)
        for load in loads:
            load.wait()

    def second_row():
        @pl.when(d > 0)
        def _():
            send_lens().wait_recv()
            send_tok().wait_recv()

        @pl.when(d < n_dp - 1)
        def _():
            send_lens().wait_send()
            send_tok().wait_send()
            send_cot().start()

        def pick(rows):
            value = jnp.where(carried_wide(), tok_b[rows].astype(F32), tok_ref[1, rows].astype(F32))
            tok_b[rows] = value.astype(BF16)

        over_chunks(quarter, pick)
        links["tB"][0]().start()
        first_norm(1)
        links["tB"][1]().start()

    steps = {"begin": begin, "prep": prepare, "LN1B": second_row, "cB": lambda: load_cotangent(1)}
    for k in range(dp_steps):

        def scan(k=k):
            scan_end(k)
            if k + 1 < dp_steps:
                scan_start(k + 1)

        steps["scan%d" % k] = scan

    def wait_all(*copies):
        for copy in copies:
            copy().wait()

    def after_wait(wait, work, *args):
        def run():
            wait()
            work(*args)

        return run

    def nothing():
        pass

    for k in range(len(weight_links) - 1):

        def weight_step(k=k):
            weight_links[k]().wait()
            weight_links[k + 1]().start()

        steps["w%d" % k] = weight_step

    weights_late = ["w"]
    for name, r in rows_ab.items():
        tokens, heads, second, cots, mids = (links[key + name] for key in ("t", "h", "n2", "c", "gm"))
        near, far, last, back = (links[key + name] for key in ("g", "m", "f", "gm"))

        def first_ready(link=tokens):
            wait_all(link[1])

        def rest_ready(link=tokens):
            link[0]().wait_send()
            wait_all(link[2])

        def cot_near(link=cots):
            link[0]().wait_send()

        def cot_rest(link=cots, second=second):
            wait_all(link[1], link[2], *second)

        def weight_ready():
            if weights_late:
                weights_late.clear()
                wait_all(share_weight, weight_links[-1])

        def mids_near(link=mids):
            wait_all(link[1])

        def mids_rest(link=mids):
            link[0]().wait_send()
            wait_all(link[2])

        steps["tab" + name] = after_wait(nothing, tables, r)
        steps["QK0" + name] = after_wait(first_ready, project, r, 0)
        steps["QK1" + name] = after_wait(rest_ready, project, r, 2)
        steps["att" + name] = after_wait(nothing, attend, r, heads)
        steps["hp" + name] = after_wait(nothing, pack_heads, r, heads)
        steps["LN2" + name] = after_wait(weight_ready, second_norm, r, heads, second)
        steps["fe0" + name] = after_wait(cot_near, feed_own, r)
        steps["fe1" + name] = after_wait(cot_rest, feed_other, r, near)
        steps["clF" + name] = after_wait(nothing, close_feed, r, far)
        steps["mix" + name] = after_wait(functools.partial(sum_end, far), finish_mixed, r)
        steps["cod" + name] = after_wait(nothing, count_codons, r)
        steps["bk2" + name] = after_wait(functools.partial(sum_end, near), back_second_norm, r)
        steps["op0" + name] = after_wait(mids_near, open_heads, r, 0)
        steps["op1" + name] = after_wait(mids_rest, open_heads, r, 2)
        for h in range(3):
            steps["ab%d%s" % (h, name)] = after_wait(nothing, attend_back, r, h)
        steps["clB" + name] = after_wait(nothing, close_back, r, last)
        steps["bk1" + name] = after_wait(functools.partial(sum_end, last), back_first_norm, r)

    def with_start(names, work, *args):
        def run():
            work(*args)
            for name in names:
                reduces[name].start()

        return run

    for i in (0, 2):
        here = slice(piece * i, piece * i + half)
        for kind, args in (("D", (act, cot, gdown, here)), ("U", (n2, slope, gup, here))):
            steps["d%s%d" % (kind, i)] = after_wait(nothing, feed_grad, 0, *args)
            steps["%s%d" % (kind, i)] = with_start(tuple("%s%d" % (kind, i + k) for k in range(2)), feed_grad, 1, *args)
    steps["dO"] = after_wait(nothing, out_grad, 0)
    steps["O"] = with_start(("O",), out_grad, 1)
    for h in range(3):
        steps["dQ%d" % h] = after_wait(nothing, qkv_grad, 0, h)
        steps["Q%d" % h] = with_start(("Q%d" % h,), qkv_grad, 1, h)

    def settle_mixed():
        get_back(return_mixed)
        settle(mixed, back_mixed)
        store_mixed.start()
        count_codons(1)
        count_codons(2)

    def settle_grad():
        get_back(return_grad)
        settle(ingrad, back_grad)
        store_grad.start()

    steps["retM"] = lambda: send_back(return_mixed)
    steps["retG"] = lambda: send_back(return_grad)
    steps["setM"] = settle_mixed
    steps["setG"] = settle_grad
    for k in range(len(cliques)):

        def small(k=k):
            small_end(k)
            if k + 1 < len(cliques):
                small_start(k + 1)

        steps["sum%d" % k] = small
    steps["sums"] = lambda: small_start(0)

    starts = {"c", "gm"}
    for step in schedule(dp_steps, len(cliques)):
        kind, _, name = step.partition(":")
        if kind == "x":
            if name[:-1] in starts:
                gather_start(links[name])
            else:
                links[name][2]().start()
        elif kind[0] == "w" and kind not in steps:
            continue
        elif kind == "p" and name[0] == "t":
            pass_tokens(rows_ab[name[1]], links[name])
        elif kind == "p":
            gather_pass(links[name])
        elif kind == "t":
            reduces[name.partition(".")[0]].tick()
        else:
            steps[kind]()
    while any(each.left() for each in reduces.values()):
        for each in reduces.values():
            each.tick()
    small_out[...] = sums[...]
    for j in range(3):
        pieces = [sums[7:8, (4 * h + j) * HEAD_DIM : (4 * h + j + 1) * HEAD_DIM] for h in range(3)]
        qkv_bias_out[j : j + 1] = jnp.concatenate(pieces, axis=1)
    store_mixed.wait()
    store_grad.wait()


def finish_kernel(
    quarter,
    count_ref,
    mixed_in,
    grad_in,
    gdown_in,
    gup_in,
    gout_in,
    gqkv_in,
    small_ref,
    qkv_bias_ref,
    codon_ref,
    freq_ref,
    mixed_out,
    grad_out,
    gdown_out,
    gup_out,
    gout_out,
    gqkv_out,
    qkv_bias_out,
    codon_out,
    *refs,
):
    vectors, (gdown, gup, gout, gqkv, fdown, fup, fout, fqkv, rows, load_sems, store_sems) = refs[:7], refs[7:]
    pairs = ((gdown_in, gdown), (gup_in, gup), (gqkv_in, gqkv), (mixed_in, rows.at[0]), (grad_in, rows.at[1]), (gout_in, gout))
    loads = [pltpu.make_async_copy(source, target, load_sems.at[i]) for i, (source, target) in enumerate(pairs)]
    for load in loads:
        load.start()
    stores = []

    def store(source, target, i, k):
        stores.append(pltpu.make_async_copy(source, target, store_sems.at[i, k]))
        stores[-1].start()

    for i, vector in enumerate(vectors):
        vector[...] = small_ref[i : i + 1].reshape(vector.shape[0])
    qkv_bias_out[...] = qkv_bias_ref[...]
    scale = jnp.full(codon_ref.shape, count_ref[0] * quarter, jnp.int32).astype(F32)
    freq = freq_ref[...].reshape(codon_ref.shape)
    codon_out[0] = jnp.log(codon_ref[...] / scale) - jnp.log(freq)

    def widen(i, low, wide, out, pieces):
        loads[i].wait()
        size = low.shape[0] // pieces
        for k in range(pieces):
            here = pl.ds(k * size, size)
            wide[here] = low[here].astype(F32)
            store(wide.at[here], out.at[here], i, k)

    widen(0, gdown, fdown, gdown_out, 4)
    widen(1, gup, fup, gup_out, 4)
    loads[2].wait()
    for h in range(3):
        for j in range(3):
            block = gqkv[h, j * HEAD_DIM : (j + 1) * HEAD_DIM]
            fqkv[j, h * HEAD_DIM : (h + 1) * HEAD_DIM] = block.astype(F32)
    store(fqkv, gqkv_out, 2, 0)
    for i, out in ((3, mixed_out), (4, grad_out)):
        loads[i].wait()
        store(rows.at[i - 3], out, i, 0)
    widen(5, gout, fout, gout_out, 1)
    for each in stores:
        each.wait()


def body(
    tokens,
    cotangent,
    lengths,
    row_counts,
    attn_gain,
    attn_shift,
    qkv_weight,
    qkv_bias,
    out_weight,
    out_bias,
    ffn_gain,
    ffn_shift,
    up_weight,
    up_bias,
    down_weight,
    down_bias,
    head_weight,
    codon_freq,
):
    slots, quarter, features = tokens.shape
    n_dp = lax.axis_size("dp")
    steps = n_dp.bit_length() - 1
    length = 4 * quarter
    half = HEAD_DIM // 2
    freqs = np.float32(BASE) ** (-np.arange(half, dtype=np.float32) / np.float32(half))
    freq_lane = np.tile(freqs.astype(np.float32), LANE // half)
    sign = np.concatenate([-np.ones(half), np.ones(half), np.zeros(HEAD_DIM)]).astype(np.float32)

    def turned(places):
        angles = places[:, None].astype(np.float64) * freq_lane[None].astype(np.float64)
        return np.stack([np.cos(angles) * np.abs(sign), np.sin(angles) * sign]).astype(np.float32)

    rope, bases = turned(np.arange(CHUNK)), turned(np.arange(0, length, CHUNK))
    vmem, smem = pl.BlockSpec(memory_space=pltpu.VMEM), pl.BlockSpec(memory_space=pltpu.SMEM)
    anywhere = pl.BlockSpec(memory_space=pl.ANY)
    wide = (quarter, features)

    def low(*shape):
        return pltpu.VMEM(shape, BF16)

    def full(*shape):
        return pltpu.VMEM(shape, F32)

    out_width = 3 * HEAD_DIM
    cliques = 3 + sum((1 << min(3, steps - k)) - 1 for k in range(0, steps, 3))
    sum_land = sum(Reduce.land_rows(features // 4, features, sum_groups(steps, name)) for name in SUMS)
    n_sums = sum(Reduce.copies_of(sum_groups(steps, name)) for name in SUMS)
    n_sems = 2 * (3 * 2 + 3 * 3 + 3 + 4 + 2) + 6 + 5 + steps + n_sums + cliques
    scratch = [
        low(2, 4, *wide),
        low(2, 4, *wide),
        low(2, 4, *wide),
        low(2, 4, *wide),
        low(2, 3, length, LANE),
        low(2, 3, length, LANE),
        low(2, 3, length, LANE),
        low(2, 3, length, LANE),
        low(3, length, LANE),
        low(2, length, 6 * LANE),
        low(2, 4, *wide),
        low(2, 4, *wide),
        low(2, 2, 4, *wide),
        low(2, 2, 2, *wide),
        low(2, 2, *wide),
        full(2, *wide),
        full(2, length, LANE),
        full(2, length, LANE),
        low(6 * LANE, features),
        full(1, 6 * LANE),
        low(2, 2 * out_width, features),
        low(*wide),
        pltpu.VMEM((steps + 1, 8, LANE), jnp.int32),
        pltpu.VMEM((steps, 8, LANE), jnp.int32),
        pltpu.VMEM((8, LANE), jnp.int32),
        pltpu.VMEM((8, LANE), jnp.int32),
        low(features, features),
        low(features, features),
        low(out_width, features),
        low(3, out_width, features),
        low(sum_land, features),
        low(*wide),
        low(*wide),
        full(8, features),
        full(cliques, 8, features),
        full(8, features),
        low(*tokens.shape),
        low(*up_weight.shape),
        low(*down_weight.shape),
        pltpu.SemaphoreType.DMA((n_sems,)),
        pltpu.SemaphoreType.DMA((n_sems,)),
        pltpu.SemaphoreType.DMA((2 + len(SUMS),)),
        pltpu.SemaphoreType.DMA((16,)),
    ]
    outs = pl.pallas_call(
        functools.partial(layer_kernel, n_dp, slots, quarter, features),
        out_shape=(
            jax.ShapeDtypeStruct(tokens.shape, BF16),
            jax.ShapeDtypeStruct(tokens.shape, BF16),
            jax.ShapeDtypeStruct((features, features), BF16),
            jax.ShapeDtypeStruct((features, features), BF16),
            jax.ShapeDtypeStruct((out_width, features), BF16),
            jax.ShapeDtypeStruct((3, out_width, features), BF16),
            jax.ShapeDtypeStruct((8, features), F32),
            jax.ShapeDtypeStruct((3, out_width), F32),
            jax.ShapeDtypeStruct((1, head_weight.shape[1]), F32),
        ),
        in_specs=[smem, smem, vmem, anywhere, anywhere, vmem, anywhere, anywhere, anywhere] + [vmem] * 12,
        out_specs=(anywhere,) * 6 + (vmem,) * 3,
        scratch_shapes=scratch,
        compiler_params=pltpu.CompilerParams(
            collective_id=0, has_side_effects=True, vmem_limit_bytes=64 * 1024 * 1024
        ),
    )(
        row_counts,
        lengths,
        tokens,
        cotangent,
        jnp.swapaxes(qkv_weight, 1, 2),
        qkv_bias,
        out_weight,
        up_weight,
        down_weight,
        attn_gain,
        attn_shift,
        out_bias,
        ffn_gain,
        ffn_shift,
        down_bias,
        up_bias,
        head_weight.T,
        jnp.asarray(freq_lane[None]),
        jnp.asarray(rope),
        jnp.asarray(bases),
        jnp.asarray(sign[None]),
    )
    mixed, input_grad, gdown, gup, gout, gqkv, small, qkv_bias_grad, codon = outs
    wide_out = (3, out_width, features)
    vector = jax.ShapeDtypeStruct((features,), F32)
    finished = pl.pallas_call(
        functools.partial(finish_kernel, quarter),
        out_shape=(
            jax.ShapeDtypeStruct(tokens.shape, BF16),
            jax.ShapeDtypeStruct(tokens.shape, BF16),
            jax.ShapeDtypeStruct(gdown.shape, F32),
            jax.ShapeDtypeStruct(gup.shape, F32),
            jax.ShapeDtypeStruct(gout.shape, F32),
            jax.ShapeDtypeStruct(wide_out, F32),
            jax.ShapeDtypeStruct((3, out_width), F32),
            jax.ShapeDtypeStruct((1, 1, codon_freq.shape[0]), F32),
        )
        + (vector,) * 7,
        in_specs=[smem] + [anywhere] * 6 + [vmem] * 4,
        out_specs=(anywhere,) * 6 + (vmem,) * 9,
        scratch_shapes=[
            low(*gdown.shape),
            low(*gup.shape),
            low(*gout.shape),
            low(*wide_out),
            full(*gdown.shape),
            full(*gup.shape),
            full(*gout.shape),
            full(*wide_out),
            low(2, *tokens.shape),
            pltpu.SemaphoreType.DMA((6,)),
            pltpu.SemaphoreType.DMA((6, 4)),
        ],
        compiler_params=pltpu.CompilerParams(vmem_limit_bytes=60 * 1024 * 1024),
    )(row_counts, mixed, input_grad, gdown, gup, gout, gqkv, small, qkv_bias_grad, codon, codon_freq)
    mixed, input_grad, gdown, gup, gout, gqkv, qkv_bias_grad, codon_gap = finished[:8]
    vectors = finished[8:]
    return (
        mixed,
        input_grad,
        vectors[0],
        vectors[1],
        jnp.swapaxes(gqkv, 1, 2),
        qkv_bias_grad,
        gout,
        vectors[2],
        vectors[3],
        vectors[4],
        gup,
        vectors[6],
        gdown,
        vectors[5],
        codon_gap,
    )


def solution(mesh):
    placed = (
        P("dp", "tensor", None),
        P("dp", "tensor", None),
        P("dp", None),
        P("dp"),
        P(),
        P(),
        P(None, None, "tensor"),
        P(None, "tensor"),
        P("tensor", None),
        P(),
        P(),
        P(),
        P(None, "tensor"),
        P("tensor"),
        P("tensor", None),
        P(),
        P(),
        P(),
    )
    return jax.shard_map(
        body,
        mesh=mesh,
        in_specs=placed,
        out_specs=(
            P("dp", "tensor", None),
            P("dp", "tensor", None),
            P(),
            P(),
            P(None, None, "tensor"),
            P(None, "tensor"),
            P("tensor", None),
            P(),
            P(),
            P(),
            P(None, "tensor"),
            P("tensor"),
            P("tensor", None),
            P(),
            P("dp", "tensor", None),
        ),
        check_vma=False,
    )
```

```python
import functools

import jax
import jax.numpy as jnp
import numpy as np
from jax import lax
from jax.experimental import pallas as pl
from jax.experimental.pallas import tpu as pltpu
from jax.sharding import PartitionSpec as P

HEAD_DIM = 64
EPS = 1e-05
BASE = 10000.0
F32 = jnp.float32
BF16 = jnp.bfloat16
MESH = pl.DeviceIdType.MESH
LANE = 128
CHUNK = 64
FAR = -1e30
MASK_AT = 64
TOTAL_AT = 68
TREE = "tree"
SUMS = {
    "D0": ((0,), 'tree'),
    "D1": ((0,), 'tree'),
    "D2": ((1,), (0,), (2,)),
    "D3": ((0,), 'tree'),
    "U0": ((1,), (0,), (2,)),
    "U1": ((0,), (1,), (2,)),
    "U2": ((1,), (0,), (2,)),
    "U3": ((0,), (1,), (2,)),
    "O": ((1,), (0,), (2,)),
    "Q0": ((0,), 'tree'),
    "Q1": ((0,), (1,), (2,)),
    "Q2": ((0,), 'tree'),
}


def dot_nn(a, b):
    return lax.dot_general(a, b, (((1,), (0,)), ((), ())), preferred_element_type=F32)


def dot_nt(a, b):
    return lax.dot_general(a, b, (((1,), (1,)), ((), ())), preferred_element_type=F32)


def dot_tn(a, b):
    return lax.dot_general(a, b, (((0,), (0,)), ((), ())), preferred_element_type=F32)


def lanes(shape):
    return lax.broadcasted_iota(jnp.int32, shape, 1)


def three_parts(value):
    high = value.astype(BF16).astype(F32)
    rest = value - high
    middle = rest.astype(BF16).astype(F32)
    return high, middle, rest - middle


def normalize(value):
    average = jnp.mean(value, -1, keepdims=True)
    centred = value - average
    inv_std = lax.rsqrt(jnp.mean(centred * centred, -1, keepdims=True) + EPS)
    return centred * inv_std, inv_std


def norm_back(incoming, normed, inv_std, gain):
    scaled = incoming * gain
    return inv_std * (
        scaled
        - jnp.mean(scaled, -1, keepdims=True)
        - normed * jnp.mean(scaled * normed, -1, keepdims=True)
    )


def swap_halves(value):
    lane = lanes(value.shape)
    return jnp.where(lane < 32, pltpu.roll(value, 96, 1), pltpu.roll(value, 32, 1))


class Copies:
    def __init__(self, send, recv):
        self.send, self.recv, self.count = send, recv, 0

    def make(self, src, dst, device):
        at = self.count
        self.count += 1
        return functools.partial(
            pltpu.make_async_remote_copy,
            src_ref=src,
            dst_ref=dst,
            send_sem=self.send.at[at],
            recv_sem=self.recv.at[at],
            device_id=device,
            device_id_type=MESH,
        )


class Region:
    def __init__(self, row, rows, lane, width):
        self.row, self.rows, self.lane, self.width = row, rows, lane, width

    def halves(self, side):
        if self.rows % 32 == 0:
            half = self.rows // 2
            cut = [Region(self.row + half * k, half, self.lane, self.width) for k in (side, 1 - side)]
        elif self.width % (2 * LANE) == 0:
            half = self.width // 2
            cut = [Region(self.row, self.rows, self.lane + half * k, half) for k in (side, 1 - side)]
        else:
            cut = None
        return cut

    def of(self, ref, start=0, rows=None):
        row, lane = self.row + start, self.lane
        if not isinstance(row, int):
            row = pl.multiple_of(row, 16)
        if not isinstance(lane, int):
            lane = pl.multiple_of(lane, LANE)
        return ref.at[pl.ds(row, rows or self.rows), pl.ds(lane, self.width)]


class Places:
    def __init__(self, width):
        self.width, self.used, self.spare = width, 0, []

    def take(self, region):
        at = (self.used, 0)
        if 2 * region.width == self.width:
            if (region.rows, region.width) in [size for size, _ in self.spare]:
                i = [size for size, _ in self.spare].index((region.rows, region.width))
                return self.spare.pop(i)[1]
            self.spare.append(((region.rows, region.width), Region(self.used, region.rows, region.width, region.width)))
        self.used += region.rows
        return Region(at[0], region.rows, at[1], region.width)


def under(condition, work):
    if condition is None:
        work()
    else:
        pl.when(condition)(work)


class Step:
    def __init__(self, copies, region, landed=(), sender=None, receiver=None):
        self.copies, self.region, self.landed = copies, region, landed
        self.sender, self.receiver = sender, receiver


class Reduce:
    def __init__(self, copies, ref, land, out, store_sem, groups, d, t):
        self.ref, self.land = ref, land
        self.plan, self.holder = [], None
        rows, width = ref.shape
        region, place, backs = Region(0, rows, 0, width), Places(width), []
        for group in groups:
            if group == TREE:
                inner = ((d >> 1) & 1) != ((d >> 2) & 1)
                there = place.take(region)
                copy = copies.make(region.of(ref), there.of(land), (d ^ 2, t))
                self.plan.append(Step([copy], region, [there], jnp.logical_not(inner), inner))
                backs.append((region, [(d ^ 2, t)], inner, jnp.logical_not(inner)))
                self.holder, group, masks = inner, (2,), [6]
            else:
                masks = None
            sends, mine = [], self.part(region, group, [(d >> bit) & 1 for bit in group])
            for mask in range(1, 1 << len(group)):
                turned = [(mask >> i) & 1 for i in range(len(group))]
                flips = masks[0] if masks else sum(turn << bit for turn, bit in zip(turned, group))
                partner = (d ^ flips, t)
                give = self.part(region, group, [((d >> bit) & 1) ^ turn for turn, bit in zip(turned, group)])
                there = place.take(mine)
                sends.append((copies.make(give.of(ref), there.of(land), partner), there, partner))
            landed = [there for _, there, _ in sends]
            self.plan.append(Step([copy for copy, _, _ in sends], mine, landed, self.holder, self.holder))
            if mine.rows * mine.width < region.rows * region.width:
                backs.append((mine, [partner for _, _, partner in sends], self.holder, self.holder))
            region = mine
        self.adds = len(self.plan)
        self.store = functools.partial(pltpu.make_async_copy, region.of(ref), region.of(out), store_sem)
        for i, (region, partners, sender, receiver) in enumerate(reversed(backs)):
            own = region.of(ref if i == 0 else out)
            sends = [copies.make(own, region.of(out), partner) for partner in partners]
            self.plan.append(Step(sends, region, (), sender, receiver))
        self.place = 0

    @staticmethod
    def part(region, group, sides):
        for side in sides:
            region = (region.halves(side) or (region,))[0]
        return region

    @staticmethod
    def land_rows(rows, width, groups):
        region, place = Region(0, rows, 0, width), Places(width)
        for group in groups:
            if group == TREE:
                place.take(region)
                group = (2,)
            region = Reduce.part(region, group, [0] * len(group))
            for _ in range(1, 1 << len(group)):
                place.take(region)
        return place.used

    @staticmethod
    def copies_of(groups):
        return sum(4 if group == TREE else 2 * ((1 << len(group)) - 1) for group in groups)

    def start(self):
        for copy in self.plan[0].copies:
            copy().start()

    def left(self):
        return len(self.plan) - self.place

    def tick(self):
        if self.place >= len(self.plan):
            return
        now, rows = self.plan[self.place], self.plan[self.place].region.rows
        size = max(size for size in (16, 32, 48, 64, 96) if rows % size == 0)

        def add(i, _):
            here = now.region.of(self.ref, i * size, size)
            total = here[...].astype(F32)
            for there in now.landed:
                total += there.of(self.land, i * size, size)[...].astype(F32)
            here[...] = total.astype(BF16)
            return _

        def receive():
            for copy in now.copies:
                copy().wait_recv()
            if now.landed:
                lax.fori_loop(0, rows // size, add, None)

        def sent():
            for copy in now.copies:
                copy().wait_send()

        under(now.sender, sent)
        under(now.receiver, receive)
        if self.place == self.adds - 1:
            under(self.holder, lambda: self.store().start())
        if self.place == self.adds or (self.place + 1 == len(self.plan) and self.place < self.adds):
            under(self.holder, lambda: self.store().wait())
        self.place += 1
        if self.place < len(self.plan):
            later = self.plan[self.place]

            def begin():
                for copy in later.copies:
                    copy().start()

            under(later.sender, begin)


def sum_groups(steps, name):
    groups = SUMS[name]
    if TREE in groups and steps < 3:
        groups = ((0,), (1,))
    first = [group if group == TREE else tuple(bit for bit in group if bit < steps) for group in groups]
    return [group for group in first if group] + [(bit,) for bit in range(3, steps)]


def schedule(dp_steps, cliques):
    names = (
        "begin", "prep", "tabA", "x:cA", "scan0", "QK0A", "scan1", "scan2", "LN1B", "p:tA", "w0", "tabB", "QK1A",
        "attA", "w1", "p:cA", "cB", "hpA", "QK0B", "p:tB", "x:cB", "w2", "QK1B", "attB", "w3", "hpB", "LN2A", "fe0A",
        "fe1A", "p:cB", "dD0", "dU0", "dU2", "dD2", "LN2B", "fe0B", "fe1B", "U2", "U0", "clFB", "bk2A", "D0", "t:U3",
        "t:U2", "x:gmA", "D2", "op0A", "t:U1", "bk2B", "t:U3", "t:D0", "t:U0", "x:mB", "x:gmB", "clFA", "t:U1",
        "t:U2", "p:gmA", "t:U3", "t:D2", "t:D0", "t:D1", "x:mA", "op1A", "t:U1", "t:U0", "ab0A", "t:U2", "t:U3",
        "t:D2", "t:D0", "dO", "t:D3", "mixB", "t:D1", "retM", "dQ0", "ab1A", "ab2A", "t:U0", "t:U1", "t:U2", "p:gmB",
        "op0B", "t:D2", "t:U3", "t:D1", "op1B", "O", "ab0B", "Q0", "t:D3", "t:U0", "t:U2", "t:D0", "ab1B", "dQ2",
        "t:O", "t:D1", "t:D2", "dQ1", "Q1", "t:D3", "t:Q0", "ab2B", "Q2", "t:U0", "clBB", "t:Q0", "t:U1", "t:Q1",
        "t:O", "t:D0", "t:D3", "t:Q2", "t:Q0", "t:D1", "t:Q1", "clBA", "t:O", "t:Q0", "t:U1", "mixA", "t:D3", "t:Q2",
        "t:Q1", "bk1B", "retG", "t:O", "t:D0", "t:Q2", "t:Q1", "bk1A", "sums", "t:Q0", "codA", "t:U0", "t:Q2", "t:D2",
        "t:O", "t:D3", "t:Q1", "setM", "t:Q2", "sum0", "setG", "t:U2", "t:Q1", "t:Q0", "t:D2", "t:D1", "t:U3", "sum1",
        "t:O", "t:Q2",
    )
    for name in names:
        if name in ("scan2", "sum1"):
            count = dp_steps if name == "scan2" else cliques
            yield from (name[:-1] + str(k) for k in range(int(name[-1]), count))
        else:
            yield name


def layer_kernel(
    n_dp,
    slots,
    quarter,
    features,
    count_ref,
    lens_ref,
    tok_ref,
    cotan_any,
    wqkv_ref,
    bqkv_ref,
    wout_ref,
    wup_any,
    wdown_any,
    attn_gain_ref,
    attn_shift_ref,
    out_bias_ref,
    ffn_gain_ref,
    ffn_shift_ref,
    down_bias_ref,
    up_bias_ref,
    head_ref,
    freq_ref,
    rope_ref,
    base_ref,
    line_ref,
    mixed_out,
    grad_out,
    gdown_out,
    gup_out,
    gout_out,
    gqkv_out,
    small_out,
    qkv_bias_out,
    codon_out,
    n1,
    n2,
    cot,
    gm,
    heads_q,
    heads_k,
    heads_v,
    head_out,
    head_grad,
    dp_low,
    act,
    slope,
    part,
    land_core,
    land_x,
    mid,
    table_c,
    table_s,
    wc,
    bc,
    wcat,
    tok_b,
    scan_mine,
    scan_land,
    lens_mine,
    lens_land,
    gdown,
    gup,
    gout,
    gqkv,
    land_sums,
    back_mixed,
    back_grad,
    sums,
    sums_land,
    vec,
    cotan_ref,
    wup_ref,
    wdown_ref,
    send_sems,
    recv_sems,
    out_sems,
    load_sems,
):
    d, t = lax.axis_index("dp"), lax.axis_index("tensor")
    core, across = (d, t ^ 1), (d, t ^ 2)
    own_rows = slots - 1
    dp_steps = n_dp.bit_length() - 1
    copies = Copies(send_sems, recv_sems)
    rows_ab = {"A": 0, "B": 1}

    vectors = (attn_gain_ref, attn_shift_ref, out_bias_ref, ffn_gain_ref, ffn_shift_ref, down_bias_ref, up_bias_ref)
    for i, ref in enumerate(vectors):
        vec[i : i + 1] = ref[...].reshape(1, features)
    attn_gain, attn_shift = vec[0:1], vec[1:2]
    out_bias, ffn_gain, ffn_shift, down_bias, up_bias = (vec[i : i + 1] for i in range(2, 7))

    cliques = [[(d, t ^ m) for m in range(1, 4)]]
    for low_bit in range(0, dp_steps, 3):
        width = min(3, dp_steps - low_bit)
        cliques.append([(d ^ (m << low_bit), t) for m in range(1, 1 << width)])
    greeted = [other for clique in cliques for other in clique]
    for k in range(dp_steps):
        greeted.append(((d + (1 << k)) % n_dp, t))
        greeted.append(((d + n_dp - (1 << k)) % n_dp, t))
    barrier = pltpu.get_barrier_semaphore()
    for other in greeted:
        pl.semaphore_signal(barrier, inc=1, device_id=other, device_id_type=MESH)

    loads = []
    for h in range(3):
        for j in range(3):
            source = wqkv_ref.at[j, pl.ds(h * HEAD_DIM, HEAD_DIM)]
            target = wc.at[pl.ds(2 * LANE * h + HEAD_DIM * j, HEAD_DIM)]
            loads.append(pltpu.make_async_copy(source, target, load_sems.at[len(loads)]))
    out_width = 3 * HEAD_DIM
    half_lanes = features // 2
    load_out = pltpu.make_async_copy(wout_ref, wcat.at[0, pl.ds(0, out_width)], load_sems.at[len(loads)])
    load_cot = pltpu.make_async_copy(cotan_any, cotan_ref, load_sems.at[len(loads) + 1])
    load_out.start()
    load_cot.start()
    loads.append(pltpu.make_async_copy(wup_any, wup_ref, load_sems.at[len(loads) + 2]))
    loads.append(pltpu.make_async_copy(wdown_any, wdown_ref, load_sems.at[len(loads) + 2]))
    for load in loads:
        load.start()

    def over_chunks(rows, body, step=CHUNK):
        def run(i, _):
            body(pl.ds(pl.multiple_of(i * step, step), step))
            return _

        lax.fori_loop(0, rows // step, run, None)

    mixed, ingrad = n2.at[0, pl.ds(0, slots)], n2.at[1, pl.ds(0, slots)]

    heads_x = land_x.at[1]
    tok_x, got_cot = gm.at[:, 1], gm.at[1, 0]

    tail_tok, tail_cot = mixed.at[slots - 1], ingrad.at[slots - 1]
    count = count_ref[0]
    count_wide = jnp.full((CHUNK, features), count, jnp.int32)

    def pick_tail(source, target):
        def body(rows):
            value = source[slots - 1, rows].astype(F32)
            for slot in range(slots - 2, -1, -1):
                value = jnp.where(count_wide == slot + 1, source[slot, rows].astype(F32), value)
            target[rows] = value.astype(BF16)

        over_chunks(quarter, body)

    after, before = (d + 1, t), (d - 1, t)
    send_tok = copies.make(tail_tok, tok_b, after)
    send_cot = copies.make(tail_cot, got_cot, after)
    send_lens = copies.make(lens_mine, lens_land, after)
    return_mixed = copies.make(mixed.at[1], back_mixed, before)
    return_grad = copies.make(ingrad.at[1], back_grad, before)

    def lens_tile(slot):
        row_at = lax.broadcasted_iota(jnp.int32, (8, LANE), 0)
        tile = jnp.zeros((8, LANE), jnp.int32)
        for gene in range(4):
            tile = jnp.where(row_at == gene, lens_ref[slot, gene], tile)
        return tile

    scan_copies = [copies.make(scan_mine.at[k], scan_land.at[k], (d + (1 << k), t)) for k in range(dp_steps)]

    def scan_start(k):
        @pl.when(d + (1 << k) < n_dp)
        def _():
            scan_copies[k]().start()

    def scan_end(k):
        scan_mine[k + 1] = scan_mine[k]

        @pl.when(d + (1 << k) < n_dp)
        def _():
            scan_copies[k]().wait_send()

        @pl.when(d >= (1 << k))
        def _():
            scan_copies[k]().wait_recv()
            scan_mine[k + 1] = scan_mine[k] + scan_land[k]

    def carried_tile():
        return (scan_mine[dp_steps] - count - d * own_rows) > 0

    def carried_wide():
        return jnp.broadcast_to(carried_tile()[0:1, 0:1], (CHUNK, features))

    def gather(full, r):
        mine = full.at[r, t]
        return (
            copies.make(mine, mine, across),
            copies.make(mine, mine, core),
            copies.make(full.at[r, t ^ 2], full.at[r, t ^ 2], core),
        )

    def gather_start(link):
        link[0]().start()
        link[1]().start()

    def gather_pass(link):
        link[0]().wait_recv()
        link[2]().start()

    def gather_end(link):
        link[0]().wait_send()
        link[1]().wait()
        link[2]().wait()

    def summing(kind, r):
        return (
            copies.make(part.at[kind, r, t ^ 1], land_core.at[kind, r, 0], core),
            copies.make(part.at[kind, r, t ^ 3], land_core.at[kind, r, 1], core),
            copies.make(part.at[kind, r, t ^ 2], land_x.at[kind, r], across),
        )

    def quarter_of(i):
        return t ^ jnp.where(i == 0, 3, jnp.where(i == 3, 0, i))

    def sum_step(link, kind, r, i, q, value):
        @pl.when(i < 2)
        def _():
            part[kind, r, q] = value.astype(BF16)

        @pl.when(i == 0)
        def _():
            link[1]().start()

        @pl.when(i == 1)
        def _():
            link[0]().start()

        @pl.when(i == 2)
        def _():
            link[1]().wait_recv()
            part[kind, r, q] = (value + land_core[kind, r, 1].astype(F32)).astype(BF16)
            if kind == 0:
                link[2]().start()

        @pl.when(i == 3)
        def _():
            part[kind, r, q] = value.astype(BF16)

    def sum_all(link, kind, r, make_part):
        def run(i, _):
            q = quarter_of(i)
            sum_step(link, kind, r, i, q, make_part(q))
            return _

        lax.fori_loop(0, 4, run, None)

    def sum_end(link):
        link[0]().wait()
        link[1]().wait_send()
        link[2]().wait()

    def sum_total(kind, r, rows):
        near = part[kind, r, t, rows].astype(F32) + land_core[kind, r, 0, rows].astype(F32)
        return near + land_x[kind, r, rows].astype(F32)

    links = {}
    for name, r in rows_ab.items():
        for key, full in (("c", cot), ("gm", gm)):
            links[key + name] = gather(full, r)
        for key, kind in (("g", 0), ("f", 0), ("m", 1)):
            links[key + name] = summing(kind, r)
        source = tok_ref.at[0] if r == 0 else tok_b
        links["t" + name] = (
            copies.make(source, tok_x.at[r], across),
            copies.make(n1.at[r, t], n1.at[r, t], core),
            copies.make(n1.at[r, t ^ 2], n1.at[r, t ^ 2], core),
        )
        links["h" + name] = tuple(
            copies.make(part.at[0, r, t ^ m, :, pl.ds(0, half_lanes)], land_core.at[0, r, s, :, pl.ds(0, half_lanes)], core)
            for s, m in ((0, 1), (1, 3))
        ) + tuple(
            copies.make(
                part.at[0, r, t ^ m, :, pl.ds(half_lanes, half_lanes)],
                heads_x.at[r, :, pl.ds(half_lanes * s, half_lanes)],
                across,
            )
            for s, m in ((1, 0), (0, 2))
        )
        links["n2" + name] = tuple(copies.make(n2.at[r, t ^ m], n2.at[r, t ^ m], core) for m in (0, 2))
    own_out, got_out = wcat.at[0, pl.ds(0, out_width)], wcat.at[1, pl.ds(0, out_width)]
    piece_of, pieces = Region(0, out_width, 0, features), []
    for bit in range(min(3, dp_steps)):
        piece_of = piece_of.halves((d >> bit) & 1)[0]
        pieces.insert(0, ((d ^ (1 << bit), t), piece_of))
    weight_links = [copies.make(piece_of.of(own_out), piece_of.of(got_out), across)]
    weight_links += [copies.make(region.of(got_out), region.of(got_out), partner) for partner, region in pieces]
    weight_links.append(copies.make(got_out, wcat.at[1, pl.ds(out_width, out_width)], core))
    share_weight = copies.make(own_out, wcat.at[0, pl.ds(out_width, out_width)], core)

    def rows_of(q):
        return pl.ds(pl.multiple_of(q * quarter, quarter), quarter)

    def add_sum(row, value):
        sums[row : row + 1] = sums[row : row + 1] + jnp.sum(value, axis=0, keepdims=True)

    def first_tokens(r, rows):
        return (tok_ref[0, rows] if r == 0 else tok_b[rows]).astype(F32)

    def first_norm(r, theirs=False):
        def body(rows):
            normed, _ = normalize(tok_x[r, rows].astype(F32) if theirs else first_tokens(r, rows))
            n1[r, t ^ 2 if theirs else t, rows] = (normed * attn_gain + attn_shift).astype(BF16)

        over_chunks(quarter, body)

    def pass_tokens(r, link):
        link[0]().wait_recv()
        first_norm(r, theirs=True)
        link[2]().start()

    def load_cotangent(r):
        if r == 1:

            @pl.when(d > 0)
            def _():
                send_cot().wait_recv()

            @pl.when(d < n_dp - 1)
            def _():
                send_cot().wait_send()

        def body(rows):
            value = cotan_ref[0, rows].astype(F32)
            if r == 1:
                value = jnp.where(carried_wide(), got_cot[rows].astype(F32), cotan_ref[1, rows].astype(F32))
            cot[r, t, rows] = value.astype(BF16)
            add_sum(5, value)

        over_chunks(quarter, body)

    def ends_of(r):
        tile = lens_tile(0) if r == 0 else jnp.where(carried_tile(), lens_land[...], lens_tile(1))
        first = tile[0:1]
        second = first + tile[1:2]
        return first, second, second + tile[2:3]

    def segment_of(ends, base, rows):
        place = lax.broadcasted_iota(jnp.int32, (rows, LANE), 0) + base
        return [place >= end for end in ends]

    def tables(r):
        ends = ends_of(r)
        turns = [end.astype(F32) * freq_ref[...] for end in ends]
        cosines = [jnp.cos(turn) for turn in turns]
        sines = [jnp.sin(turn) * line_ref[...] for turn in turns]

        def body(rows):
            passed = segment_of(ends, rows.start, CHUNK)
            at = pl.ds(rows.start // CHUNK, 1)
            cos_base, sin_base = base_ref[0, at], base_ref[1, at]
            cos_start = jnp.broadcast_to(cos_base, (CHUNK, LANE))
            sin_start = jnp.broadcast_to(sin_base, (CHUNK, LANE))
            for ge, cosine, sine in zip(passed, cosines, sines):
                cos_start = jnp.where(ge, cos_base * cosine + sin_base * sine, cos_start)
                sin_start = jnp.where(ge, sin_base * cosine - cos_base * sine, sin_start)
            cos_place, sin_place = rope_ref[0], rope_ref[1]
            table_c[r, rows] = cos_place * cos_start - sin_place * sin_start
            table_s[r, rows] = sin_place * cos_start + cos_place * sin_start

        over_chunks(4 * quarter, body)

    def project(r, first):
        ends = ends_of(r)

        def run(i, _):
            q = t ^ (i + first)
            rows = rows_of(q)
            both = dot_nt(n1[r, q], wc[...]) + bc[...]
            lane = lanes((quarter, LANE))
            ge = segment_of(ends, q * quarter, quarter)
            gene = sum(g.astype(jnp.int32) for g in ge)
            in_mask = (lane >= MASK_AT) & (lane < TOTAL_AT)
            same = in_mask & (lane - MASK_AT == gene)
            extra_q = jnp.where(in_mask & ~same, FAR, 0.0)
            extra_k = jnp.where(same | ((lane >= TOTAL_AT) & (lane < TOTAL_AT + 3)), 1.0, 0.0)
            extra_v = jnp.where((lane >= MASK_AT) & (lane < MASK_AT + 3), 1.0, 0.0)
            cosine, sine = table_c[r, rows], table_s[r, rows]
            for h in range(3):
                query = both[:, 2 * LANE * h : 2 * LANE * h + LANE]
                key = pltpu.roll(query, HEAD_DIM, 1)
                value = both[:, 2 * LANE * h + LANE : 2 * LANE * (h + 1)]
                query = (query * cosine + swap_halves(query) * sine) * HEAD_DIM**-0.5 + extra_q
                key = key * cosine + swap_halves(key) * sine + extra_k
                heads_q[r, h, rows] = query.astype(BF16)
                heads_k[r, h, rows] = key.astype(BF16)
                heads_v[r, h, rows] = (value + extra_v).astype(BF16)
            return _

        lax.fori_loop(0, 2, run, None)

    def attend(r, link):
        def run(q, _):
            rows = rows_of(q)
            lane = lanes((quarter, LANE))
            queries = [heads_q[r, h, rows] for h in range(3)]
            scores = [dot_nt(queries[h], heads_k[r, h]) for h in range(3)]
            for h in range(3):
                top = jnp.max(scores[h], -1, keepdims=True)
                probs = jnp.exp(scores[h] - top).astype(BF16)
                mixed_values = dot_nn(probs, heads_v[r, h])
                total = mixed_values[:, MASK_AT : MASK_AT + 1]
                out = jnp.where(lane < HEAD_DIM, mixed_values * (1.0 / total), 0.0).astype(BF16)
                head_out[r, h, rows] = out
                part[0, r, q, :, h * LANE : (h + 1) * LANE] = out
                query = queries[h].astype(F32)
                for at, value in enumerate(three_parts(-(top + jnp.log(total)))):
                    query = jnp.where(lane == TOTAL_AT + at, value, query)
                heads_q[r, h, rows] = query.astype(BF16)
            return _

        lax.fori_loop(0, 4, run, None)
        link[1]().start()
        link[0]().start()

    def pack_heads(r, link):
        for s, m in ((1, 2), (0, 0)):
            link[s]().wait_recv()
            q = t ^ m
            blocks = [part[0, r, q, :, h * LANE : (h + 1) * LANE].astype(F32) for h in range(3)]
            blocks += [land_core[0, r, s, :, h * LANE : (h + 1) * LANE].astype(F32) for h in range(3)]
            for j in range(3):
                pair = blocks[2 * j] + pltpu.roll(blocks[2 * j + 1], HEAD_DIM, 1)
                part[0, r, q, :, half_lanes + j * LANE : half_lanes + (j + 1) * LANE] = pair.astype(BF16)
            link[3 if m else 2]().start()

    def second_norm(r, heads, out):
        for s, m in ((1, 2), (0, 0)):
            q = t ^ m
            near = dot_nn(part[0, r, q, :, half_lanes:], wcat[0])
            heads[2 if s else 3]().wait_recv()
            attention = near + dot_nn(heads_x[r, :, half_lanes * s : half_lanes * (s + 1)], wcat[1])
            for k in range(quarter // CHUNK):
                rows = slice(k * CHUNK, (k + 1) * CHUNK)
                tokens = tok_x[r, rows].astype(F32) if s else first_tokens(r, rows)
                middle = tokens + attention[rows] + out_bias
                if s == 0:
                    mid[r, rows] = middle
                normed, _ = normalize(middle)
                n2[r, q, rows] = (normed * ffn_gain + ffn_shift).astype(BF16)
            out[1 if m else 0]().start()
        for copy in heads:
            copy().wait_send()

    def feed(r, q):
        hidden = dot_nn(n2[r, q], wup_ref[...]) + up_bias
        below = 0.5 * (1.0 + lax.erf(hidden * 0.5**0.5))
        density = jnp.exp(hidden * hidden * -0.5) * (2.0 * np.pi) ** -0.5
        act[r, q] = (hidden * below).astype(BF16)
        grad = dot_nt(cot[r, q], wdown_ref[...]) * (below + hidden * density)
        add_sum(6, grad)
        low = grad.astype(BF16)
        slope[r, q] = low
        part[0, r, q] = dot_nt(low, wup_ref[...]).astype(BF16)

    def feed_own(r):
        def run(i, _):
            feed(r, t ^ (2 - 2 * i))
            return _

        lax.fori_loop(0, 2, run, None)

    def feed_other(r, link):
        def run(i, _):
            feed(r, t ^ (3 - 2 * i))

            @pl.when(i == 0)
            def _():
                link[1]().start()

            @pl.when(i == 1)
            def _():
                link[0]().start()

            return _

        lax.fori_loop(0, 2, run, None)
        link[1]().wait_recv()

        def add(rows):
            total = part[0, r, t ^ 2, rows].astype(F32) + land_core[0, r, 1, rows].astype(F32)
            part[0, r, t ^ 2, rows] = total.astype(BF16)

        over_chunks(quarter, add)
        link[2]().start()

    def close_feed(r, link):
        sum_all(link, 1, r, lambda q: dot_nn(act[r, q], wdown_ref[...]))

    def finish_mixed(r):
        def body(rows):
            mixed[r, rows] = (mid[r, rows] + sum_total(1, r, rows) + down_bias).astype(BF16)

        over_chunks(quarter, body)

    def back_second_norm(r):
        def body(rows):
            incoming = sum_total(0, r, rows)
            normed, inv_std = normalize(mid[r, rows])
            grad = cot[r, t, rows].astype(F32) + norm_back(incoming, normed, inv_std, ffn_gain)
            gm[r, t, rows] = grad.astype(BF16)
            add_sum(3, incoming * normed)
            add_sum(4, incoming)
            add_sum(2, grad)

        over_chunks(quarter, body)

    def open_heads(r, first):
        def run(i, _):
            q = t ^ (i + first)
            rows = rows_of(q)
            grads = dot_nt(gm[r, q], wcat[0, 0 : 2 * LANE])
            lane = lanes((quarter, LANE))
            pair, last = grads[:, 0:LANE], grads[:, LANE : 2 * LANE]
            for h, low in enumerate((pair, pltpu.roll(pair, HEAD_DIM, 1), last)):
                low = jnp.where(lane < HEAD_DIM, low, 0.0).astype(BF16).astype(F32)
                dots = jnp.sum(low * head_out[r, h, rows].astype(F32), -1, keepdims=True)
                for at, value in enumerate(three_parts(-dots)):
                    low = jnp.where(lane == MASK_AT + at, value, low)
                head_grad[h, rows] = low.astype(BF16)
            return _

        lax.fori_loop(0, 2, run, None)

    def unrotate(r, rows, value):
        return value * table_c[r, rows] - swap_halves(value) * table_s[r, rows]

    def attend_back(r, h):
        first, second = 2 * LANE * h, 2 * LANE * h + LANE
        lane = lanes((quarter, LANE))
        dq_total, bias_k, bias_v = None, 0.0, 0.0
        for b in range(4):
            rows = slice(b * quarter, (b + 1) * quarter)
            keys = heads_k[r, h, rows]
            probs = jnp.exp(dot_nt(keys, heads_q[r, h]))
            low = (probs * dot_nt(heads_v[r, h, rows], head_grad[h])).astype(BF16)
            dv = jnp.where(lane < HEAD_DIM, dot_nn(probs.astype(BF16), head_grad[h]), 0.0)
            dk = unrotate(r, rows, jnp.where(lane < HEAD_DIM, dot_nn(low, heads_q[r, h]), 0.0))
            dp_low[r, rows, first:second] = pltpu.roll(dk, HEAD_DIM, 1).astype(BF16)
            dp_low[r, rows, second : second + LANE] = dv.astype(BF16)
            bias_k += jnp.sum(dk, axis=0, keepdims=True)
            bias_v += jnp.sum(dv, axis=0, keepdims=True)
            one = dot_tn(keys, low)
            dq_total = one if dq_total is None else dq_total + one
        dq_total = jnp.transpose(dq_total)
        bias_q = 0.0
        for b in range(4):
            rows = slice(b * quarter, (b + 1) * quarter)
            dq = unrotate(r, rows, jnp.where(lane < HEAD_DIM, dq_total[rows], 0.0) * HEAD_DIM**-0.5)
            dp_low[r, rows, first:second] = (dp_low[r, rows, first:second].astype(F32) + dq).astype(BF16)
            bias_q += jnp.sum(dq, axis=0, keepdims=True)
        sums[7:8, first:second] = sums[7:8, first:second] + bias_q + pltpu.roll(bias_k, HEAD_DIM, 1)
        sums[7:8, second : second + LANE] = sums[7:8, second : second + LANE] + bias_v

    def close_back(r, link):
        sum_all(link, 0, r, lambda q: dot_nn(dp_low[r, rows_of(q)], wc[...]))

    def back_first_norm(r):
        def body(rows):
            incoming = sum_total(0, r, rows)
            normed, inv_std = normalize(first_tokens(r, rows))
            grad = gm[r, t, rows].astype(F32) + norm_back(incoming, normed, inv_std, attn_gain)
            ingrad[r, rows] = grad.astype(BF16)
            add_sum(0, incoming * normed)
            add_sum(1, incoming)

        over_chunks(quarter, body)

    def tall(ref, r, here):
        return ref[r, :, :, here].reshape(4 * quarter, here.stop - here.start)

    everything = slice(0, features)

    def add_grad(r, target, here, one):
        target[here] = (one if r == 0 else one + target[here].astype(F32)).astype(BF16)

    def feed_grad(r, left, right, target, here):
        add_grad(r, target, here, dot_tn(tall(left, r, here), tall(right, r, everything)))

    def out_grad(r):
        for h in range(3):
            one = dot_tn(head_out[r, h], tall(gm, r, everything))
            add_grad(r, gout, slice(h * HEAD_DIM, (h + 1) * HEAD_DIM), one[0:HEAD_DIM])

    def qkv_grad(r, h):
        one = dot_tn(dp_low[r, :, 2 * LANE * h : 2 * LANE * (h + 1)], tall(n1, r, everything))
        add_grad(r, gqkv, h, one[0 : 3 * HEAD_DIM])

    piece, half = features // 4, features // 2
    reduces, used = {}, 0
    for i, name in enumerate(SUMS):
        at = int(name[1:] or 0)
        if name[0] in "DU":
            ref, out = ((gdown, gdown_out) if name[0] == "D" else (gup, gup_out))
            ref, out = ref.at[pl.ds(piece * at, piece)], out.at[pl.ds(piece * at, piece)]
        else:
            ref, out = (gout, gout_out) if name == "O" else (gqkv.at[at], gqkv_out.at[at])
        groups = sum_groups(dp_steps, name)
        size = Reduce.land_rows(*ref.shape, groups)
        reduces[name] = Reduce(copies, ref, land_sums.at[pl.ds(used, size)], out, out_sems.at[2 + i], groups, d, t)
        used += size

    def settle(own, back):
        def body(rows):
            mine, returned = own[1, rows].astype(F32), back[rows].astype(F32)
            middle = jnp.where(carried_wide(), returned, mine)
            own[1, rows] = jnp.where(count_wide >= 2, middle, 0.0).astype(BF16)
            own[2, rows] = jnp.where(count_wide >= 3, returned, 0.0).astype(BF16)

        over_chunks(quarter, body)

    store_mixed = pltpu.make_async_copy(mixed, mixed_out, out_sems.at[0])
    store_grad = pltpu.make_async_copy(ingrad, grad_out, out_sems.at[1])

    def count_codons(slot):
        logits = dot_nt(mixed[slot], head_ref[...])
        raised = jnp.exp(logits - jnp.max(logits, -1, keepdims=True))
        probs = raised / jnp.sum(raised, -1, keepdims=True)
        one = jnp.sum(probs, axis=0, keepdims=True)
        one = jnp.where(jnp.full(one.shape, count, jnp.int32) > slot, one, 0.0)
        codon_out[...] = one if slot == 0 else codon_out[...] + one

    def send_back(copy):
        @pl.when(d > 0)
        def _():
            copy().start()

    def get_back(copy):
        @pl.when(d > 0)
        def _():
            copy().wait_send()

        @pl.when(d < n_dp - 1)
        def _():
            copy().wait_recv()

    shared = lax.broadcasted_iota(jnp.int32, (8, features), 0) < 6
    sum_links, used = [], 0
    for clique in cliques:
        sum_links.append([(copies.make(sums, sums_land.at[used + i], other), used + i) for i, other in enumerate(clique)])
        used += len(clique)

    def small_start(k):
        for copy, _ in sum_links[k]:
            copy().start()

    def small_end(k):
        for copy, _ in sum_links[k]:
            copy().wait()
        extra = sum(sums_land[at] for _, at in sum_links[k])
        sums[...] = sums[...] + (jnp.where(shared, extra, 0.0) if k == 0 else extra)

    def begin():
        sums[...] = jnp.zeros_like(sums)
        pick_tail(tok_ref, tail_tok)
        tail_lens = lens_tile(slots - 1)
        for slot in range(slots - 2, -1, -1):
            tail_lens = jnp.where(jnp.full((8, LANE), count, jnp.int32) == slot + 1, lens_tile(slot), tail_lens)
        lens_mine[...] = tail_lens
        scan_mine[0] = jnp.full((8, LANE), count, jnp.int32)
        pl.semaphore_wait(barrier, len(greeted))
        links["tA"][0]().start()
        scan_start(0)

        @pl.when(d < n_dp - 1)
        def _():
            send_lens().start()
            send_tok().start()

        load_out.wait()
        weight_links[0]().start()
        share_weight().start()
        first_norm(0)
        links["tA"][1]().start()

        @pl.when(d == 0)
        def _():
            tok_b[...] = jnp.zeros_like(tok_b)
            got_cot[...] = jnp.zeros_like(got_cot)
            lens_land[...] = jnp.zeros_like(lens_land)

        @pl.when(d == n_dp - 1)
        def _():
            back_mixed[...] = jnp.zeros_like(back_mixed)
            back_grad[...] = jnp.zeros_like(back_grad)

        load_cot.wait()
        pick_tail(cotan_ref, tail_cot)
        load_cotangent(0)

    def prepare():
        empty = jnp.zeros((HEAD_DIM, features), BF16)
        for h in range(3):
            wc[2 * LANE * h + 3 * HEAD_DIM : 2 * LANE * (h + 1)] = empty
            bias = [bqkv_ref[j : j + 1, h * HEAD_DIM : (h + 1) * HEAD_DIM] for j in range(3)]
            bc[:, 2 * LANE * h : 2 * LANE * (h + 1)] = jnp.concatenate(bias + [jnp.zeros_like(bias[0])], axis=1)
        for load in loads:
            load.wait()

    def second_row():
        @pl.when(d > 0)
        def _():
            send_lens().wait_recv()
            send_tok().wait_recv()

        @pl.when(d < n_dp - 1)
        def _():
            send_lens().wait_send()
            send_tok().wait_send()
            send_cot().start()

        def pick(rows):
            value = jnp.where(carried_wide(), tok_b[rows].astype(F32), tok_ref[1, rows].astype(F32))
            tok_b[rows] = value.astype(BF16)

        over_chunks(quarter, pick)
        links["tB"][0]().start()
        first_norm(1)
        links["tB"][1]().start()

    steps = {"begin": begin, "prep": prepare, "LN1B": second_row, "cB": lambda: load_cotangent(1)}
    for k in range(dp_steps):

        def scan(k=k):
            scan_end(k)
            if k + 1 < dp_steps:
                scan_start(k + 1)

        steps["scan%d" % k] = scan

    def wait_all(*copies):
        for copy in copies:
            copy().wait()

    def after_wait(wait, work, *args):
        def run():
            wait()
            work(*args)

        return run

    def nothing():
        pass

    for k in range(len(weight_links) - 1):

        def weight_step(k=k):
            weight_links[k]().wait()
            weight_links[k + 1]().start()

        steps["w%d" % k] = weight_step

    weights_late = ["w"]
    for name, r in rows_ab.items():
        tokens, heads, second, cots, mids = (links[key + name] for key in ("t", "h", "n2", "c", "gm"))
        near, far, last, back = (links[key + name] for key in ("g", "m", "f", "gm"))

        def first_ready(link=tokens):
            wait_all(link[1])

        def rest_ready(link=tokens):
            link[0]().wait_send()
            wait_all(link[2])

        def cot_near(link=cots):
            link[0]().wait_send()

        def cot_rest(link=cots, second=second):
            wait_all(link[1], link[2], *second)

        def weight_ready():
            if weights_late:
                weights_late.clear()
                wait_all(share_weight, weight_links[-1])

        def mids_near(link=mids):
            wait_all(link[1])

        def mids_rest(link=mids):
            link[0]().wait_send()
            wait_all(link[2])

        steps["tab" + name] = after_wait(nothing, tables, r)
        steps["QK0" + name] = after_wait(first_ready, project, r, 0)
        steps["QK1" + name] = after_wait(rest_ready, project, r, 2)
        steps["att" + name] = after_wait(nothing, attend, r, heads)
        steps["hp" + name] = after_wait(nothing, pack_heads, r, heads)
        steps["LN2" + name] = after_wait(weight_ready, second_norm, r, heads, second)
        steps["fe0" + name] = after_wait(cot_near, feed_own, r)
        steps["fe1" + name] = after_wait(cot_rest, feed_other, r, near)
        steps["clF" + name] = after_wait(nothing, close_feed, r, far)
        steps["mix" + name] = after_wait(functools.partial(sum_end, far), finish_mixed, r)
        steps["cod" + name] = after_wait(nothing, count_codons, r)
        steps["bk2" + name] = after_wait(functools.partial(sum_end, near), back_second_norm, r)
        steps["op0" + name] = after_wait(mids_near, open_heads, r, 0)
        steps["op1" + name] = after_wait(mids_rest, open_heads, r, 2)
        for h in range(3):
            steps["ab%d%s" % (h, name)] = after_wait(nothing, attend_back, r, h)
        steps["clB" + name] = after_wait(nothing, close_back, r, last)
        steps["bk1" + name] = after_wait(functools.partial(sum_end, last), back_first_norm, r)

    def with_start(names, work, *args):
        def run():
            work(*args)
            for name in names:
                reduces[name].start()

        return run

    for i in (0, 2):
        here = slice(piece * i, piece * i + half)
        for kind, args in (("D", (act, cot, gdown, here)), ("U", (n2, slope, gup, here))):
            steps["d%s%d" % (kind, i)] = after_wait(nothing, feed_grad, 0, *args)
            steps["%s%d" % (kind, i)] = with_start(tuple("%s%d" % (kind, i + k) for k in range(2)), feed_grad, 1, *args)
    steps["dO"] = after_wait(nothing, out_grad, 0)
    steps["O"] = with_start(("O",), out_grad, 1)
    for h in range(3):
        steps["dQ%d" % h] = after_wait(nothing, qkv_grad, 0, h)
        steps["Q%d" % h] = with_start(("Q%d" % h,), qkv_grad, 1, h)

    def settle_mixed():
        get_back(return_mixed)
        settle(mixed, back_mixed)
        store_mixed.start()
        count_codons(1)
        count_codons(2)

    def settle_grad():
        get_back(return_grad)
        settle(ingrad, back_grad)
        store_grad.start()

    steps["retM"] = lambda: send_back(return_mixed)
    steps["retG"] = lambda: send_back(return_grad)
    steps["setM"] = settle_mixed
    steps["setG"] = settle_grad
    for k in range(len(cliques)):

        def small(k=k):
            small_end(k)
            if k + 1 < len(cliques):
                small_start(k + 1)

        steps["sum%d" % k] = small
    steps["sums"] = lambda: small_start(0)

    starts = {"c", "gm"}
    for step in schedule(dp_steps, len(cliques)):
        kind, _, name = step.partition(":")
        if kind == "x":
            if name[:-1] in starts:
                gather_start(links[name])
            else:
                links[name][2]().start()
        elif kind[0] == "w" and kind not in steps:
            continue
        elif kind == "p" and name[0] == "t":
            pass_tokens(rows_ab[name[1]], links[name])
        elif kind == "p":
            gather_pass(links[name])
        elif kind == "t":
            reduces[name.partition(".")[0]].tick()
        else:
            steps[kind]()
    while any(each.left() for each in reduces.values()):
        for each in reduces.values():
            each.tick()
    small_out[...] = sums[...]
    for j in range(3):
        pieces = [sums[7:8, (4 * h + j) * HEAD_DIM : (4 * h + j + 1) * HEAD_DIM] for h in range(3)]
        qkv_bias_out[j : j + 1] = jnp.concatenate(pieces, axis=1)
    store_mixed.wait()
    store_grad.wait()


def finish_kernel(
    quarter,
    count_ref,
    mixed_in,
    grad_in,
    gdown_in,
    gup_in,
    gout_in,
    gqkv_in,
    small_ref,
    qkv_bias_ref,
    codon_ref,
    freq_ref,
    mixed_out,
    grad_out,
    gdown_out,
    gup_out,
    gout_out,
    gqkv_out,
    qkv_bias_out,
    codon_out,
    *refs,
):
    vectors, (gdown, gup, gout, gqkv, fdown, fup, fout, fqkv, rows, load_sems, store_sems) = refs[:7], refs[7:]
    pairs = ((gdown_in, gdown), (gup_in, gup), (gqkv_in, gqkv), (mixed_in, rows.at[0]), (grad_in, rows.at[1]), (gout_in, gout))
    loads = [pltpu.make_async_copy(source, target, load_sems.at[i]) for i, (source, target) in enumerate(pairs)]
    for load in loads:
        load.start()
    stores = []

    def store(source, target, i, k):
        stores.append(pltpu.make_async_copy(source, target, store_sems.at[i, k]))
        stores[-1].start()

    for i, vector in enumerate(vectors):
        vector[...] = small_ref[i : i + 1].reshape(vector.shape[0])
    qkv_bias_out[...] = qkv_bias_ref[...]
    scale = jnp.full(codon_ref.shape, count_ref[0] * quarter, jnp.int32).astype(F32)
    freq = freq_ref[...].reshape(codon_ref.shape)
    codon_out[0] = jnp.log(codon_ref[...] / scale) - jnp.log(freq)

    def widen(i, low, wide, out, pieces):
        loads[i].wait()
        size = low.shape[0] // pieces
        for k in range(pieces):
            here = pl.ds(k * size, size)
            wide[here] = low[here].astype(F32)
            store(wide.at[here], out.at[here], i, k)

    widen(0, gdown, fdown, gdown_out, 4)
    widen(1, gup, fup, gup_out, 4)
    loads[2].wait()
    for h in range(3):
        for j in range(3):
            block = gqkv[h, j * HEAD_DIM : (j + 1) * HEAD_DIM]
            fqkv[j, h * HEAD_DIM : (h + 1) * HEAD_DIM] = block.astype(F32)
    store(fqkv, gqkv_out, 2, 0)
    for i, out in ((3, mixed_out), (4, grad_out)):
        loads[i].wait()
        store(rows.at[i - 3], out, i, 0)
    widen(5, gout, fout, gout_out, 1)
    for each in stores:
        each.wait()


def body(
    tokens,
    cotangent,
    lengths,
    row_counts,
    attn_gain,
    attn_shift,
    qkv_weight,
    qkv_bias,
    out_weight,
    out_bias,
    ffn_gain,
    ffn_shift,
    up_weight,
    up_bias,
    down_weight,
    down_bias,
    head_weight,
    codon_freq,
):
    slots, quarter, features = tokens.shape
    n_dp = lax.axis_size("dp")
    steps = n_dp.bit_length() - 1
    length = 4 * quarter
    half = HEAD_DIM // 2
    freqs = np.float32(BASE) ** (-np.arange(half, dtype=np.float32) / np.float32(half))
    freq_lane = np.tile(freqs.astype(np.float32), LANE // half)
    sign = np.concatenate([-np.ones(half), np.ones(half), np.zeros(HEAD_DIM)]).astype(np.float32)

    def turned(places):
        angles = places[:, None].astype(np.float64) * freq_lane[None].astype(np.float64)
        return np.stack([np.cos(angles) * np.abs(sign), np.sin(angles) * sign]).astype(np.float32)

    rope, bases = turned(np.arange(CHUNK)), turned(np.arange(0, length, CHUNK))
    vmem, smem = pl.BlockSpec(memory_space=pltpu.VMEM), pl.BlockSpec(memory_space=pltpu.SMEM)
    anywhere = pl.BlockSpec(memory_space=pl.ANY)
    wide = (quarter, features)

    def low(*shape):
        return pltpu.VMEM(shape, BF16)

    def full(*shape):
        return pltpu.VMEM(shape, F32)

    out_width = 3 * HEAD_DIM
    cliques = 3 + sum((1 << min(3, steps - k)) - 1 for k in range(0, steps, 3))
    sum_land = sum(Reduce.land_rows(features // 4, features, sum_groups(steps, name)) for name in SUMS)
    n_sums = sum(Reduce.copies_of(sum_groups(steps, name)) for name in SUMS)
    n_sems = 2 * (3 * 2 + 3 * 3 + 3 + 4 + 2) + 6 + 5 + steps + n_sums + cliques
    scratch = [
        low(2, 4, *wide),
        low(2, 4, *wide),
        low(2, 4, *wide),
        low(2, 4, *wide),
        low(2, 3, length, LANE),
        low(2, 3, length, LANE),
        low(2, 3, length, LANE),
        low(2, 3, length, LANE),
        low(3, length, LANE),
        low(2, length, 6 * LANE),
        low(2, 4, *wide),
        low(2, 4, *wide),
        low(2, 2, 4, *wide),
        low(2, 2, 2, *wide),
        low(2, 2, *wide),
        full(2, *wide),
        full(2, length, LANE),
        full(2, length, LANE),
        low(6 * LANE, features),
        full(1, 6 * LANE),
        low(2, 2 * out_width, features),
        low(*wide),
        pltpu.VMEM((steps + 1, 8, LANE), jnp.int32),
        pltpu.VMEM((steps, 8, LANE), jnp.int32),
        pltpu.VMEM((8, LANE), jnp.int32),
        pltpu.VMEM((8, LANE), jnp.int32),
        low(features, features),
        low(features, features),
        low(out_width, features),
        low(3, out_width, features),
        low(sum_land, features),
        low(*wide),
        low(*wide),
        full(8, features),
        full(cliques, 8, features),
        full(8, features),
        low(*tokens.shape),
        low(*up_weight.shape),
        low(*down_weight.shape),
        pltpu.SemaphoreType.DMA((n_sems,)),
        pltpu.SemaphoreType.DMA((n_sems,)),
        pltpu.SemaphoreType.DMA((2 + len(SUMS),)),
        pltpu.SemaphoreType.DMA((16,)),
    ]
    outs = pl.pallas_call(
        functools.partial(layer_kernel, n_dp, slots, quarter, features),
        out_shape=(
            jax.ShapeDtypeStruct(tokens.shape, BF16),
            jax.ShapeDtypeStruct(tokens.shape, BF16),
            jax.ShapeDtypeStruct((features, features), BF16),
            jax.ShapeDtypeStruct((features, features), BF16),
            jax.ShapeDtypeStruct((out_width, features), BF16),
            jax.ShapeDtypeStruct((3, out_width, features), BF16),
            jax.ShapeDtypeStruct((8, features), F32),
            jax.ShapeDtypeStruct((3, out_width), F32),
            jax.ShapeDtypeStruct((1, head_weight.shape[1]), F32),
        ),
        in_specs=[smem, smem, vmem, anywhere, anywhere, vmem, anywhere, anywhere, anywhere] + [vmem] * 12,
        out_specs=(anywhere,) * 6 + (vmem,) * 3,
        scratch_shapes=scratch,
        compiler_params=pltpu.CompilerParams(
            collective_id=0, has_side_effects=True, vmem_limit_bytes=64 * 1024 * 1024
        ),
    )(
        row_counts,
        lengths,
        tokens,
        cotangent,
        jnp.swapaxes(qkv_weight, 1, 2),
        qkv_bias,
        out_weight,
        up_weight,
        down_weight,
        attn_gain,
        attn_shift,
        out_bias,
        ffn_gain,
        ffn_shift,
        down_bias,
        up_bias,
        head_weight.T,
        jnp.asarray(freq_lane[None]),
        jnp.asarray(rope),
        jnp.asarray(bases),
        jnp.asarray(sign[None]),
    )
    mixed, input_grad, gdown, gup, gout, gqkv, small, qkv_bias_grad, codon = outs
    wide_out = (3, out_width, features)
    vector = jax.ShapeDtypeStruct((features,), F32)
    finished = pl.pallas_call(
        functools.partial(finish_kernel, quarter),
        out_shape=(
            jax.ShapeDtypeStruct(tokens.shape, BF16),
            jax.ShapeDtypeStruct(tokens.shape, BF16),
            jax.ShapeDtypeStruct(gdown.shape, F32),
            jax.ShapeDtypeStruct(gup.shape, F32),
            jax.ShapeDtypeStruct(gout.shape, F32),
            jax.ShapeDtypeStruct(wide_out, F32),
            jax.ShapeDtypeStruct((3, out_width), F32),
            jax.ShapeDtypeStruct((1, 1, codon_freq.shape[0]), F32),
        )
        + (vector,) * 7,
        in_specs=[smem] + [anywhere] * 6 + [vmem] * 4,
        out_specs=(anywhere,) * 6 + (vmem,) * 9,
        scratch_shapes=[
            low(*gdown.shape),
            low(*gup.shape),
            low(*gout.shape),
            low(*wide_out),
            full(*gdown.shape),
            full(*gup.shape),
            full(*gout.shape),
            full(*wide_out),
            low(2, *tokens.shape),
            pltpu.SemaphoreType.DMA((6,)),
            pltpu.SemaphoreType.DMA((6, 4)),
        ],
        compiler_params=pltpu.CompilerParams(vmem_limit_bytes=60 * 1024 * 1024),
    )(row_counts, mixed, input_grad, gdown, gup, gout, gqkv, small, qkv_bias_grad, codon, codon_freq)
    mixed, input_grad, gdown, gup, gout, gqkv, qkv_bias_grad, codon_gap = finished[:8]
    vectors = finished[8:]
    return (
        mixed,
        input_grad,
        vectors[0],
        vectors[1],
        jnp.swapaxes(gqkv, 1, 2),
        qkv_bias_grad,
        gout,
        vectors[2],
        vectors[3],
        vectors[4],
        gup,
        vectors[6],
        gdown,
        vectors[5],
        codon_gap,
    )


def solution(mesh):
    placed = (
        P("dp", "tensor", None),
        P("dp", "tensor", None),
        P("dp", None),
        P("dp"),
        P(),
        P(),
        P(None, None, "tensor"),
        P(None, "tensor"),
        P("tensor", None),
        P(),
        P(),
        P(),
        P(None, "tensor"),
        P("tensor"),
        P("tensor", None),
        P(),
        P(),
        P(),
    )
    return jax.shard_map(
        body,
        mesh=mesh,
        in_specs=placed,
        out_specs=(
            P("dp", "tensor", None),
            P("dp", "tensor", None),
            P(),
            P(),
            P(None, None, "tensor"),
            P(None, "tensor"),
            P("tensor", None),
            P(),
            P(),
            P(),
            P(None, "tensor"),
            P("tensor"),
            P("tensor", None),
            P(),
            P("dp", "tensor", None),
        ),
        check_vma=False,
    )
```
